512 devices in a mesh: rows: 128 (over z, y, core), cols: 4 (over x).
Axes of the slice: x: 4, y: 4, z: 16, core: 2. Of those that a mesh axis runs over, the one named last changes fastest.
Arguments:
- latent: bfloat16 [4, 128, 1024], P(None, 'rows', 'cols'), may hold values from -18 to 18
- deep: bfloat16 [320, 128, 1024], P(None, 'rows', 'cols'), may hold values from -6 to 6
- timestep: int32 [1], replicated, may hold values from 0 to 999
- in_weight: bfloat16 [36, 320], replicated, may hold values from -1 to 1
- front_weight: bfloat16 [5760, 320], P('rows'), may hold values from -0.078125 to 0.078125
- middle_weight: bfloat16 [2880, 320], P('cols'), may hold values from -0.109375 to 0.109375
- skip_weight: bfloat16 [640, 320], P('cols'), may hold values from -0.25 to 0.25
- out_weight: bfloat16 [2880, 4], replicated, may hold values from -0.109375 to 0.109375
- time_weight: bfloat16 [320, 1280], replicated, may hold values from -0.3125 to 0.3125
- time_second: bfloat16 [1280, 1280], P('cols'), may hold values from -0.15625 to 0.15625
- time_proj: bfloat16 [1280, 320], replicated, may hold values from -0.15625 to 0.15625
- input_gain: float32 [640], replicated, may hold values from 0.1 to 1.9
- middle_gain: float32 [320], replicated, may hold values from 0.1 to 1.9
- output_gain: float32 [320], replicated, may hold values from 0.1 to 1.9
Outputs:
- noise: float32 [4, 128, 1024], P(None, 'rows', 'cols')
The draws below stay inside these ranges and needn't reach their ends.
All inputs are finite; a program needn't handle non-finite values.
Results may differ from the reference program's by a relative error of at most 0.0047.
Values may be sent and summed in bfloat16 or wider, within the bound.
No kernel may reach another device: no remote copies, remote signals or barrier semaphores. Data moves between devices by JAX's collectives and lax.ppermute only.
A program may use at most 64 MiB of HBM per device.

```python
import math
import jax
import jax.numpy as jnp
from jax import lax

C = 320
CIN = 4
GROUPS = 32
FREQ = 320
TIME = 1280
H = 128
W = 1024


def draw_latent(key, part):
    key_base = jax.random.fold_in(key, 11)
    key_rough = jax.random.fold_in(key, 23)
    positions = jnp.arange(H, dtype=jnp.float32) / H
    rising = 3.0 ** positions
    rough = jax.random.uniform(key_rough, (CIN, H, W), jnp.float32, 0.5, 1.5)
    base = jnp.clip(jax.random.normal(key_base, (CIN, H, W), jnp.float32), -4.0, 4.0)
    return (base * rough * rising[None, :, None]).astype(jnp.bfloat16)


def draw_deep(key, part):
    map_count = 6
    wave_count = 3
    key_rowfreq = jax.random.fold_in(key, 101)
    key_colfreq = jax.random.fold_in(key, 103)
    key_phase = jax.random.fold_in(key, 107)
    key_amplitude = jax.random.fold_in(key, 109)
    key_loadings = jax.random.fold_in(key, 113)
    key_jitter = jax.random.fold_in(key, 127)
    key_offset = jax.random.fold_in(key, 131)
    freq_rows = jax.random.randint(key_rowfreq, (map_count, wave_count), 1, 5).astype(jnp.float32)
    freq_cols = jax.random.randint(key_colfreq, (map_count, wave_count), 1, 9).astype(jnp.float32)
    phases = jax.random.uniform(key_phase, (map_count, wave_count), jnp.float32, 0.0, 2.0 * math.pi)
    amplitude = jax.random.normal(key_amplitude, (map_count, wave_count), jnp.float32)
    row_pos = jnp.arange(H, dtype=jnp.float32) / H
    col_pos = jnp.arange(W, dtype=jnp.float32) / W
    smooth_maps = jnp.zeros((map_count, H, W), jnp.float32)
    for wave_index in range(wave_count):
        angle_grid = 2.0 * math.pi * (freq_rows[:, wave_index, None, None] * row_pos[None, :, None] + freq_cols[:, wave_index, None, None] * col_pos[None, None, :]) + phases[:, wave_index, None, None]
        smooth_maps = smooth_maps + amplitude[:, wave_index, None, None] * jnp.cos(angle_grid)
    map_norms = jnp.sqrt(0.5 * jnp.sum(amplitude * amplitude, axis=1) + 0.001)
    smooth_maps = smooth_maps / map_norms[:, None, None]
    loadings = jax.random.normal(key_loadings, (C, map_count), jnp.float32) * (1.1 / math.sqrt(map_count))
    common_part = jnp.einsum('ck,khw->chw', loadings, smooth_maps)
    offsets = 0.3 * jax.random.normal(key_offset, (C,), jnp.float32)
    jitter = 0.5 * jax.random.normal(key_jitter, (C, H, W), jnp.float32)
    result_value = common_part + jitter + offsets[:, None, None]
    return jnp.clip(result_value, -6.0, 6.0).astype(jnp.bfloat16)


def shard_levels(stream_key, shape, shards, smallest, largest):
    def one(dim, shards_of):
        steps = jax.random.uniform(jax.random.fold_in(jax.random.fold_in(stream_key, 6), dim), (shards_of,), jnp.float32, smallest / len(shards), largest / len(shards))
        return jnp.repeat(jnp.exp(steps), shape[dim] // shards_of).reshape((-1,) + (1,) * (len(shape) - dim - 1))

    level = one(*shards[0])
    for cut in shards[1:]:
        level = level * one(*cut)
    return level


def noise(key, shape, width, most, cuts=(), held_as=jnp.bfloat16):
    level = shard_levels(key, shape, cuts, -0.22, 0.18) if cuts else 1.0
    values = jax.random.normal(key, shape, jnp.float32) * width * level
    return jnp.minimum(jnp.maximum(values, -most), most).astype(held_as)


def setup_inputs(seed: int = 0) -> dict:
    seeds = jax.random.split(jax.random.key(seed), 15)
    latent = draw_latent(jax.random.fold_in(seeds[14], 71), 0)
    deep = draw_deep(jax.random.fold_in(seeds[14], 71), 0)
    timestep = jax.random.randint(seeds[2], (1,), 0, 1000).astype(jnp.int32)
    in_weight = noise(seeds[3], (9 * CIN, C), (9 * CIN) ** -0.5, 1.0)
    front_weight = noise(seeds[4], (18 * C, C), (18 * C) ** -0.5, 0.078125, ((0, 128),))
    middle_weight = noise(seeds[5], (9 * C, C), (9 * C) ** -0.5, 0.109375, ((0, 4),))
    skip_weight = noise(seeds[6], (2 * C, C), (2 * C) ** -0.5, 0.25, ((0, 4),))
    out_weight = noise(seeds[7], (9 * C, CIN), (9 * C) ** -0.5, 0.109375)
    time_weight = noise(seeds[8], (FREQ, TIME), FREQ ** -0.5, 0.3125)
    time_second = noise(seeds[9], (TIME, TIME), TIME ** -0.5, 0.15625, ((0, 4),))
    time_proj = noise(seeds[10], (TIME, C), TIME ** -0.5, 0.15625)
    input_gain = jnp.clip(1.0 + 0.18 * jax.random.normal(seeds[11], (2 * C,), jnp.float32), 0.1, 1.9)
    middle_gain = jnp.clip(1.0 + 0.18 * jax.random.normal(seeds[12], (C,), jnp.float32), 0.1, 1.9)
    output_gain = jnp.clip(1.0 + 0.18 * jax.random.normal(seeds[13], (C,), jnp.float32), 0.1, 1.9)
    return {"latent": latent, "deep": deep, "timestep": timestep, "in_weight": in_weight, "front_weight": front_weight, "middle_weight": middle_weight, "skip_weight": skip_weight, "out_weight": out_weight, "time_weight": time_weight, "time_second": time_second, "time_proj": time_proj, "input_gain": input_gain, "middle_gain": middle_gain, "output_gain": output_gain}


epsilon = 1e-05

def convolve(field, weight):
    channels = field.shape[0]
    kernel = weight.astype(jnp.float32).reshape(3, 3, channels, -1).transpose(3, 2, 0, 1)
    result = lax.conv_general_dilated(field.astype(jnp.float32)[None], kernel, (1, 1), ((1, 1), (1, 1)), dimension_numbers=('NCHW', 'OIHW', 'NCHW'), precision=lax.Precision.HIGHEST)
    return result[0]

def norm_silu(values, gain):
    grouped = values.reshape(GROUPS, -1)
    center = lax.optimization_barrier(jnp.mean(grouped, axis=1, keepdims=True))
    offsets = grouped - center
    spread = lax.optimization_barrier(jnp.mean(offsets * offsets, axis=1, keepdims=True))
    scaled = (offsets * lax.rsqrt(spread + epsilon)).reshape(values.shape) * gain[:, None, None]
    return jax.nn.silu(scaled).astype(jnp.bfloat16)

def time_shift_of(timestep, time_weight, time_second, time_proj):
    half_width = time_weight.shape[0] // 2
    ratios = jnp.exp(-math.log(10000.0) * jnp.arange(half_width, dtype=jnp.float32) / half_width)
    angles = timestep[0].astype(jnp.float32) * ratios
    features = jnp.concatenate([jnp.cos(angles), jnp.sin(angles)])
    hidden = jax.nn.silu(jnp.dot(features, time_weight.astype(jnp.float32), precision=lax.Precision.HIGHEST))
    embedded = jnp.dot(hidden, time_second.astype(jnp.float32), precision=lax.Precision.HIGHEST)
    return jnp.dot(jax.nn.silu(embedded), time_proj.astype(jnp.float32), precision=lax.Precision.HIGHEST)

def reference(latent, deep, timestep, in_weight, front_weight, middle_weight, skip_weight, out_weight, time_weight, time_second, time_proj, input_gain, middle_gain, output_gain):
    skip_feat = convolve(latent, in_weight).astype(jnp.bfloat16)
    joined = jnp.concatenate([deep, skip_feat], axis=0)
    act_one = norm_silu(joined.astype(jnp.float32), input_gain)
    time_shift = time_shift_of(timestep, time_weight, time_second, time_proj)
    hidden_one = convolve(act_one, front_weight) + time_shift[:, None, None]
    act_two = norm_silu(hidden_one, middle_gain)
    flat_joined = joined.reshape(joined.shape[0], -1)
    shortcut = jnp.dot(jnp.transpose(skip_weight), flat_joined, preferred_element_type=jnp.float32)
    shortcut = shortcut.reshape(-1, joined.shape[1], joined.shape[2])
    block_out = convolve(act_two, middle_weight) + shortcut
    act_three = norm_silu(block_out, output_gain)
    return convolve(act_three, out_weight)
```

```python
import math

import jax
import jax.numpy as jnp
from jax import lax
from jax.experimental import pallas as pl
from jax.experimental.pallas import tpu as pltpu
from jax.sharding import Mesh
from jax.sharding import PartitionSpec as P

ROWS = ("zp", "zl", "y", "core")
DEPTH = ("zp", "zl")
PLANE = ("y", "core", "x")
EPS = 1e-05
F32 = jnp.float32
BF16 = jnp.bfloat16
HIGH = lax.Precision.HIGHEST

C = 320
HALF = 160
WIDE = 256
GAP = 16
SEG = WIDE + GAP
IN_ROWS = 8
MID_ROWS = 6
OUT_ROWS = 4
A_LEN = IN_ROWS * SEG + GAP
H_LEN = MID_ROWS * SEG + GAP
B_LEN = OUT_ROWS * SEG + GAP
MERGED = 512
LANES = 384
CHUNK = 48
VMEM = pl.BlockSpec(memory_space=pltpu.VMEM)
SMEM = pl.BlockSpec(memory_space=pltpu.SMEM)


def call(kernel, out_shape, in_specs, scratch=()):
    return pl.pallas_call(
        kernel,
        out_shape=out_shape,
        in_specs=in_specs,
        out_specs=jax.tree.map(lambda _: VMEM, out_shape),
        scratch_shapes=list(scratch),
        compiler_params=pltpu.CompilerParams(vmem_limit_bytes=40 * 1024 * 1024),
    )


def sds(shape, dtype):
    return jax.ShapeDtypeStruct(shape, dtype)


def rows_at(start, size):
    return pl.ds(pl.multiple_of(start, 16), size)


def same_group(n, m, size_n, size_m):
    i = lax.broadcasted_iota(jnp.int32, (n, m), 0)
    j = lax.broadcasted_iota(jnp.int32, (n, m), 1)
    return ((i // size_n) == (j // size_m)).astype(F32)


def exact_dot(a, b):
    return jnp.dot(a, b, preferred_element_type=F32, precision=HIGH)


def tap_dot(a, b):
    return jnp.dot(a, b, preferred_element_type=F32)


def silu_half(h):
    return h + h * jnp.tanh(h)


def pack_kernel(deep_ref, prev_ref, here_ref, next_ref, out_ref, first_ref, last_ref, tall):
    tall[0:C, :] = deep_ref[...].astype(F32)
    tall[C:LANES, :] = jnp.zeros((LANES - C, WIDE), F32)
    for i, ref in enumerate((prev_ref, here_ref, next_ref)):
        tall[C + 4 * i : C + 4 * i + 4, :] = ref[...].astype(F32)
    out = tall[...].T.astype(BF16)
    out_ref[...] = out
    first_ref[...] = out[0:GAP]
    last_ref[...] = out[WIDE - GAP : WIDE]


def skip_of(tail, wpad_ref, lo, hi):
    n = tail.shape[0]
    left = pltpu.roll(tail, 1, 0)[lo:hi].astype(BF16)
    right = pltpu.roll(tail, n - 1, 0)[lo:hi].astype(BF16)
    mid = tail[lo:hi].astype(BF16)
    stacked = jnp.concatenate([left, mid, right], axis=1)
    return tap_dot(stacked, wpad_ref[...]).astype(BF16).astype(F32)


def join(cells, skip):
    lane = lax.broadcasted_iota(jnp.int32, (cells.shape[0], 128), 1)
    mixed = jnp.where(lane < 64, cells[:, 256:384], skip[:, 0:128])
    return jnp.concatenate([cells[:, 0:256], mixed, skip[:, 128:384]], axis=1)


def stats_kernel(cells_ref, left_ref, right_ref, wpad_ref, row_ref, stat_ref):
    sub = lax.broadcasted_iota(jnp.int32, (GAP, LANES), 0)
    gap = jnp.where(sub < 8, right_ref[...].astype(F32), left_ref[...].astype(F32))
    cells = jnp.concatenate([cells_ref[...].astype(F32), gap], axis=0)
    row_ref[...] = cells.astype(BF16)
    skip = skip_of(cells[:, 256:384], wpad_ref, 0, WIDE)
    joined = join(cells[0:WIDE], skip)
    sums = jnp.sum(joined, axis=0, keepdims=True)
    squares = jnp.sum(joined * joined, axis=0, keepdims=True)
    both = jnp.concatenate([sums, squares, jnp.zeros((6, 2 * C), F32)], axis=0)
    stat_ref[...] = exact_dot(both, same_group(2 * C, 128, 20, 1))


def keep_mask(r, first_row, first_col):
    i = lax.broadcasted_iota(jnp.int32, (SEG, 1), 0)
    here = first_row + r
    row = jnp.where(i < 8, here - 1, here)
    col = first_col + jnp.where(i < 8, i + WIDE, i - GAP)
    good = (row >= 0) & (row < 128) & (col >= 0) & (col < 1024)
    return good.astype(F32)


def shift_add(merged_ref, start, size):
    back = merged_ref[pl.ds(start - 1, size), :]
    mid = merged_ref[pl.ds(start, size), :]
    ahead = merged_ref[pl.ds(start + 1, size), :]
    low = back[:, 0:128] + mid[:, 128:256] + ahead[:, 256:384]
    high = (
        back[:, 384:512]
        + pltpu.roll(mid[:, 384:512], 96, 1)
        + pltpu.roll(ahead[:, 384:512], 64, 1)
    )
    return jnp.concatenate([low, high[:, 0:32]], axis=1)


def first_kernel(
    place_ref, rows_ref, stat_ref, wm_ref, wpad_ref, gain_ref, shift_ref,
    hidden_ref, joined_ref, sum_ref,
    raw, act, merged,
):
    first_row, first_col = place_ref[0], place_ref[1]
    order = ((0, 3), (0, 0), (1, 0), (0, 1), (1, 1), (0, 2), (1, 2), (1, 3))
    sub = lax.broadcasted_iota(jnp.int32, (GAP, LANES), 0)
    zeros = jnp.zeros((GAP, LANES), BF16)
    raw[0:GAP, :] = zeros
    raw[GAP + A_LEN : GAP + A_LEN + GAP, :] = zeros
    for r in range(IN_ROWS + 1):
        after = rows_ref[order[r]] if r < IN_ROWS else None
        gap_right = rows_ref[order[r - 1]][WIDE:SEG].astype(F32) if r else jnp.zeros((GAP, LANES), F32)
        gap_left = after[WIDE:SEG].astype(F32) if r < IN_ROWS else gap_right
        raw[GAP + r * SEG : 2 * GAP + r * SEG, :] = jnp.where(sub < 8, gap_right, gap_left).astype(BF16)
        if r < IN_ROWS:
            raw[2 * GAP + r * SEG : GAP + (r + 1) * SEG, :] = after[0:WIDE]

    totals = jnp.sum(stat_ref[...], axis=0, keepdims=True) / (20.0 * 131072.0)
    mean = totals[:, 0:32]
    var = totals[:, 32:64] - mean * mean
    pair = jnp.concatenate([lax.rsqrt(var + EPS), mean, jnp.zeros((6, 32), F32)[:, :]], axis=0)
    spread = exact_dot(pair, same_group(32, 2 * C, 1, 20))
    scale = spread[0:1] * gain_ref[...] * 0.5
    offset = -spread[1:2] * scale

    def one(r, size):
        base = r * SEG
        tail = raw[rows_at(base, size + 2 * GAP), 256:384].astype(F32)
        skip = skip_of(tail, wpad_ref, GAP, GAP + size)
        joined = join(raw[rows_at(base + GAP, size), :].astype(F32), skip)
        values = silu_half(joined * scale + offset) * keep_mask(r, first_row, first_col)[0:size]
        act[rows_at(base, size), :] = values.astype(BF16)
        return joined.astype(BF16)

    def build(r, carry):
        joined = one(r, SEG)

        @pl.when((r >= 2) & (r < 6))
        def _():
            joined_ref[rows_at((r - 2) * SEG, SEG), :] = joined

        @pl.when(r == 6)
        def _():
            joined_ref[4 * SEG : B_LEN, :] = joined[0:GAP]

        return carry

    lax.fori_loop(0, IN_ROWS, build, 0)
    one(IN_ROWS, GAP)

    def conv(start, size):
        taps = [act[rows_at(start + a * SEG, size), :] for a in range(3)]
        merged[rows_at(start + GAP, size), :] = tap_dot(jnp.concatenate(taps, axis=1), wm_ref[...])

    merged[0:GAP, :] = jnp.zeros((GAP, MERGED), F32)
    merged[GAP + H_LEN : GAP + H_LEN + GAP, :] = jnp.zeros((GAP, MERGED), F32)

    def convs(i, carry):
        conv(i * 2 * SEG, 2 * SEG)
        return carry

    lax.fori_loop(0, 3, convs, 0)
    conv(6 * SEG, GAP)

    sums = jnp.zeros((1, HALF), F32)
    squares = jnp.zeros((1, HALF), F32)
    for r in range(MID_ROWS):
        values = shift_add(merged, GAP + r * SEG, SEG) + shift_ref[...]
        hidden_ref[r * SEG : (r + 1) * SEG, :] = values
        if r in (2, 3):
            sums = sums + jnp.sum(values[GAP:], axis=0, keepdims=True)
            squares = squares + jnp.sum(values[GAP:] * values[GAP:], axis=0, keepdims=True)
    hidden_ref[6 * SEG : H_LEN, :] = shift_add(merged, GAP + 6 * SEG, GAP) + shift_ref[...]
    sum_ref[...] = jnp.concatenate([sums, squares], axis=0)


def affine(stat_ref, gain_ref, core):
    both = jnp.sum(stat_ref[...], axis=0)
    found = []
    for which in (0, 1):
        sums = both[2 * which : 2 * which + 2]
        padded = jnp.concatenate([sums, jnp.zeros((6, HALF), F32)], axis=0)
        totals = exact_dot(padded, same_group(HALF, HALF, 10, 10)) / (10.0 * 131072.0)
        mean = totals[0:1]
        scale = lax.rsqrt(totals[1:2] - mean * mean + EPS) * gain_ref[which : which + 1] * 0.5
        found.append((scale, -mean * scale))
    (scale_0, offset_0), (scale_1, offset_1) = found
    first = core == 0
    own = (jnp.where(first, scale_0, scale_1), jnp.where(first, offset_0, offset_1))
    other = (jnp.where(first, scale_1, scale_0), jnp.where(first, offset_1, offset_0))
    return own, other


def second_kernel(
    place_ref, own_ref, other_ref, stat_ref, gain_ref, wm_ref, wskip_ref, joined_ref,
    block_ref, sum_ref,
    act_own, act_other, merged,
):
    first_row, first_col, core = place_ref[0] + 1, place_ref[1], place_ref[2]
    own, other = affine(stat_ref, gain_ref, core)

    def one(r, size):
        mask = keep_mask(r, first_row, first_col)[0:size]
        where = rows_at(r * SEG, size)
        for source, target, (scale, offset) in ((own_ref, act_own, own), (other_ref, act_other, other)):
            target[where, :] = (silu_half(source[where, :] * scale + offset) * mask).astype(BF16)

    def build(r, carry):
        one(r, SEG)
        return carry

    lax.fori_loop(0, MID_ROWS, build, 0)
    one(MID_ROWS, GAP)

    def conv(start, size):
        total = None
        for source, weights in ((act_own, wm_ref[core]), (act_other, wm_ref[1 - core])):
            for a in range(3):
                part = tap_dot(source[rows_at(start + a * SEG, size), :], weights[a * HALF : (a + 1) * HALF])
                total = part if total is None else total + part
        merged[rows_at(start + GAP, size), :] = total

    merged[0:GAP, :] = jnp.zeros((GAP, MERGED), F32)
    merged[GAP + B_LEN : GAP + B_LEN + GAP, :] = jnp.zeros((GAP, MERGED), F32)

    def convs(i, carry):
        conv(i * 2 * SEG, 2 * SEG)
        return carry

    lax.fori_loop(0, 2, convs, 0)
    conv(4 * SEG, GAP)

    sums = jnp.zeros((1, HALF), F32)
    squares = jnp.zeros((1, HALF), F32)
    for r in range(OUT_ROWS + 1):
        size = SEG if r < OUT_ROWS else GAP
        where = slice(r * SEG, r * SEG + size)
        values = shift_add(merged, GAP + r * SEG, size) + tap_dot(joined_ref[where, :], wskip_ref[...])
        block_ref[where, :] = values
        if r in (1, 2):
            sums = sums + jnp.sum(values[GAP:], axis=0, keepdims=True)
            squares = squares + jnp.sum(values[GAP:] * values[GAP:], axis=0, keepdims=True)
    sum_ref[...] = jnp.concatenate([sums, squares], axis=0)


def third_kernel(place_ref, own_ref, other_ref, stat_ref, gain_ref, wout_ref, noise_ref):
    core = place_ref[2]
    first_row, first_col = place_ref[0] + 2 + core, place_ref[1]
    own, other = affine(stat_ref, gain_ref, core)
    parts = []
    for r in range(4):
        size = SEG if r < 3 else GAP
        mask = keep_mask(r, first_row, first_col)[0:size]
        where = rows_at(core * SEG + r * SEG, size)
        total = None
        for source, (scale, offset), which in ((own_ref, own, core), (other_ref, other, 1 - core)):
            act = (silu_half(source[where, :] * scale + offset) * mask).astype(BF16)
            part = tap_dot(act, wout_ref[which])
            total = part if total is None else total + part
        parts.append(total)
    parts.append(jnp.zeros((896 - 3 * SEG - GAP, 128), F32))
    turned = jnp.concatenate(parts, axis=0).T
    noise = None
    for a in range(3):
        for b in range(3):
            tap = 3 * a + b
            at = a * SEG + GAP + b - 1
            piece = turned[8 * tap : 8 * tap + 8, at : at + WIDE]
            noise = piece if noise is None else noise + piece
    noise_ref[...] = noise[0:4]


def place_merged(out_ref, at, size, b, piece):
    out_ref[at : at + size, 128 * b : 128 * (b + 1)] = piece[:, 0:128]
    out_ref[at : at + size, 384 + 32 * b : 384 + 32 * (b + 1)] = piece[:, 128:160]


def front_weight_kernel(found_ref, out_ref):
    out_ref[:, 480:512] = jnp.zeros((3 * 2 * C, 32), BF16)
    for chunk in range(5760 // CHUNK):
        plane, j = divmod(chunk, 15)
        s, q = divmod(plane, 4)
        row = chunk * CHUNK
        end = row + CHUNK
        while row < end:
            tap, channel = divmod(row, 2 * C)
            size = min(end - row, 2 * C - channel)
            a, b = divmod(tap, 3)
            i = row - chunk * CHUNK
            piece = found_ref[j, 48 * s + i : 48 * s + i + size, 160 * q : 160 * (q + 1)]
            place_merged(out_ref, a * 2 * C + channel, size, b, piece)
            row += size


def middle_weight_kernel(found_ref, out_ref, skip_ref):
    out_ref[:, :, 480:512] = jnp.zeros((2, 3 * HALF, 32), BF16)
    for tap in range(9):
        a, b = divmod(tap, 3)
        for half in (0, 1):
            for part in (0, 1):
                row = tap * C + half * HALF + part * 80
                x, i = divmod(row, 720)
                piece = found_ref[x, i : i + 80, :]
                place_merged(out_ref.at[half], a * HALF + part * 80, 80, b, piece)
    for x in range(4):
        skip_ref[x * HALF : (x + 1) * HALF, :] = found_ref[x, 720:880, :]


def from_everyone(x, axis):
    count = lax.axis_size(axis)
    return lax.all_to_all(jnp.broadcast_to(x[None], (count, *x.shape)), axis, 0, 0, tiled=True)


def shifted(x, axis, step):
    count = lax.axis_size(axis)
    return lax.ppermute(x, axis, [(i, i + step) for i in range(count) if 0 <= i + step < count])


def summed_halves(sums):
    near = from_everyone(sums, PLANE).reshape(4, 2, 4, 2, HALF).sum(axis=(0, 2))
    return from_everyone(near.reshape(4, HALF), DEPTH)


def shards(
    latent, deep, timestep, in_weight, front_weight, middle_weight, skip_weight, out_weight,
    time_weight, time_second, time_proj, input_gain, middle_gain, output_gain,
):
    core, x, y = lax.axis_index("core"), lax.axis_index("x"), lax.axis_index("y")
    chip_row = 2 * (lax.axis_index(("zp", "zl", "y")))
    place = jnp.stack([chip_row - 3, x * WIDE, core]).astype(jnp.int32)

    halves = front_weight.reshape(45, 2, HALF).transpose(1, 0, 2)
    spread = jnp.broadcast_to(halves[None], (8, 2, 45, HALF)).reshape(16, 45, HALF)
    planes = lax.all_to_all(spread, ("zl", "y", "core"), 0, 0, tiled=True).reshape(720, HALF)
    planes = jnp.pad(planes, ((0, CHUNK), (0, 0)))
    mine = lax.dynamic_slice_in_dim(planes, CHUNK * (4 * y + x), CHUNK, 0)
    deepest = from_everyone(mine, "zp")
    dense = deepest.reshape(2, 4, CHUNK, HALF).transpose(0, 2, 1, 3).reshape(2 * CHUNK, 4 * HALF)
    front_found = lax.all_gather(dense, ("y", "x"), axis=0)

    wpad = in_weight.reshape(3, 3, 4, C).transpose(1, 0, 2, 3).reshape(3, 12, C)
    wpad = jnp.pad(wpad, ((0, 0), (64, 52), (64, 0))).reshape(LANES, LANES)
    above, below = shifted(latent, ROWS, 1), shifted(latent, ROWS, -1)
    cells, first, last = call(
        pack_kernel,
        (sds((WIDE, LANES), BF16), sds((GAP, LANES), BF16), sds((GAP, LANES), BF16)),
        [VMEM] * 4,
        [pltpu.VMEM((LANES, WIDE), F32)],
    )(deep.reshape(C, WIDE), above.reshape(4, WIDE), latent.reshape(4, WIDE), below.reshape(4, WIDE))
    from_right, from_left = shifted(first, "x", -1), shifted(last, "x", 1)
    row, stats = call(stats_kernel, (sds((SEG, LANES), BF16), sds((8, 128), F32)), [VMEM] * 4)(
        cells, from_left, from_right, wpad
    )

    count = lax.axis_size(ROWS)
    crossed = [(i, i + 3) if i % 2 else (i, i - 3) for i in range(count)]
    crossed = [(i, j) for i, j in crossed if 0 <= j < count]
    around = jnp.stack([shifted(row, ROWS, 2), row, shifted(row, ROWS, -2), lax.ppermute(row, ROWS, crossed)])
    rows = lax.all_gather(around, "core", axis=0)

    half_width = time_weight.shape[0] // 2
    ratios = jnp.exp(-math.log(10000.0) * jnp.arange(half_width, dtype=F32) / half_width)
    angles = timestep[0].astype(F32) * ratios
    features = jnp.concatenate([jnp.cos(angles), jnp.sin(angles)])
    depth_here = time_second.shape[0]
    weight_here = lax.dynamic_slice_in_dim(time_weight, x * depth_here, depth_here, 1)
    hidden = jax.nn.silu(jnp.dot(features, weight_here.astype(F32), precision=HIGH))
    columns = lax.dynamic_slice_in_dim(time_second, (2 * y + core) * HALF, HALF, 1)
    partial = jnp.dot(hidden, columns.astype(F32), precision=HIGH)

    sent = jnp.concatenate([stats[0, 0:32], stats[1, 0:32], partial])
    near = from_everyone(sent[None], PLANE).reshape(8, 4, 224)
    embedded = jax.nn.silu(near[:, :, 64:].sum(axis=1).reshape(8 * HALF))
    proj = lax.dynamic_slice_in_dim(time_proj, core * HALF, HALF, 1)
    time_shift = jnp.dot(embedded, proj.astype(F32), precision=HIGH)
    wide = from_everyone(near[:, :, 0:64].sum(axis=(0, 1))[None], DEPTH).reshape(16, 64)

    front = call(front_weight_kernel, sds((3 * 2 * C, MERGED), BF16), [VMEM])(front_found)
    hidden_own, joined, sums = call(
        first_kernel,
        (sds((H_LEN, HALF), F32), sds((B_LEN, 2 * C), BF16), sds((2, HALF), F32)),
        [SMEM] + [VMEM] * 6,
        [
            pltpu.VMEM((A_LEN + 2 * GAP, LANES), BF16),
            pltpu.VMEM((A_LEN, 2 * C), BF16),
            pltpu.VMEM((H_LEN + 2 * GAP, MERGED), F32),
        ],
    )(place, rows, wide, front, wpad, input_gain[None], time_shift[None])

    both = jnp.concatenate([middle_weight, skip_weight], axis=0).reshape(880, 2, HALF)
    kept = lax.dynamic_slice_in_dim(both, core, 1, 1).reshape(880, HALF)
    kept, front_found = lax.optimization_barrier((kept, front_found))
    middle_found = lax.all_gather(kept, "x", axis=0)
    middle, shortcut = call(
        middle_weight_kernel,
        (sds((2, 3 * HALF, MERGED), BF16), sds((2 * C, HALF), BF16)),
        [VMEM],
    )(middle_found)

    swap = [(0, 1), (1, 0)]
    hidden_other = lax.ppermute(hidden_own, "core", swap)
    block_own, sums = call(
        second_kernel,
        (sds((B_LEN, HALF), F32), sds((2, HALF), F32)),
        [SMEM] + [VMEM] * 7,
        [
            pltpu.VMEM((H_LEN, HALF), BF16),
            pltpu.VMEM((H_LEN, HALF), BF16),
            pltpu.VMEM((B_LEN + 2 * GAP, MERGED), F32),
        ],
    )(place, hidden_own, hidden_other, summed_halves(sums), middle_gain.reshape(2, HALF), middle, shortcut, joined)

    wout = out_weight.reshape(9, 2, HALF, 4).transpose(1, 2, 0, 3)
    wout = jnp.pad(jnp.pad(wout, ((0, 0), (0, 0), (0, 0), (0, 4))).reshape(2, HALF, 72), ((0, 0), (0, 0), (0, 56)))
    block_other = lax.ppermute(block_own, "core", swap)
    noise = call(third_kernel, sds((4, WIDE), F32), [SMEM] + [VMEM] * 5)(
        place, block_own, block_other, summed_halves(sums), output_gain.reshape(2, HALF), wout
    )
    return noise.reshape(4, 1, WIDE)


def solution(mesh):
    finer = Mesh(
        mesh.devices.reshape(8, 2, 4, 2, mesh.shape["cols"]), ("zp", "zl", "y", "core", "x")
    )
    in_specs = (
        P(None, ROWS, "x"),
        P(None, ROWS, "x"),
        P(),
        P(),
        P(ROWS, None),
        P("x", None),
        P("x", None),
        P(),
        P(),
        P("x", None),
        P(),
        P(),
        P(),
        P(),
    )
    return jax.shard_map(
        shards, mesh=finer, in_specs=in_specs, out_specs=P(None, ROWS, "x"), check_vma=False
    )
```

```python
import math

import jax
import jax.numpy as jnp
from jax import lax
from jax.experimental import pallas as pl
from jax.experimental.pallas import tpu as pltpu
from jax.sharding import Mesh
from jax.sharding import PartitionSpec as P

ROWS = ("zp", "zl", "y", "core")
DEPTH = ("zp", "zl")
PLANE = ("y", "core", "x")
EPS = 1e-05
F32 = jnp.float32
BF16 = jnp.bfloat16
HIGH = lax.Precision.HIGHEST

C = 320
HALF = 160
WIDE = 256
GAP = 16
SEG = WIDE + GAP
IN_ROWS = 8
MID_ROWS = 6
OUT_ROWS = 4
A_LEN = IN_ROWS * SEG + GAP
H_LEN = MID_ROWS * SEG + GAP
B_LEN = OUT_ROWS * SEG + GAP
MERGED = 512
LANES = 384
SWAP = 256
VMEM = pl.BlockSpec(memory_space=pltpu.VMEM)
SMEM = pl.BlockSpec(memory_space=pltpu.SMEM)


def call(kernel, out_shape, in_specs, scratch=(), limit=16):
    return pl.pallas_call(
        kernel,
        out_shape=out_shape,
        in_specs=in_specs,
        out_specs=jax.tree.map(lambda _: VMEM, out_shape),
        scratch_shapes=list(scratch),
        compiler_params=pltpu.CompilerParams(vmem_limit_bytes=limit * 1024 * 1024),
    )


def sds(shape, dtype):
    return jax.ShapeDtypeStruct(shape, dtype)


def rows_at(start, size):
    return pl.ds(pl.multiple_of(start, 16), size)


def same_group(n, m, size_n, size_m):
    i = lax.broadcasted_iota(jnp.int32, (n, m), 0)
    j = lax.broadcasted_iota(jnp.int32, (n, m), 1)
    return ((i // size_n) == (j // size_m)).astype(F32)


def exact_dot(a, b):
    return jnp.dot(a, b, preferred_element_type=F32, precision=HIGH)


def tap_dot(a, b):
    return jnp.dot(a, b, preferred_element_type=F32)


def silu_half(h):
    return h + h * jnp.tanh(h)


def pack_kernel(deep_ref, prev_ref, here_ref, next_ref, out_ref, first_ref, last_ref, tall):
    tall[0:C, :] = deep_ref[...].astype(F32)
    tall[C:LANES, :] = jnp.zeros((LANES - C, WIDE), F32)
    for i, ref in enumerate((prev_ref, here_ref, next_ref)):
        tall[C + 4 * i : C + 4 * i + 4, :] = ref[...].astype(F32)
    out = tall[...].T.astype(BF16)
    out_ref[...] = out
    first_ref[...] = out[0:GAP]
    last_ref[...] = out[WIDE - GAP : WIDE]


def skip_of(tail, wpad_ref, lo, hi):
    n = tail.shape[0]
    left = pltpu.roll(tail, 1, 0)[lo:hi].astype(BF16)
    right = pltpu.roll(tail, n - 1, 0)[lo:hi].astype(BF16)
    mid = tail[lo:hi].astype(BF16)
    stacked = jnp.concatenate([left, mid, right], axis=1)
    return tap_dot(stacked, wpad_ref[...]).astype(BF16).astype(F32)


def join(cells, skip):
    lane = lax.broadcasted_iota(jnp.int32, (cells.shape[0], 128), 1)
    mixed = jnp.where(lane < 64, cells[:, 256:384], skip[:, 0:128])
    return jnp.concatenate([cells[:, 0:256], mixed, skip[:, 128:384]], axis=1)


def stats_kernel(cells_ref, left_ref, right_ref, wpad_ref, row_ref, stat_ref):
    sub = lax.broadcasted_iota(jnp.int32, (GAP, LANES), 0)
    gap = jnp.where(sub < 8, right_ref[...].astype(F32), left_ref[...].astype(F32))
    cells = jnp.concatenate([cells_ref[...].astype(F32), gap], axis=0)
    row_ref[...] = cells.astype(BF16)
    skip = skip_of(cells[:, 256:384], wpad_ref, 0, WIDE)
    joined = join(cells[0:WIDE], skip)
    sums = jnp.sum(joined, axis=0, keepdims=True)
    squares = jnp.sum(joined * joined, axis=0, keepdims=True)
    both = jnp.concatenate([sums, squares, jnp.zeros((6, 2 * C), F32)], axis=0)
    stat_ref[...] = exact_dot(both, same_group(2 * C, 128, 20, 1))


def keep_mask(r, first_row, first_col):
    i = lax.broadcasted_iota(jnp.int32, (SEG, 1), 0)
    here = first_row + r
    row = jnp.where(i < 8, here - 1, here)
    col = first_col + jnp.where(i < 8, i + WIDE, i - GAP)
    good = (row >= 0) & (row < 128) & (col >= 0) & (col < 1024)
    return good.astype(F32)


def shift_add(merged_ref, start, size):
    back = merged_ref[pl.ds(start - 1, size), :]
    mid = merged_ref[pl.ds(start, size), :]
    ahead = merged_ref[pl.ds(start + 1, size), :]
    low = back[:, 0:128] + mid[:, 128:256] + ahead[:, 256:384]
    high = (
        back[:, 384:512]
        + pltpu.roll(mid[:, 384:512], 96, 1)
        + pltpu.roll(ahead[:, 384:512], 64, 1)
    )
    return jnp.concatenate([low, high[:, 0:32]], axis=1)


def join_kernel(place_ref, own_ref, other_ref, wpad_ref, joined_ref, raw):
    order = ((0, 3), (0, 0), (1, 0), (0, 1), (1, 1), (0, 2), (1, 2), (1, 3))
    sub = lax.broadcasted_iota(jnp.int32, (GAP, LANES), 0)
    zeros = jnp.zeros((GAP, LANES), BF16)
    raw[0:GAP, :] = zeros
    raw[GAP + A_LEN : GAP + A_LEN + GAP, :] = zeros

    def lay_out(sources):
        for r in range(IN_ROWS + 1):
            before, after = None, None
            if r:
                which, at = order[r - 1]
                before = sources[which][at, WIDE:SEG, :].astype(F32)
            if r < IN_ROWS:
                which, at = order[r]
                after = sources[which][at, WIDE:SEG, :].astype(F32)
                raw[2 * GAP + r * SEG : GAP + (r + 1) * SEG, :] = sources[which][at, 0:WIDE, :]
            before = after if before is None else before
            after = before if after is None else after
            raw[GAP + r * SEG : 2 * GAP + r * SEG, :] = jnp.where(sub < 8, before, after).astype(BF16)

    @pl.when(place_ref[2] == 0)
    def _():
        lay_out((own_ref, other_ref))

    @pl.when(place_ref[2] == 1)
    def _():
        lay_out((other_ref, own_ref))

    def one(r, size):
        base = r * SEG
        tail = raw[rows_at(base, size + 2 * GAP), 256:384].astype(F32)
        skip = skip_of(tail, wpad_ref, GAP, GAP + size)
        joined = join(raw[rows_at(base + GAP, size), :].astype(F32), skip)
        joined_ref[rows_at(base, size), :] = joined.astype(BF16)

    def build(r, carry):
        one(r, SEG)
        return carry

    lax.fori_loop(0, IN_ROWS, build, 0)
    one(IN_ROWS, GAP)


def first_kernel(
    place_ref, joined_ref, stat_ref, wm_ref, gain_ref, shift_ref,
    hidden_ref, sum_ref,
    act, merged,
):
    first_row, first_col = place_ref[0], place_ref[1]
    totals = jnp.sum(stat_ref[...], axis=0, keepdims=True) / (20.0 * 131072.0)
    mean = totals[:, 0:32]
    var = totals[:, 32:64] - mean * mean
    pair = jnp.concatenate([lax.rsqrt(var + EPS), mean, jnp.zeros((6, 32), F32)], axis=0)
    spread = exact_dot(pair, same_group(32, 2 * C, 1, 20))
    scale = spread[0:1] * gain_ref[...] * 0.5
    offset = -spread[1:2] * scale

    def build(r):
        where = slice(r * SEG, r * SEG + (SEG if r < IN_ROWS else GAP))
        mask = keep_mask(r, first_row, first_col)[0 : where.stop - where.start]
        for lane in range(0, 2 * C, 128):
            at = slice(lane, lane + 128)
            values = joined_ref[where, at].astype(F32) * scale[:, at] + offset[:, at]
            act[where, at] = (silu_half(values) * mask).astype(BF16)

    def conv(start, size):
        taps = [act[start + a * SEG : start + a * SEG + size, :] for a in range(3)]
        merged[start + GAP : start + GAP + size, :] = tap_dot(jnp.concatenate(taps, axis=1), wm_ref[...])

    merged[0:GAP, :] = jnp.zeros((GAP, MERGED), F32)
    merged[GAP + H_LEN : GAP + H_LEN + GAP, :] = jnp.zeros((GAP, MERGED), F32)
    for r in range(4):
        build(r)
    conv(0, 2 * SEG)
    build(4)
    build(5)
    conv(2 * SEG, 2 * SEG)
    for r in range(6, 9):
        build(r)
    conv(4 * SEG, 2 * SEG + GAP)

    sums = jnp.zeros((1, HALF), F32)
    squares = jnp.zeros((1, HALF), F32)
    for r in range(MID_ROWS + 1):
        size = SEG if r < MID_ROWS else GAP
        values = shift_add(merged, GAP + r * SEG, size) + shift_ref[...]
        hidden_ref[r * SEG : r * SEG + size, 0:HALF] = values
        if r in (2, 3):
            sums = sums + jnp.sum(values[GAP:], axis=0, keepdims=True)
            squares = squares + jnp.sum(values[GAP:] * values[GAP:], axis=0, keepdims=True)
    hidden_ref[:, HALF:SWAP] = jnp.zeros((H_LEN, SWAP - HALF), F32)
    sum_ref[...] = jnp.concatenate([sums, squares], axis=0)


def affine(stat_ref, gain_ref, core):
    both = jnp.sum(stat_ref[...], axis=0)
    found = []
    for which in (0, 1):
        sums = both[2 * which : 2 * which + 2]
        padded = jnp.concatenate([sums, jnp.zeros((6, HALF), F32)], axis=0)
        totals = exact_dot(padded, same_group(HALF, HALF, 10, 10)) / (10.0 * 131072.0)
        mean = totals[0:1]
        scale = lax.rsqrt(totals[1:2] - mean * mean + EPS) * gain_ref[which : which + 1] * 0.5
        found.append((scale, -mean * scale))
    (scale_0, offset_0), (scale_1, offset_1) = found
    first = core == 0
    own = (jnp.where(first, scale_0, scale_1), jnp.where(first, offset_0, offset_1))
    other = (jnp.where(first, scale_1, scale_0), jnp.where(first, offset_1, offset_0))
    return own, other


def second_kernel(
    place_ref, own_ref, other_ref, stat_ref, gain_ref, wm_ref, wskip_ref, joined_ref,
    block_ref, sum_ref,
    act_own, act_other, merged,
):
    first_row, first_col, core = place_ref[0] + 1, place_ref[1], place_ref[2]
    own, other = affine(stat_ref, gain_ref, core)

    def one(r, size):
        mask = keep_mask(r, first_row, first_col)[0:size]
        where = rows_at(r * SEG, size)
        for source, target, (scale, offset) in ((own_ref, act_own, own), (other_ref, act_other, other)):
            target[where, :] = (silu_half(source[where, 0:HALF] * scale + offset) * mask).astype(BF16)

    def build(r, carry):
        one(r, SEG)
        return carry

    lax.fori_loop(0, MID_ROWS, build, 0)
    one(MID_ROWS, GAP)

    def conv(start, size):
        total = None
        for source, weights in ((act_own, wm_ref[core]), (act_other, wm_ref[1 - core])):
            for a in range(3):
                part = tap_dot(source[rows_at(start + a * SEG, size), :], weights[a * HALF : (a + 1) * HALF])
                total = part if total is None else total + part
        merged[rows_at(start + GAP, size), :] = total

    merged[0:GAP, :] = jnp.zeros((GAP, MERGED), F32)
    merged[GAP + B_LEN : GAP + B_LEN + GAP, :] = jnp.zeros((GAP, MERGED), F32)

    def convs(i, carry):
        conv(i * 2 * SEG, 2 * SEG)
        return carry

    lax.fori_loop(0, 2, convs, 0)
    conv(4 * SEG, GAP)

    sums = jnp.zeros((1, HALF), F32)
    squares = jnp.zeros((1, HALF), F32)
    for r in range(OUT_ROWS + 1):
        size = SEG if r < OUT_ROWS else GAP
        where = slice(r * SEG, r * SEG + size)
        values = shift_add(merged, GAP + r * SEG, size) + tap_dot(
            joined_ref[2 * SEG + where.start : 2 * SEG + where.stop, :], wskip_ref[...]
        )
        block_ref[where, 0:HALF] = values
        if r in (1, 2):
            sums = sums + jnp.sum(values[GAP:], axis=0, keepdims=True)
            squares = squares + jnp.sum(values[GAP:] * values[GAP:], axis=0, keepdims=True)
    block_ref[:, HALF:SWAP] = jnp.zeros((B_LEN, SWAP - HALF), F32)
    sum_ref[...] = jnp.concatenate([sums, squares], axis=0)


def third_kernel(place_ref, own_ref, other_ref, stat_ref, gain_ref, wout_ref, noise_ref):
    core = place_ref[2]
    first_row, first_col = place_ref[0] + 2 + core, place_ref[1]
    own, other = affine(stat_ref, gain_ref, core)
    parts = []
    for r in range(4):
        size = SEG if r < 3 else GAP
        mask = keep_mask(r, first_row, first_col)[0:size]
        where = rows_at(core * SEG + r * SEG, size)
        total = None
        for source, (scale, offset), which in ((own_ref, own, core), (other_ref, other, 1 - core)):
            act = (silu_half(source[where, 0:HALF] * scale + offset) * mask).astype(BF16)
            part = tap_dot(act, wout_ref[which])
            total = part if total is None else total + part
        parts.append(total)
    parts.append(jnp.zeros((896 - 3 * SEG - GAP, 128), F32))
    turned = jnp.concatenate(parts, axis=0).T
    noise = None
    for a in range(3):
        for b in range(3):
            tap = 3 * a + b
            at = a * SEG + GAP + b - 1
            piece = turned[8 * tap : 8 * tap + 8, at : at + WIDE]
            noise = piece if noise is None else noise + piece
    noise_ref[...] = noise[0:4]


def place_merged(out_ref, at, size, b, piece):
    out_ref[at : at + size, 128 * b : 128 * (b + 1)] = piece[:, 0:128]
    out_ref[at : at + size, 384 + 32 * b : 384 + 32 * (b + 1)] = piece[:, 128:160]


def front_weight_kernel(found_ref, out_ref, rows):
    out_ref[:, 480:512] = jnp.zeros((3 * 2 * C, 32), BF16)
    to = lax.broadcasted_iota(jnp.int32, (360, 384), 0)
    source = lax.broadcasted_iota(jnp.int32, (360, 384), 1)
    j, rest = source // 24, source % 24
    part, i = rest // 12, rest % 12
    at = 12 * (j % 4) + i
    goal = 45 * (2 * (j // 4) + part) + at
    picks = ((to == goal) & (at < 45)).astype(BF16)
    for d in range(4):
        found = [found_ref[j, 24 * d : 24 * (d + 1), :].astype(F32) for j in range(16)]
        rows[360 * d : 360 * (d + 1), :] = tap_dot(picks, jnp.concatenate(found, axis=0).astype(BF16))
    for q in range(4):
        row = 1440 * q
        while row < 1440 * (q + 1):
            tap, channel = divmod(row, 2 * C)
            size = min(1440 * (q + 1) - row, 2 * C - channel)
            a, b = divmod(tap, 3)
            k = row - 1440 * q
            piece = rows[k : k + size, 160 * q : 160 * (q + 1)].astype(BF16)
            place_merged(out_ref, a * 2 * C + channel, size, b, piece)
            row += size


def middle_weight_kernel(found_ref, out_ref, skip_ref):
    out_ref[:, :, 480:512] = jnp.zeros((2, 3 * HALF, 32), BF16)

    def pieces(x, row, size):
        while size:
            q, i = divmod(row, 224)
            some = min(size, 224 - i)
            yield some, found_ref[x, i : i + some, 160 * q : 160 * (q + 1)]
            row, size = row + some, size - some

    for tap in range(9):
        a, b = divmod(tap, 3)
        for half in (0, 1):
            at = a * HALF
            for part in (0, 1):
                x, i = divmod(tap * C + half * HALF + part * 80, 720)
                for size, piece in pieces(x, i, 80):
                    place_merged(out_ref.at[half], at, size, b, piece)
                    at += size
    at = 0
    for x in range(4):
        for size, piece in pieces(x, 720, HALF):
            skip_ref[at : at + size, :] = piece
            at += size


def from_everyone(x, axis):
    count = lax.axis_size(axis)
    return lax.all_to_all(jnp.broadcast_to(x[None], (count, *x.shape)), axis, 0, 0, tiled=True)


def shifted(x, axis, step):
    count = lax.axis_size(axis)
    return lax.ppermute(x, axis, [(i, i + step) for i in range(count) if 0 <= i + step < count])


def summed_halves(sums):
    near = from_everyone(sums, PLANE).reshape(4, 2, 4, 2, HALF).sum(axis=(0, 2))
    return from_everyone(near.reshape(4, HALF), DEPTH)


def shards(
    latent, deep, timestep, in_weight, front_weight, middle_weight, skip_weight, out_weight,
    time_weight, time_second, time_proj, input_gain, middle_gain, output_gain,
):
    core, x, y = lax.axis_index("core"), lax.axis_index("x"), lax.axis_index("y")
    chip_row = 2 * (lax.axis_index(("zp", "zl", "y")))
    place = jnp.stack([chip_row - 3, x * WIDE, core]).astype(jnp.int32)

    swap = [(0, 1), (1, 0)]
    quarter = lax.dynamic_slice_in_dim(jnp.pad(front_weight, ((0, 3), (0, 0))), 12 * x, 12, 0)
    kept = lax.dynamic_slice_in_dim(quarter, core * HALF, HALF, 1)
    given = lax.dynamic_slice_in_dim(quarter, (1 - core) * HALF, HALF, 1)
    taken = lax.ppermute(given, "core", swap)
    first_core = core == 0
    mine = jnp.concatenate([jnp.where(first_core, kept, taken), jnp.where(first_core, taken, kept)], axis=0)
    deepest = from_everyone(mine, DEPTH)
    dense = deepest.reshape(4, 4, 24, HALF).transpose(1, 2, 0, 3).reshape(96, 4 * HALF)
    front_found = lax.all_gather(dense, ("y", "x"), axis=0)

    wpad = in_weight.reshape(3, 3, 4, C).transpose(1, 0, 2, 3).reshape(3, 12, C)
    wpad = jnp.pad(wpad, ((0, 0), (64, 52), (64, 0))).reshape(LANES, LANES)
    above, below = shifted(latent, ROWS, 1), shifted(latent, ROWS, -1)
    cells, first, last = call(
        pack_kernel,
        (sds((WIDE, LANES), BF16), sds((GAP, LANES), BF16), sds((GAP, LANES), BF16)),
        [VMEM] * 4,
        [pltpu.VMEM((LANES, WIDE), F32)],
    )(deep.reshape(C, WIDE), above.reshape(4, WIDE), latent.reshape(4, WIDE), below.reshape(4, WIDE))
    from_right, from_left = shifted(first, "x", -1), shifted(last, "x", 1)
    row, stats = call(stats_kernel, (sds((SEG, LANES), BF16), sds((8, 128), F32)), [VMEM] * 4)(
        cells, from_left, from_right, wpad
    )

    count = lax.axis_size(ROWS)
    crossed = [(i, i + 3) if i % 2 else (i, i - 3) for i in range(count)]
    crossed = [(i, j) for i, j in crossed if 0 <= j < count]
    around = jnp.stack([shifted(row, ROWS, 2), row, shifted(row, ROWS, -2), lax.ppermute(row, ROWS, crossed)])
    joined = call(
        join_kernel, sds((A_LEN, 2 * C), BF16), [SMEM] + [VMEM] * 3, [pltpu.VMEM((A_LEN + 2 * GAP, LANES), BF16)]
    )(place, around, lax.ppermute(around, "core", swap), wpad)

    half_width = time_weight.shape[0] // 2
    ratios = jnp.exp(-math.log(10000.0) * jnp.arange(half_width, dtype=F32) / half_width)
    angles = timestep[0].astype(F32) * ratios
    features = jnp.concatenate([jnp.cos(angles), jnp.sin(angles)])
    depth_here = time_second.shape[0]
    weight_here = lax.dynamic_slice_in_dim(time_weight, x * depth_here, depth_here, 1)
    hidden = jax.nn.silu(jnp.dot(features, weight_here.astype(F32), precision=HIGH))
    columns = lax.dynamic_slice_in_dim(time_second, (2 * y + core) * HALF, HALF, 1)
    partial = jnp.dot(hidden, columns.astype(F32), precision=HIGH)

    sent = jnp.concatenate([stats[0, 0:32], stats[1, 0:32], partial])
    near = from_everyone(sent[None], PLANE).reshape(8, 4, 224)
    embedded = jax.nn.silu(near[:, :, 64:].sum(axis=1).reshape(8 * HALF))
    proj = lax.dynamic_slice_in_dim(time_proj, core * HALF, HALF, 1)
    time_shift = jnp.dot(embedded, proj.astype(F32), precision=HIGH)
    wide = from_everyone(near[:, :, 0:64].sum(axis=(0, 1))[None], DEPTH).reshape(16, 64)

    front = call(
        front_weight_kernel, sds((3 * 2 * C, MERGED), BF16), [VMEM], [pltpu.VMEM((1440, 4 * HALF), F32)]
    )(front_found)
    hidden_own, sums = call(
        first_kernel,
        (sds((H_LEN, SWAP), F32), sds((2, HALF), F32)),
        [SMEM] + [VMEM] * 5,
        [pltpu.VMEM((A_LEN, 2 * C), BF16), pltpu.VMEM((H_LEN + 2 * GAP, MERGED), F32)],
        24,
    )(place, joined, wide, front, input_gain[None], time_shift[None])

    both = jnp.concatenate([middle_weight, skip_weight], axis=0).reshape(880, 2, HALF)
    kept = lax.dynamic_slice_in_dim(both, core, 1, 1).reshape(880, HALF)
    kept = jnp.pad(kept, ((0, 16), (0, 0))).reshape(4, 224, HALF).transpose(1, 0, 2).reshape(224, 4 * HALF)
    kept, front_found = lax.optimization_barrier((kept, front_found))
    middle_found = lax.all_gather(kept, "x", axis=0)
    middle, shortcut = call(
        middle_weight_kernel,
        (sds((2, 3 * HALF, MERGED), BF16), sds((2 * C, HALF), BF16)),
        [VMEM],
    )(middle_found)

    hidden_other = lax.ppermute(hidden_own, "core", swap)
    block_own, sums = call(
        second_kernel,
        (sds((B_LEN, SWAP), F32), sds((2, HALF), F32)),
        [SMEM] + [VMEM] * 7,
        [
            pltpu.VMEM((H_LEN, HALF), BF16),
            pltpu.VMEM((H_LEN, HALF), BF16),
            pltpu.VMEM((B_LEN + 2 * GAP, MERGED), F32),
        ],
    )(place, hidden_own, hidden_other, summed_halves(sums), middle_gain.reshape(2, HALF), middle, shortcut, joined)

    wout = out_weight.reshape(9, 2, HALF, 4).transpose(1, 2, 0, 3)
    wout = jnp.pad(jnp.pad(wout, ((0, 0), (0, 0), (0, 0), (0, 4))).reshape(2, HALF, 72), ((0, 0), (0, 0), (0, 56)))
    block_other = lax.ppermute(block_own, "core", swap)
    noise = call(third_kernel, sds((4, WIDE), F32), [SMEM] + [VMEM] * 5)(
        place, block_own, block_other, summed_halves(sums), output_gain.reshape(2, HALF), wout
    )
    return noise.reshape(4, 1, WIDE)


def solution(mesh):
    finer = Mesh(
        mesh.devices.reshape(8, 2, 4, 2, mesh.shape["cols"]), ("zp", "zl", "y", "core", "x")
    )
    in_specs = (
        P(None, ROWS, "x"),
        P(None, ROWS, "x"),
        P(),
        P(),
        P(ROWS, None),
        P("x", None),
        P("x", None),
        P(),
        P(),
        P("x", None),
        P(),
        P(),
        P(),
        P(),
    )
    return jax.shard_map(
        shards, mesh=finer, in_specs=in_specs, out_specs=P(None, ROWS, "x"), check_vma=False
    )
```

```python
import math

import jax
import jax.numpy as jnp
from jax import lax
from jax.experimental import pallas as pl
from jax.experimental.pallas import tpu as pltpu
from jax.sharding import Mesh
from jax.sharding import PartitionSpec as P

ROWS = ("zp", "zl", "y", "core")
DEPTH = ("zp", "zl")
PLANE = ("y", "core", "x")
EPS = 1e-05
F32 = jnp.float32
BF16 = jnp.bfloat16
HIGH = lax.Precision.HIGHEST

C = 320
HALF = 160
WIDE = 256
GAP = 16
SEG = WIDE + GAP
IN_ROWS = 8
MID_ROWS = 6
OUT_ROWS = 4
A_LEN = IN_ROWS * SEG + GAP
H_LEN = MID_ROWS * SEG + GAP
B_LEN = OUT_ROWS * SEG + GAP
MERGED = 512
LANES = 384
SWAP = 256
VMEM = pl.BlockSpec(memory_space=pltpu.VMEM)


def call(kernel, out_shape, in_specs, scratch=(), limit=16):
    return pl.pallas_call(
        kernel,
        out_shape=out_shape,
        in_specs=in_specs,
        out_specs=jax.tree.map(lambda _: VMEM, out_shape),
        scratch_shapes=list(scratch),
        compiler_params=pltpu.CompilerParams(vmem_limit_bytes=limit * 1024 * 1024),
    )


def sds(shape, dtype):
    return jax.ShapeDtypeStruct(shape, dtype)


def rows_at(start, size):
    return pl.ds(pl.multiple_of(start, 16), size)


def place():
    return 2 * lax.axis_index(("zp", "zl", "y")), lax.axis_index("x") * WIDE, lax.axis_index("core")


def same_group(n, m, size_n, size_m):
    i = lax.broadcasted_iota(jnp.int32, (n, m), 0)
    j = lax.broadcasted_iota(jnp.int32, (n, m), 1)
    return ((i // size_n) == (j // size_m)).astype(F32)


def exact_dot(a, b):
    return jnp.dot(a, b, preferred_element_type=F32, precision=HIGH)


def tap_dot(a, b):
    return jnp.dot(a, b, preferred_element_type=F32)


def silu_half(h):
    return h + h * jnp.tanh(h)


def pack_kernel(deep_ref, prev_ref, here_ref, next_ref, out_ref, first_ref, last_ref, tall):
    tall[0:C, :] = deep_ref[...].astype(F32)
    tall[C:LANES, :] = jnp.zeros((LANES - C, WIDE), F32)
    for i, ref in enumerate((prev_ref, here_ref, next_ref)):
        tall[C + 4 * i : C + 4 * i + 4, :] = ref[...].astype(F32)
    out = tall[...].T.astype(BF16)
    out_ref[...] = out
    first_ref[...] = out[0:GAP]
    last_ref[...] = out[WIDE - GAP : WIDE]


def skip_of(tail, wpad_ref, lo, hi):
    n = tail.shape[0]
    left = pltpu.roll(tail, 1, 0)[lo:hi].astype(BF16)
    right = pltpu.roll(tail, n - 1, 0)[lo:hi].astype(BF16)
    mid = tail[lo:hi].astype(BF16)
    stacked = jnp.concatenate([left, mid, right], axis=1)
    return tap_dot(stacked, wpad_ref[...]).astype(BF16).astype(F32)


def join(cells, skip):
    lane = lax.broadcasted_iota(jnp.int32, (cells.shape[0], 128), 1)
    mixed = jnp.where(lane < 64, cells[:, 256:384], skip[:, 0:128])
    return jnp.concatenate([cells[:, 0:256], mixed, skip[:, 128:384]], axis=1)


def three_terms(values):
    high = values.astype(BF16).astype(F32)
    middle = (values - high).astype(BF16).astype(F32)
    return high, middle, values - high - middle


def stats_kernel(cells_ref, left_ref, right_ref, wpad_ref, quarter_ref, row_ref, sent_ref):
    sub = lax.broadcasted_iota(jnp.int32, (GAP, LANES), 0)
    gap = jnp.where(sub < 8, right_ref[...].astype(F32), left_ref[...].astype(F32))
    cells = jnp.concatenate([cells_ref[...].astype(F32), gap], axis=0)
    row_ref[...] = cells.astype(BF16)
    skip = skip_of(cells[:, 256:384], wpad_ref, 0, WIDE)
    joined = join(cells[0:WIDE], skip)
    sums = jnp.sum(joined, axis=0, keepdims=True)
    squares = jnp.sum(joined * joined, axis=0, keepdims=True)
    both = jnp.concatenate([sums, squares, jnp.zeros((6, 2 * C), F32)], axis=0)
    grouped = exact_dot(both, same_group(2 * C, 32, 20, 1))
    terms = three_terms(jnp.concatenate([grouped[0:1], grouped[1:2]], axis=1))
    line = jnp.concatenate([*terms, jnp.zeros((1, C - 192), F32)], axis=1)
    message = jnp.concatenate([quarter_ref[...].astype(F32), line, jnp.zeros((3, C), F32)], axis=0).astype(BF16)
    for z in range(sent_ref.shape[0]):
        sent_ref[z] = message


def plane_kernel(got_ref, part_ref, sent_ref, rows):
    total = jnp.zeros((1, 64), F32)
    for z in range(16):
        got = got_ref[z].astype(F32)
        q, d = divmod(z, 4)
        for half in (0, 1):
            rows[half, 12 * d : 12 * d + 12, 160 * q : 160 * (q + 1)] = got[0:12, 160 * half : 160 * (half + 1)]
        total = total + got[12:13, 0:64] + got[12:13, 64:128] + got[12:13, 128:192]
    first = jnp.concatenate([*three_terms(total), jnp.zeros((1, 4 * HALF - 192), F32)], axis=1)
    second = jnp.concatenate([*three_terms(part_ref[...]), jnp.zeros((1, HALF), F32)], axis=1)
    tail = jnp.concatenate([first, second, jnp.zeros((6, 4 * HALF), F32)], axis=0).astype(BF16)
    for half in (0, 1):
        block = rows[half].astype(BF16)
        for y in range(4):
            for x in range(4):
                sent_ref[8 * y + 4 * half + x, 0:48, :] = block
                sent_ref[8 * y + 4 * half + x, 48:56, :] = tail


def keep_mask(r, first_row, first_col):
    i = lax.broadcasted_iota(jnp.int32, (SEG, 1), 0)
    here = first_row + r
    row = jnp.where(i < 8, here - 1, here)
    col = first_col + jnp.where(i < 8, i + WIDE, i - GAP)
    good = (row >= 0) & (row < 128) & (col >= 0) & (col < 1024)
    return good.astype(F32)


def shift_add(merged_ref, start, size):
    back = merged_ref[pl.ds(start - 1, size), :]
    mid = merged_ref[pl.ds(start, size), :]
    ahead = merged_ref[pl.ds(start + 1, size), :]
    low = back[:, 0:128] + mid[:, 128:256] + ahead[:, 256:384]
    high = (
        back[:, 384:512]
        + pltpu.roll(mid[:, 384:512], 96, 1)
        + pltpu.roll(ahead[:, 384:512], 64, 1)
    )
    return jnp.concatenate([low, high[:, 0:32]], axis=1)


def join_kernel(own_ref, other_ref, wpad_ref, joined_ref, raw):
    order = ((0, 3), (0, 0), (1, 0), (0, 1), (1, 1), (0, 2), (1, 2), (1, 3))
    sub = lax.broadcasted_iota(jnp.int32, (GAP, LANES), 0)
    zeros = jnp.zeros((GAP, LANES), BF16)
    raw[0:GAP, :] = zeros
    raw[GAP + A_LEN : GAP + A_LEN + GAP, :] = zeros

    def lay_out(sources):
        for r in range(IN_ROWS + 1):
            before, after = None, None
            if r:
                which, at = order[r - 1]
                before = sources[which][at, WIDE:SEG, :].astype(F32)
            if r < IN_ROWS:
                which, at = order[r]
                after = sources[which][at, WIDE:SEG, :].astype(F32)
                raw[2 * GAP + r * SEG : GAP + (r + 1) * SEG, :] = sources[which][at, 0:WIDE, :]
            before = after if before is None else before
            after = before if after is None else after
            raw[GAP + r * SEG : 2 * GAP + r * SEG, :] = jnp.where(sub < 8, before, after).astype(BF16)

    core = lax.axis_index("core")

    @pl.when(core == 0)
    def _():
        lay_out((own_ref, other_ref))

    @pl.when(core == 1)
    def _():
        lay_out((other_ref, own_ref))

    def one(r, size):
        base = r * SEG
        tail = raw[rows_at(base, size + 2 * GAP), 256:384].astype(F32)
        skip = skip_of(tail, wpad_ref, GAP, GAP + size)
        joined = join(raw[rows_at(base + GAP, size), :].astype(F32), skip)
        joined_ref[rows_at(base, size), :] = joined.astype(BF16)

    def build(r, carry):
        one(r, SEG)
        return carry

    lax.fori_loop(0, IN_ROWS, build, 0)
    one(IN_ROWS, GAP)


def first_kernel(
    joined_ref, stat_ref, wm_ref, gain_ref, shift_ref,
    hidden_ref, sum_ref,
    act, merged,
):
    chip_row, first_col, _ = place()
    first_row = chip_row - 3
    totals = stat_ref[...] / (20.0 * 131072.0)
    mean = totals[:, 0:32]
    var = totals[:, 32:64] - mean * mean
    pair = jnp.concatenate([lax.rsqrt(var + EPS), mean, jnp.zeros((6, 32), F32)], axis=0)
    spread = exact_dot(pair, same_group(32, 2 * C, 1, 20))
    scale = spread[0:1] * gain_ref[...] * 0.5
    offset = -spread[1:2] * scale

    def build(r):
        where = slice(r * SEG, r * SEG + (SEG if r < IN_ROWS else GAP))
        mask = keep_mask(r, first_row, first_col)[0 : where.stop - where.start]
        for lane in range(0, 2 * C, 128):
            at = slice(lane, lane + 128)
            values = joined_ref[where, at].astype(F32) * scale[:, at] + offset[:, at]
            act[where, at] = (silu_half(values) * mask).astype(BF16)

    def conv(start, size):
        taps = [act[start + a * SEG : start + a * SEG + size, :] for a in range(3)]
        merged[start + GAP : start + GAP + size, :] = tap_dot(jnp.concatenate(taps, axis=1), wm_ref[...])

    merged[0:GAP, :] = jnp.zeros((GAP, MERGED), F32)
    merged[GAP + H_LEN : GAP + H_LEN + GAP, :] = jnp.zeros((GAP, MERGED), F32)
    for r in range(4):
        build(r)
    conv(0, 2 * SEG)
    build(4)
    build(5)
    conv(2 * SEG, 2 * SEG)
    for r in range(6, 9):
        build(r)
    conv(4 * SEG, 2 * SEG + GAP)

    sums = jnp.zeros((1, HALF), F32)
    squares = jnp.zeros((1, HALF), F32)
    for r in range(MID_ROWS + 1):
        size = SEG if r < MID_ROWS else GAP
        values = shift_add(merged, GAP + r * SEG, size) + shift_ref[...]
        hidden_ref[r * SEG : r * SEG + size, 0:HALF] = values
        if r in (2, 3):
            sums = sums + jnp.sum(values[GAP:], axis=0, keepdims=True)
            squares = squares + jnp.sum(values[GAP:] * values[GAP:], axis=0, keepdims=True)
    hidden_ref[:, HALF:SWAP] = jnp.zeros((H_LEN, SWAP - HALF), F32)
    sum_ref[...] = jnp.concatenate([sums, squares], axis=0)


def affine(stat_ref, gain_ref):
    both = jnp.sum(stat_ref[...], axis=0)
    found = []
    for which in (0, 1):
        sums = both[2 * which : 2 * which + 2]
        padded = jnp.concatenate([sums, jnp.zeros((6, HALF), F32)], axis=0)
        totals = exact_dot(padded, same_group(HALF, HALF, 10, 10)) / (10.0 * 131072.0)
        mean = totals[0:1]
        scale = lax.rsqrt(totals[1:2] - mean * mean + EPS) * gain_ref[which : which + 1] * 0.5
        found.append((scale, -mean * scale))
    return found


def second_kernel(own_ref, other_ref, stat_ref, gain_ref, wm_ref, short_ref, block_ref, sum_ref, act, merged):
    chip_row, first_col, core = place()
    first_row = chip_row - 2
    affines = affine(stat_ref, gain_ref)
    first = core == 0

    def build(r):
        where = slice(r * SEG, r * SEG + (SEG if r < MID_ROWS else GAP))
        mask = keep_mask(r, first_row, first_col)[0 : where.stop - where.start]
        own, other = own_ref[where, 0:HALF], other_ref[where, 0:HALF]
        parts = []
        for which, (scale, offset) in enumerate(affines):
            values = jnp.where(first, own, other) if which == 0 else jnp.where(first, other, own)
            parts.append(silu_half(values * scale + offset) * mask)
        parts.append(jnp.zeros((where.stop - where.start, LANES - C), F32))
        act[where, :] = jnp.concatenate(parts, axis=1).astype(BF16)

    def conv(start, size):
        taps = [act[start + a * SEG : start + a * SEG + size, :] for a in range(3)]
        merged[start + GAP : start + GAP + size, :] = tap_dot(jnp.concatenate(taps, axis=1), wm_ref[...])

    merged[0:GAP, :] = jnp.zeros((GAP, MERGED), F32)
    merged[GAP + B_LEN : GAP + B_LEN + GAP, :] = jnp.zeros((GAP, MERGED), F32)
    for r in range(4):
        build(r)
    conv(0, 2 * SEG)
    for r in range(4, 7):
        build(r)
    conv(2 * SEG, 2 * SEG + GAP)

    sums = jnp.zeros((1, HALF), F32)
    squares = jnp.zeros((1, HALF), F32)
    for r in range(OUT_ROWS + 1):
        size = SEG if r < OUT_ROWS else GAP
        where = slice(r * SEG, r * SEG + size)
        values = shift_add(merged, GAP + r * SEG, size) + short_ref[where, :]
        block_ref[where, 0:HALF] = values
        if r in (1, 2):
            sums = sums + jnp.sum(values[GAP:], axis=0, keepdims=True)
            squares = squares + jnp.sum(values[GAP:] * values[GAP:], axis=0, keepdims=True)
    block_ref[:, HALF:SWAP] = jnp.zeros((B_LEN, SWAP - HALF), F32)
    sum_ref[...] = jnp.concatenate([sums, squares], axis=0)


def third_kernel(own_ref, other_ref, stat_ref, gain_ref, wout_ref, noise_ref):
    chip_row, first_col, core = place()
    first_row = chip_row - 1 + core
    affines = affine(stat_ref, gain_ref)
    first = core == 0
    parts = []
    for r in range(4):
        size = SEG if r < 3 else GAP
        mask = keep_mask(r, first_row, first_col)[0:size]
        where = rows_at(core * SEG + r * SEG, size)
        total = None
        own, other = own_ref[where, 0:HALF], other_ref[where, 0:HALF]
        for which, (scale, offset) in enumerate(affines):
            values = jnp.where(first, own, other) if which == 0 else jnp.where(first, other, own)
            act = (silu_half(values * scale + offset) * mask).astype(BF16)
            part = tap_dot(act, wout_ref[which])
            total = part if total is None else total + part
        parts.append(total)
    parts.append(jnp.zeros((896 - 3 * SEG - GAP, 128), F32))
    turned = jnp.concatenate(parts, axis=0).T
    noise = None
    for a in range(3):
        for b in range(3):
            tap = 3 * a + b
            at = a * SEG + GAP + b - 1
            piece = turned[8 * tap : 8 * tap + 8, at : at + WIDE]
            noise = piece if noise is None else noise + piece
    for o in range(4):
        noise_ref[o] = noise[o : o + 1]


def place_merged(out_ref, at, size, b, piece):
    out_ref[at : at + size, 128 * b : 128 * (b + 1)] = piece[:, 0:128]
    out_ref[at : at + size, 384 + 32 * b : 384 + 32 * (b + 1)] = piece[:, 128:160]


def front_weight_kernel(found_ref, proj_ref, out_ref, stat_ref, shift_ref, rows):
    out_ref[:, 480:512] = jnp.zeros((3 * 2 * C, 32), BF16)
    sums = jnp.zeros((1, 64), F32)
    embedded = []
    for shard in range(8):
        part = jnp.zeros((1, HALF), F32)
        for x in range(4):
            j = 4 * shard + x
            found = found_ref[j].astype(F32)
            size = 12 if x < 3 else 9
            for d in range(4):
                at = 360 * d + 45 * shard + 12 * x
                rows[at : at + size, :] = found[12 * d : 12 * d + size]
            for term in range(3):
                sums = sums + found[48:49, 64 * term : 64 * (term + 1)]
                part = part + found[49:50, HALF * term : HALF * (term + 1)]
        embedded.append(part)
    stat_ref[...] = jnp.concatenate([sums, jnp.zeros((1, 64), F32)], axis=1)
    values = jnp.concatenate(embedded, axis=0)
    values = jnp.concatenate([values / (1.0 + jnp.exp(-values)), jnp.zeros((8, WIDE - HALF), F32)], axis=1)
    turned = jnp.concatenate([values, jnp.zeros((120, WIDE), F32)], axis=0).T[0:HALF]
    shift = jnp.zeros((HALF, HALF), F32)
    for shard in range(8):
        shift = shift + turned[:, shard : shard + 1] * proj_ref[shard].astype(F32)
    shift_ref[...] = jnp.sum(shift, axis=0, keepdims=True)
    for q in range(4):
        row = 1440 * q
        while row < 1440 * (q + 1):
            tap, channel = divmod(row, 2 * C)
            size = min(1440 * (q + 1) - row, 2 * C - channel)
            a, b = divmod(tap, 3)
            k = row - 1440 * q
            piece = rows[k : k + size, 160 * q : 160 * (q + 1)].astype(BF16)
            place_merged(out_ref, a * 2 * C + channel, size, b, piece)
            row += size


def middle_weight_kernel(found_ref, joined_ref, out_ref, short_ref, skip):
    out_ref[:, 480:512] = jnp.zeros((3 * LANES, 32), BF16)

    def pieces(x, row, size):
        while size:
            q, i = divmod(row, 224)
            some = min(size, 224 - i)
            yield some, found_ref[x, i : i + some, 160 * q : 160 * (q + 1)]
            row, size = row + some, size - some

    for a in range(3):
        out_ref[a * LANES + C : (a + 1) * LANES, :] = jnp.zeros((LANES - C, MERGED), BF16)
    for tap in range(9):
        a, b = divmod(tap, 3)
        at = a * LANES
        for part in range(4):
            x, i = divmod(tap * C + part * 80, 720)
            for size, piece in pieces(x, i, 80):
                place_merged(out_ref, at, size, b, piece)
                at += size
    at = 0
    for x in range(4):
        for size, piece in pieces(x, 720, HALF):
            skip[at : at + size, :] = piece
            at += size
    short_ref[...] = tap_dot(joined_ref[2 * SEG : 2 * SEG + B_LEN, :], skip[...])


def from_everyone(x, axis):
    count = lax.axis_size(axis)
    return lax.all_to_all(jnp.broadcast_to(x[None], (count, *x.shape)), axis, 0, 0, tiled=True)


def shifted(x, axis, step):
    count = lax.axis_size(axis)
    return lax.ppermute(x, axis, [(i, i + step) for i in range(count) if 0 <= i + step < count])


def summed_halves(sums, kept):
    near = from_everyone(sums, PLANE).reshape(4, 2, 4, 2, HALF).sum(axis=(0, 2))
    near, kept = lax.optimization_barrier((near, kept))
    return from_everyone(near.reshape(4, HALF), DEPTH), kept


def shards(
    latent, deep, timestep, in_weight, front_weight, middle_weight, skip_weight, out_weight,
    time_weight, time_second, time_proj, input_gain, middle_gain, output_gain,
):
    core, x, y = lax.axis_index("core"), lax.axis_index("x"), lax.axis_index("y")
    depths = lax.axis_size(DEPTH)

    above, below = shifted(latent, ROWS, 1), shifted(latent, ROWS, -1)
    cells, first, last = call(
        pack_kernel,
        (sds((WIDE, LANES), BF16), sds((GAP, LANES), BF16), sds((GAP, LANES), BF16)),
        [VMEM] * 4,
        [pltpu.VMEM((LANES, WIDE), F32)],
    )(deep.reshape(C, WIDE), above.reshape(4, WIDE), latent.reshape(4, WIDE), below.reshape(4, WIDE))
    from_right, from_left = shifted(first, "x", -1), shifted(last, "x", 1)
    wpad = in_weight.reshape(3, 3, 4, C).transpose(1, 0, 2, 3).reshape(3, 12, C)
    wpad = jnp.pad(wpad, ((0, 0), (64, 52), (64, 0))).reshape(LANES, LANES)
    quarter = lax.dynamic_slice_in_dim(jnp.pad(front_weight, ((0, 3), (0, 0))), 12 * x, 12, 0)
    row, sent = call(stats_kernel, (sds((SEG, LANES), BF16), sds((depths, 16, C), BF16)), [VMEM] * 5)(
        cells, from_left, from_right, wpad, quarter
    )

    half_width = time_weight.shape[0] // 2
    ratios = jnp.exp(-math.log(10000.0) * jnp.arange(half_width, dtype=F32) / half_width)
    angles = timestep[0].astype(F32) * ratios
    features = jnp.concatenate([jnp.cos(angles), jnp.sin(angles)])
    depth_here = time_second.shape[0]
    weight_here = lax.dynamic_slice_in_dim(time_weight, x * depth_here, depth_here, 1)
    hidden = jax.nn.silu(jnp.dot(features, weight_here.astype(F32), precision=HIGH))
    columns = lax.dynamic_slice_in_dim(time_second, (2 * y + core) * HALF, HALF, 1)
    part = jnp.dot(hidden, columns.astype(F32), precision=HIGH)
    proj = lax.dynamic_slice_in_dim(time_proj, core * HALF, HALF, 1).reshape(8, HALF, HALF)

    got = lax.all_to_all(sent, DEPTH, 0, 0, tiled=True)
    sent = call(plane_kernel, sds((32, 56, 4 * HALF), BF16), [VMEM] * 2, [pltpu.VMEM((2, 48, 4 * HALF), F32)])(
        got, part[None]
    )
    found = lax.all_to_all(sent, PLANE, 0, 0, tiled=True)

    count = lax.axis_size(ROWS)
    crossed = [(i, i + 3) if i % 2 else (i, i - 3) for i in range(count)]
    crossed = [(i, j) for i, j in crossed if 0 <= j < count]
    around = jnp.stack([shifted(row, ROWS, 2), row, shifted(row, ROWS, -2), lax.ppermute(row, ROWS, crossed)])
    swap = [(0, 1), (1, 0)]
    joined = call(
        join_kernel, sds((A_LEN, 2 * C), BF16), [VMEM] * 3, [pltpu.VMEM((A_LEN + 2 * GAP, LANES), BF16)]
    )(around, lax.ppermute(around, "core", swap), wpad)

    both = jnp.concatenate([middle_weight, skip_weight], axis=0).reshape(880, 2, HALF)
    kept = lax.dynamic_slice_in_dim(both, core, 1, 1).reshape(880, HALF)
    kept = jnp.pad(kept, ((0, 16), (0, 0))).reshape(4, 224, HALF).transpose(1, 0, 2).reshape(224, 4 * HALF)
    kept, found = lax.optimization_barrier((kept, found))
    middle_found = lax.all_gather(kept, "x", axis=0)

    front, wide, time_shift = call(
        front_weight_kernel,
        (sds((3 * 2 * C, MERGED), BF16), sds((1, 128), F32), sds((1, HALF), F32)),
        [VMEM] * 2,
        [pltpu.VMEM((1440, 4 * HALF), F32)],
    )(found, proj)
    hidden_own, sums = call(
        first_kernel,
        (sds((H_LEN, SWAP), F32), sds((2, HALF), F32)),
        [VMEM] * 5,
        [pltpu.VMEM((A_LEN, 2 * C), BF16), pltpu.VMEM((H_LEN + 2 * GAP, MERGED), F32)],
        24,
    )(joined, wide, front, input_gain[None], time_shift)

    middle, shortcut = call(
        middle_weight_kernel,
        (sds((3 * LANES, MERGED), BF16), sds((B_LEN, HALF), F32)),
        [VMEM] * 2,
        [pltpu.VMEM((2 * C, HALF), BF16)],
    )(middle_found, joined)

    totals, hidden_own = summed_halves(sums, hidden_own)
    hidden_other = lax.ppermute(hidden_own, "core", swap)
    block_own, sums = call(
        second_kernel,
        (sds((B_LEN, SWAP), F32), sds((2, HALF), F32)),
        [VMEM] * 6,
        [pltpu.VMEM((H_LEN, LANES), BF16), pltpu.VMEM((B_LEN + 2 * GAP, MERGED), F32)],
    )(hidden_own, hidden_other, totals, middle_gain.reshape(2, HALF), middle, shortcut)

    wout = out_weight.reshape(9, 2, HALF, 4).transpose(1, 2, 0, 3)
    wout = jnp.pad(jnp.pad(wout, ((0, 0), (0, 0), (0, 0), (0, 4))).reshape(2, HALF, 72), ((0, 0), (0, 0), (0, 56)))
    totals, block_own = summed_halves(sums, block_own)
    block_other = lax.ppermute(block_own, "core", swap)
    return call(third_kernel, sds((4, 1, WIDE), F32), [VMEM] * 5)(
        block_own, block_other, totals, output_gain.reshape(2, HALF), wout
    )


def solution(mesh):
    finer = Mesh(
        mesh.devices.reshape(8, 2, 4, 2, mesh.shape["cols"]), ("zp", "zl", "y", "core", "x")
    )
    in_specs = (
        P(None, ROWS, "x"),
        P(None, ROWS, "x"),
        P(),
        P(),
        P(ROWS, None),
        P("x", None),
        P("x", None),
        P(),
        P(),
        P("x", None),
        P(),
        P(),
        P(),
        P(),
    )
    return jax.shard_map(
        shards, mesh=finer, in_specs=in_specs, out_specs=P(None, ROWS, "x"), check_vma=False
    )
```

```python
import math

import jax
import jax.numpy as jnp
from jax import lax
from jax.experimental import pallas as pl
from jax.experimental.pallas import tpu as pltpu
from jax.sharding import Mesh
from jax.sharding import PartitionSpec as P

ROWS = ("zp", "zl", "y", "core")
DEPTH = ("zp", "zl")
PLANE = ("y", "core", "x")
EPS = 1e-05
F32 = jnp.float32
BF16 = jnp.bfloat16
HIGH = lax.Precision.HIGHEST

C = 320
HALF = 160
WIDE = 256
GAP = 16
SEG = WIDE + GAP
IN_ROWS = 8
MID_ROWS = 6
OUT_ROWS = 4
A_LEN = IN_ROWS * SEG + GAP
H_LEN = MID_ROWS * SEG + GAP
B_LEN = OUT_ROWS * SEG + GAP
MERGED = 512
LANES = 384
SWAP = 256
VMEM = pl.BlockSpec(memory_space=pltpu.VMEM)
ANY = pl.BlockSpec(memory_space=pltpu.HBM)


def call(kernel, out_shape, in_specs, scratch=(), limit=16, out_spec=VMEM):
    return pl.pallas_call(
        kernel,
        out_shape=out_shape,
        in_specs=in_specs,
        out_specs=jax.tree.map(lambda _: out_spec, out_shape),
        scratch_shapes=list(scratch),
        compiler_params=pltpu.CompilerParams(vmem_limit_bytes=limit * 1024 * 1024),
    )


def sds(shape, dtype):
    return jax.ShapeDtypeStruct(shape, dtype)


def rows_at(start, size):
    return pl.ds(pl.multiple_of(start, 16), size)


def place():
    return 2 * lax.axis_index(("zp", "zl", "y")), lax.axis_index("x") * WIDE, lax.axis_index("core")


def same_group(n, m, size_n, size_m):
    i = lax.broadcasted_iota(jnp.int32, (n, m), 0)
    j = lax.broadcasted_iota(jnp.int32, (n, m), 1)
    return ((i // size_n) == (j // size_m)).astype(F32)


def exact_dot(a, b):
    return jnp.dot(a, b, preferred_element_type=F32, precision=HIGH)


def tap_dot(a, b):
    return jnp.dot(a, b, preferred_element_type=F32)


def silu_half(h):
    return h + h * jnp.tanh(h)


def pack_kernel(deep_ref, prev_ref, here_ref, next_ref, weight_ref, out_ref, first_ref, last_ref, wpad_ref, tall, wide):
    tall[0:C, :] = deep_ref[...].astype(F32)
    tall[C:LANES, :] = jnp.zeros((LANES - C, WIDE), F32)
    for i, ref in enumerate((prev_ref, here_ref, next_ref)):
        tall[C + 4 * i : C + 4 * i + 4, :] = ref[...].astype(F32)
    out = tall[...].T.astype(BF16)
    out_ref[...] = out
    first_ref[...] = out[0:GAP]
    last_ref[...] = out[WIDE - GAP : WIDE]
    wide[...] = jnp.zeros((LANES, LANES), F32)
    weight = weight_ref[...].astype(F32)
    for tap in range(9):
        a, b = divmod(tap, 3)
        at = 128 * b + 64 + 4 * a
        wide[at : at + 4, 64:LANES] = weight[4 * tap : 4 * tap + 4]
    wpad_ref[...] = wide[...].astype(BF16)


def skip_of(tail, wpad_ref, lo, hi):
    n = tail.shape[0]
    left = pltpu.roll(tail, 1, 0)[lo:hi].astype(BF16)
    right = pltpu.roll(tail, n - 1, 0)[lo:hi].astype(BF16)
    mid = tail[lo:hi].astype(BF16)
    stacked = jnp.concatenate([left, mid, right], axis=1)
    return tap_dot(stacked, wpad_ref[...]).astype(BF16).astype(F32)


def join(cells, skip):
    lane = lax.broadcasted_iota(jnp.int32, (cells.shape[0], 128), 1)
    mixed = jnp.where(lane < 64, cells[:, 256:384], skip[:, 0:128])
    return jnp.concatenate([cells[:, 0:256], mixed, skip[:, 128:384]], axis=1)


def three_terms(values):
    high = values.astype(BF16).astype(F32)
    middle = (values - high).astype(BF16).astype(F32)
    return high, middle, values - high - middle


def stats_kernel(cells_ref, left_ref, right_ref, wpad_ref, quarter_ref, row_ref, sent_ref):
    sub = lax.broadcasted_iota(jnp.int32, (GAP, LANES), 0)
    gap = jnp.where(sub < 8, right_ref[...].astype(F32), left_ref[...].astype(F32))
    cells = jnp.concatenate([cells_ref[...].astype(F32), gap], axis=0)
    row_ref[...] = cells.astype(BF16)
    skip = skip_of(cells[:, 256:384], wpad_ref, 0, WIDE)
    joined = join(cells[0:WIDE], skip)
    sums = jnp.sum(joined, axis=0, keepdims=True)
    squares = jnp.sum(joined * joined, axis=0, keepdims=True)
    both = jnp.concatenate([sums, squares, jnp.zeros((6, 2 * C), F32)], axis=0)
    grouped = exact_dot(both, same_group(2 * C, 32, 20, 1))
    terms = three_terms(jnp.concatenate([grouped[0:1], grouped[1:2]], axis=1))
    line = jnp.concatenate([*terms, jnp.zeros((1, C - 192), F32)], axis=1)
    message = jnp.concatenate([quarter_ref[...].astype(F32), line, jnp.zeros((3, C), F32)], axis=0).astype(BF16)
    for z in range(sent_ref.shape[0]):
        sent_ref[z] = message


def plane_kernel(got_ref, part_ref, sent_hbm, rows, blocks, sems):
    total = jnp.zeros((1, 64), F32)
    for z in range(16):
        got = got_ref[z].astype(F32)
        q, d = divmod(z, 4)
        for half in (0, 1):
            rows[half, 12 * d : 12 * d + 12, 160 * q : 160 * (q + 1)] = got[0:12, 160 * half : 160 * (half + 1)]
        total = total + got[12:13, 0:64] + got[12:13, 64:128] + got[12:13, 128:192]
    first = jnp.concatenate([*three_terms(total), jnp.zeros((1, 4 * HALF - 192), F32)], axis=1)
    second = jnp.concatenate([*three_terms(part_ref[...]), jnp.zeros((1, HALF), F32)], axis=1)
    tail = jnp.concatenate([first, second, jnp.zeros((6, 4 * HALF), F32)], axis=0).astype(BF16)
    copies = []
    for half in (0, 1):
        blocks[half, 0:48, :] = rows[half].astype(BF16)
        blocks[half, 48:56, :] = tail
        for i in range(16):
            goal = 8 * (i // 4) + 4 * half + i % 4
            copies.append(pltpu.make_async_copy(blocks.at[half], sent_hbm.at[goal], sems.at[goal]))
            copies[-1].start()
    for copy in copies:
        copy.wait()


def keep_mask(r, first_row, first_col):
    i = lax.broadcasted_iota(jnp.int32, (SEG, 1), 0)
    here = first_row + r
    row = jnp.where(i < 8, here - 1, here)
    col = first_col + jnp.where(i < 8, i + WIDE, i - GAP)
    good = (row >= 0) & (row < 128) & (col >= 0) & (col < 1024)
    return good.astype(F32)


def shift_add(merged_ref, start, size):
    back = merged_ref[pl.ds(start - 1, size), :]
    mid = merged_ref[pl.ds(start, size), :]
    ahead = merged_ref[pl.ds(start + 1, size), :]
    low = back[:, 0:128] + mid[:, 128:256] + ahead[:, 256:384]
    high = (
        back[:, 384:512]
        + pltpu.roll(mid[:, 384:512], 96, 1)
        + pltpu.roll(ahead[:, 384:512], 64, 1)
    )
    return jnp.concatenate([low, high[:, 0:32]], axis=1)


def join_kernel(own_ref, other_ref, wpad_ref, joined_ref, raw):
    order = ((0, 3), (0, 0), (1, 0), (0, 1), (1, 1), (0, 2), (1, 2), (1, 3))
    sub = lax.broadcasted_iota(jnp.int32, (GAP, LANES), 0)
    zeros = jnp.zeros((GAP, LANES), BF16)
    raw[0:GAP, :] = zeros
    raw[GAP + A_LEN : GAP + A_LEN + GAP, :] = zeros

    def lay_out(sources):
        for r in range(IN_ROWS + 1):
            before, after = None, None
            if r:
                which, at = order[r - 1]
                before = sources[which][at, WIDE:SEG, :].astype(F32)
            if r < IN_ROWS:
                which, at = order[r]
                after = sources[which][at, WIDE:SEG, :].astype(F32)
                raw[2 * GAP + r * SEG : GAP + (r + 1) * SEG, :] = sources[which][at, 0:WIDE, :]
            before = after if before is None else before
            after = before if after is None else after
            raw[GAP + r * SEG : 2 * GAP + r * SEG, :] = jnp.where(sub < 8, before, after).astype(BF16)

    core = lax.axis_index("core")

    @pl.when(core == 0)
    def _():
        lay_out((own_ref, other_ref))

    @pl.when(core == 1)
    def _():
        lay_out((other_ref, own_ref))

    def one(r, size):
        base = r * SEG
        tail = raw[rows_at(base, size + 2 * GAP), 256:384].astype(F32)
        skip = skip_of(tail, wpad_ref, GAP, GAP + size)
        joined = join(raw[rows_at(base + GAP, size), :].astype(F32), skip)
        joined_ref[rows_at(base, size), :] = joined.astype(BF16)

    def build(r, carry):
        one(r, SEG)
        return carry

    lax.fori_loop(0, IN_ROWS, build, 0)
    one(IN_ROWS, GAP)


def first_kernel(
    joined_hbm, found_hbm, proj_ref, gain_ref,
    hidden_ref, sum_ref,
    joined_ref, found_ref, rows, wm_ref, act, merged, sems,
):
    copies = [pltpu.make_async_copy(found_hbm, found_ref, sems.at[0])]
    for i, part in enumerate((slice(0, 4 * SEG), slice(4 * SEG, A_LEN))):
        copies.append(pltpu.make_async_copy(joined_hbm.at[part], joined_ref.at[part], sems.at[i + 1]))
    for copy in copies:
        copy.start()
    copies[0].wait()
    chip_row, first_col, _ = place()
    first_row = chip_row - 3
    sums, shift = front_weight(found_ref, proj_ref, wm_ref, rows)
    totals = sums / (20.0 * 131072.0)
    mean = totals[:, 0:32]
    var = totals[:, 32:64] - mean * mean
    pair = jnp.concatenate([lax.rsqrt(var + EPS), mean, jnp.zeros((6, 32), F32)], axis=0)
    spread = exact_dot(pair, same_group(32, 2 * C, 1, 20))
    scale = spread[0:1] * gain_ref[...] * 0.5
    offset = -spread[1:2] * scale

    def build(r):
        where = slice(r * SEG, r * SEG + (SEG if r < IN_ROWS else GAP))
        mask = keep_mask(r, first_row, first_col)[0 : where.stop - where.start]
        for lane in range(0, 2 * C, 128):
            at = slice(lane, lane + 128)
            values = joined_ref[where, at].astype(F32) * scale[:, at] + offset[:, at]
            act[where, at] = (silu_half(values) * mask).astype(BF16)

    def conv(start, size):
        taps = [act[start + a * SEG : start + a * SEG + size, :] for a in range(3)]
        merged[start + GAP : start + GAP + size, :] = tap_dot(jnp.concatenate(taps, axis=1), wm_ref[...])

    merged[0:GAP, :] = jnp.zeros((GAP, MERGED), F32)
    merged[GAP + H_LEN : GAP + H_LEN + GAP, :] = jnp.zeros((GAP, MERGED), F32)
    copies[1].wait()
    for r in range(4):
        build(r)
    copies[2].wait()
    conv(0, 2 * SEG)
    build(4)
    build(5)
    conv(2 * SEG, 2 * SEG)
    for r in range(6, 9):
        build(r)
    conv(4 * SEG, 2 * SEG + GAP)

    sums = jnp.zeros((1, HALF), F32)
    squares = jnp.zeros((1, HALF), F32)
    for r in range(MID_ROWS + 1):
        size = SEG if r < MID_ROWS else GAP
        values = shift_add(merged, GAP + r * SEG, size) + shift
        hidden_ref[r * SEG : r * SEG + size, 0:HALF] = values
        if r in (2, 3):
            sums = sums + jnp.sum(values[GAP:], axis=0, keepdims=True)
            squares = squares + jnp.sum(values[GAP:] * values[GAP:], axis=0, keepdims=True)
    hidden_ref[:, HALF:SWAP] = jnp.zeros((H_LEN, SWAP - HALF), F32)
    send_sums(sums, squares, sum_ref)


def send_sums(sums, squares, sent_ref):
    both = jnp.concatenate([sums, squares, jnp.zeros((6, HALF), F32)], axis=0)
    grouped = exact_dot(both, same_group(HALF, 16, 10, 1))
    line = jnp.concatenate([grouped[0:1], grouped[1:2], jnp.zeros((1, 96), F32)], axis=1)
    for i in range(32):
        sent_ref[i] = line


def plane_sums_kernel(got_ref, sent_ref):
    cores = [jnp.zeros((1, 32), F32), jnp.zeros((1, 32), F32)]
    for i in range(32):
        half = (i // 4) % 2
        cores[half] = cores[half] + got_ref[i][:, 0:32]
    line = jnp.concatenate([*cores, jnp.zeros((1, 64), F32)], axis=1)
    for i in range(sent_ref.shape[0]):
        sent_ref[i] = line


def affine(stat_ref, gain_ref):
    both = stat_ref[0]
    for i in range(1, stat_ref.shape[0]):
        both = both + stat_ref[i]
    found = []
    for which in (0, 1):
        at = 32 * which
        padded = jnp.concatenate([both[:, at : at + 16], both[:, at + 16 : at + 32], jnp.zeros((6, 16), F32)], axis=0)
        totals = exact_dot(padded, same_group(16, HALF, 1, 10)) / (10.0 * 131072.0)
        mean = totals[0:1]
        scale = lax.rsqrt(totals[1:2] - mean * mean + EPS) * gain_ref[which : which + 1] * 0.5
        found.append((scale, -mean * scale))
    return found


def second_kernel(
    own_hbm, other_hbm, stat_ref, gain_ref, found_hbm, joined_hbm,
    block_ref, sum_ref,
    own_ref, other_ref, found_ref, joined_ref, wm_ref, skip, act, merged, sems,
):
    early, late = slice(0, 4 * SEG), slice(4 * SEG, H_LEN)
    copies = [
        pltpu.make_async_copy(own_hbm.at[early], own_ref.at[early], sems.at[0]),
        pltpu.make_async_copy(other_hbm.at[early], other_ref.at[early], sems.at[1]),
        pltpu.make_async_copy(found_hbm, found_ref, sems.at[2]),
        pltpu.make_async_copy(own_hbm.at[late], own_ref.at[late], sems.at[3]),
        pltpu.make_async_copy(other_hbm.at[late], other_ref.at[late], sems.at[4]),
        pltpu.make_async_copy(joined_hbm.at[2 * SEG : 2 * SEG + B_LEN], joined_ref, sems.at[5]),
    ]
    for copy in copies:
        copy.start()
    chip_row, first_col, core = place()
    first_row = chip_row - 2
    affines = affine(stat_ref, gain_ref)
    first = core == 0

    def build(r):
        where = slice(r * SEG, r * SEG + (SEG if r < MID_ROWS else GAP))
        mask = keep_mask(r, first_row, first_col)[0 : where.stop - where.start]
        own, other = own_ref[where, 0:HALF], other_ref[where, 0:HALF]
        parts = []
        for which, (scale, offset) in enumerate(affines):
            values = jnp.where(first, own, other) if which == 0 else jnp.where(first, other, own)
            parts.append(silu_half(values * scale + offset) * mask)
        parts.append(jnp.zeros((where.stop - where.start, LANES - C), F32))
        act[where, :] = jnp.concatenate(parts, axis=1).astype(BF16)

    def conv(start, size):
        taps = [act[start + a * SEG : start + a * SEG + size, :] for a in range(3)]
        merged[start + GAP : start + GAP + size, :] = tap_dot(jnp.concatenate(taps, axis=1), wm_ref[...])

    merged[0:GAP, :] = jnp.zeros((GAP, MERGED), F32)
    merged[GAP + B_LEN : GAP + B_LEN + GAP, :] = jnp.zeros((GAP, MERGED), F32)
    copies[0].wait()
    copies[1].wait()
    for r in range(4):
        build(r)
    copies[2].wait()
    middle_weight(found_ref, wm_ref, skip)
    copies[3].wait()
    copies[4].wait()
    conv(0, 2 * SEG)
    for r in range(4, 7):
        build(r)
    conv(2 * SEG, 2 * SEG + GAP)
    copies[5].wait()

    sums = jnp.zeros((1, HALF), F32)
    squares = jnp.zeros((1, HALF), F32)
    for r in range(OUT_ROWS + 1):
        size = SEG if r < OUT_ROWS else GAP
        where = slice(r * SEG, r * SEG + size)
        values = shift_add(merged, GAP + r * SEG, size) + tap_dot(joined_ref[where, :], skip[...])
        block_ref[where, 0:HALF] = values
        if r in (1, 2):
            sums = sums + jnp.sum(values[GAP:], axis=0, keepdims=True)
            squares = squares + jnp.sum(values[GAP:] * values[GAP:], axis=0, keepdims=True)
    block_ref[:, HALF:SWAP] = jnp.zeros((B_LEN, SWAP - HALF), F32)
    send_sums(sums, squares, sum_ref)


def third_kernel(own_hbm, other_hbm, stat_ref, gain_ref, wout_ref, noise_ref, own_ref, other_ref, sems):
    chip_row, first_col, core = place()
    needed = pl.ds(pl.multiple_of(core * SEG, 16), 3 * SEG + GAP)
    copies = [
        pltpu.make_async_copy(own_hbm.at[needed], own_ref, sems.at[0]),
        pltpu.make_async_copy(other_hbm.at[needed], other_ref, sems.at[1]),
    ]
    for copy in copies:
        copy.start()
    first_row = chip_row - 1 + core
    affines = affine(stat_ref, gain_ref)
    first = core == 0
    for copy in copies:
        copy.wait()
    parts = []
    for r in range(4):
        size = SEG if r < 3 else GAP
        mask = keep_mask(r, first_row, first_col)[0:size]
        where = slice(r * SEG, r * SEG + size)
        total = None
        own, other = own_ref[where, 0:HALF], other_ref[where, 0:HALF]
        for which, (scale, offset) in enumerate(affines):
            values = jnp.where(first, own, other) if which == 0 else jnp.where(first, other, own)
            act = (silu_half(values * scale + offset) * mask).astype(BF16)
            part = tap_dot(act, wout_ref[which])
            total = part if total is None else total + part
        parts.append(total)
    parts.append(jnp.zeros((896 - 3 * SEG - GAP, 128), F32))
    turned = jnp.concatenate(parts, axis=0).T
    noise = None
    for a in range(3):
        for b in range(3):
            tap = 3 * a + b
            at = a * SEG + GAP + b - 1
            piece = turned[8 * tap : 8 * tap + 8, at : at + WIDE]
            noise = piece if noise is None else noise + piece
    for o in range(4):
        noise_ref[o] = noise[o : o + 1]


def place_merged(out_ref, at, size, b, piece):
    out_ref[at : at + size, 128 * b : 128 * (b + 1)] = piece[:, 0:128]
    out_ref[at : at + size, 384 + 32 * b : 384 + 32 * (b + 1)] = piece[:, 128:160]


def front_weight(found_ref, proj_ref, out_ref, rows):
    out_ref[:, 480:512] = jnp.zeros((3 * 2 * C, 32), BF16)
    sums = jnp.zeros((1, 64), F32)
    embedded = []
    for shard in range(8):
        part = jnp.zeros((1, HALF), F32)
        for x in range(4):
            j = 4 * shard + x
            found = found_ref[j].astype(F32)
            size = 12 if x < 3 else 9
            for d in range(4):
                at = 360 * d + 45 * shard + 12 * x
                rows[at : at + size, :] = found[12 * d : 12 * d + size]
            for term in range(3):
                sums = sums + found[48:49, 64 * term : 64 * (term + 1)]
                part = part + found[49:50, HALF * term : HALF * (term + 1)]
        embedded.append(part)
    values = jnp.concatenate(embedded, axis=1)
    values = values / (1.0 + jnp.exp(-values))
    proj = proj_ref[rows_at(lax.axis_index("core") * HALF, HALF), :].astype(F32)
    shift = jnp.sum(proj * values, axis=1, keepdims=True)
    shift = jnp.concatenate([jnp.broadcast_to(shift, (HALF, 128)), jnp.zeros((WIDE - HALF, 128), F32)], axis=0)
    shift = shift.T[0:1, 0:HALF]
    for q in range(4):
        row = 1440 * q
        while row < 1440 * (q + 1):
            tap, channel = divmod(row, 2 * C)
            size = min(1440 * (q + 1) - row, 2 * C - channel)
            a, b = divmod(tap, 3)
            k = row - 1440 * q
            piece = rows[k : k + size, 160 * q : 160 * (q + 1)].astype(BF16)
            place_merged(out_ref, a * 2 * C + channel, size, b, piece)
            row += size
    return sums, shift


def share_kernel(middle_ref, skip_ref, out_ref):
    core = lax.axis_index("core")
    middle = middle_ref[rows_at(core * HALF, HALF), :].astype(F32).T
    wide = skip_ref[...].astype(F32)
    skip = jnp.where(core == 0, wide[:, 0:HALF], wide[:, HALF:C])
    whole = jnp.concatenate([middle, skip, jnp.zeros((16, HALF), F32)], axis=0)
    parts = [whole[224 * q : 224 * (q + 1)] for q in range(4)]
    out_ref[...] = jnp.concatenate(parts, axis=1).astype(BF16)


def middle_weight(found_ref, out_ref, skip_ref):
    out_ref[:, 480:512] = jnp.zeros((3 * LANES, 32), BF16)

    def pieces(x, row, size):
        while size:
            q, i = divmod(row, 224)
            some = min(size, 224 - i)
            yield some, found_ref[x, i : i + some, 160 * q : 160 * (q + 1)]
            row, size = row + some, size - some

    for a in range(3):
        out_ref[a * LANES + C : (a + 1) * LANES, :] = jnp.zeros((LANES - C, MERGED), BF16)
    for tap in range(9):
        a, b = divmod(tap, 3)
        at = a * LANES
        for part in range(4):
            x, i = divmod(tap * C + part * 80, 720)
            for size, piece in pieces(x, i, 80):
                place_merged(out_ref, at, size, b, piece)
                at += size
    at = 0
    for x in range(4):
        for size, piece in pieces(x, 720, HALF):
            skip_ref[at : at + size, :] = piece
            at += size


def shifted(x, axis, step):
    count = lax.axis_size(axis)
    return lax.ppermute(x, axis, [(i, i + step) for i in range(count) if 0 <= i + step < count])


def summed(sums, kept):
    near = lax.all_to_all(sums, PLANE, 0, 0, tiled=True)
    near = call(plane_sums_kernel, sds((lax.axis_size(DEPTH), 1, 128), F32), [VMEM])(near)
    near, kept = lax.optimization_barrier((near, kept))
    return lax.all_to_all(near, DEPTH, 0, 0, tiled=True), kept


def shards(
    latent, deep, timestep, in_weight, front_weight, middle_weight, skip_weight, out_weight,
    time_weight, time_second, time_proj, input_gain, middle_gain, output_gain,
):
    core, x, y = lax.axis_index("core"), lax.axis_index("x"), lax.axis_index("y")
    depths = lax.axis_size(DEPTH)

    packed = call(share_kernel, sds((224, 4 * HALF), BF16), [VMEM] * 2)(middle_weight.T, skip_weight)

    above, below = shifted(latent, ROWS, 1), shifted(latent, ROWS, -1)
    quarter = lax.dynamic_slice_in_dim(jnp.pad(front_weight, ((0, 3), (0, 0))), 12 * x, 12, 0)
    above, packed, quarter = lax.optimization_barrier((above, packed, quarter))
    cells, first, last, wpad = call(
        pack_kernel,
        (sds((WIDE, LANES), BF16), sds((GAP, LANES), BF16), sds((GAP, LANES), BF16), sds((LANES, LANES), BF16)),
        [VMEM] * 5,
        [pltpu.VMEM((LANES, WIDE), F32), pltpu.VMEM((LANES, LANES), F32)],
    )(deep.reshape(C, WIDE), above.reshape(4, WIDE), latent.reshape(4, WIDE), below.reshape(4, WIDE), in_weight)
    from_right, from_left = shifted(first, "x", -1), shifted(last, "x", 1)
    packed, from_right, from_left = lax.optimization_barrier((packed, from_right, from_left))
    middle_found = lax.all_gather(packed, "x", axis=0)
    row, sent = call(stats_kernel, (sds((SEG, LANES), BF16), sds((depths, 16, C), BF16)), [VMEM] * 5)(
        cells, from_left, from_right, wpad, quarter
    )

    count = lax.axis_size(ROWS)
    crossed = [(i, i + 3) if i % 2 else (i, i - 3) for i in range(count)]
    crossed = [(i, j) for i, j in crossed if 0 <= j < count]
    before, after, across = shifted(row, ROWS, 2), shifted(row, ROWS, -2), lax.ppermute(row, ROWS, crossed)

    half_width = time_weight.shape[0] // 2
    ratios = jnp.exp(-math.log(10000.0) * jnp.arange(half_width, dtype=F32) / half_width)
    angles = timestep[0].astype(F32) * ratios
    features = jnp.concatenate([jnp.cos(angles), jnp.sin(angles)])
    depth_here = time_second.shape[0]
    weight_here = lax.dynamic_slice_in_dim(time_weight, x * depth_here, depth_here, 1)
    hidden = jax.nn.silu(jnp.dot(features, weight_here.astype(F32), precision=HIGH))
    columns = lax.dynamic_slice_in_dim(time_second, (2 * y + core) * HALF, HALF, 1)
    part = jnp.dot(hidden, columns.astype(F32), precision=HIGH)

    got = lax.all_to_all(sent, DEPTH, 0, 0, tiled=True)
    scratch = [
        pltpu.VMEM((2, 48, 4 * HALF), F32),
        pltpu.VMEM((2, 56, 4 * HALF), BF16),
        pltpu.SemaphoreType.DMA((32,)),
    ]
    sent = call(plane_kernel, sds((32, 56, 4 * HALF), BF16), [VMEM] * 2, scratch, 52, ANY)(got, part[None])
    around = jnp.stack([before, row, after, across])
    sent, around, middle_found = lax.optimization_barrier((sent, around, middle_found))
    found = lax.all_to_all(sent, PLANE, 0, 0, tiled=True)
    swap = [(0, 1), (1, 0)]
    joined = call(
        join_kernel, sds((A_LEN, 2 * C), BF16), [VMEM] * 3, [pltpu.VMEM((A_LEN + 2 * GAP, LANES), BF16)], 60
    )(around, lax.ppermute(around, "core", swap), wpad)
    hidden_own, sums = call(
        first_kernel,
        (sds((H_LEN, SWAP), F32), sds((32, 1, 128), F32)),
        [ANY, ANY, VMEM, VMEM],
        [
            pltpu.VMEM((A_LEN, 2 * C), BF16),
            pltpu.VMEM((32, 56, 4 * HALF), BF16),
            pltpu.VMEM((1440, 4 * HALF), F32),
            pltpu.VMEM((3 * 2 * C, MERGED), BF16),
            pltpu.VMEM((A_LEN, 2 * C), BF16),
            pltpu.VMEM((H_LEN + 2 * GAP, MERGED), F32),
            pltpu.SemaphoreType.DMA((3,)),
        ],
        52,
    )(joined, found, time_proj.T, input_gain[None])

    totals, hidden_own = summed(sums, hidden_own)
    hidden_other = lax.ppermute(hidden_own, "core", swap)
    block_own, sums = call(
        second_kernel,
        (sds((B_LEN, SWAP), F32), sds((32, 1, 128), F32)),
        [ANY, ANY, VMEM, VMEM, ANY, ANY],
        [
            pltpu.VMEM((H_LEN, SWAP), F32),
            pltpu.VMEM((H_LEN, SWAP), F32),
            pltpu.VMEM((4, 224, 4 * HALF), BF16),
            pltpu.VMEM((B_LEN, 2 * C), BF16),
            pltpu.VMEM((3 * LANES, MERGED), BF16),
            pltpu.VMEM((2 * C, HALF), BF16),
            pltpu.VMEM((H_LEN, LANES), BF16),
            pltpu.VMEM((B_LEN + 2 * GAP, MERGED), F32),
            pltpu.SemaphoreType.DMA((6,)),
        ],
        52,
    )(hidden_own, hidden_other, totals, middle_gain.reshape(2, HALF), middle_found, joined)

    wout = out_weight.reshape(9, 2, HALF, 4).transpose(1, 2, 0, 3)
    wout = jnp.pad(jnp.pad(wout, ((0, 0), (0, 0), (0, 0), (0, 4))).reshape(2, HALF, 72), ((0, 0), (0, 0), (0, 56)))
    totals, block_own = summed(sums, block_own)
    block_other = lax.ppermute(block_own, "core", swap)
    scratch = [
        pltpu.VMEM((3 * SEG + GAP, SWAP), F32),
        pltpu.VMEM((3 * SEG + GAP, SWAP), F32),
        pltpu.SemaphoreType.DMA((2,)),
    ]
    return call(third_kernel, sds((4, 1, WIDE), F32), [ANY, ANY, VMEM, VMEM, VMEM], scratch, 30)(
        block_own, block_other, totals, output_gain.reshape(2, HALF), wout
    )


def solution(mesh):
    finer = Mesh(
        mesh.devices.reshape(8, 2, 4, 2, mesh.shape["cols"]), ("zp", "zl", "y", "core", "x")
    )
    in_specs = (
        P(None, ROWS, "x"),
        P(None, ROWS, "x"),
        P(),
        P(),
        P(ROWS, None),
        P("x", None),
        P("x", None),
        P(),
        P(),
        P("x", None),
        P(),
        P(),
        P(),
        P(),
    )
    return jax.shard_map(
        shards, mesh=finer, in_specs=in_specs, out_specs=P(None, ROWS, "x"), check_vma=False
    )
```

```python
import math

import jax
import jax.numpy as jnp
from jax import lax
from jax.experimental import pallas as pl
from jax.experimental.pallas import tpu as pltpu
from jax.sharding import Mesh
from jax.sharding import PartitionSpec as P

ROWS = ("zp", "zl", "y", "core")
DEPTH = ("zp", "zl")
PLANE = ("y", "core", "x")
EPS = 1e-05
F32 = jnp.float32
BF16 = jnp.bfloat16
HIGH = lax.Precision.HIGHEST

C = 320
HALF = 160
WIDE = 256
GAP = 16
SEG = WIDE + GAP
IN_ROWS = 8
MID_ROWS = 6
OUT_ROWS = 4
A_LEN = IN_ROWS * SEG + GAP
H_LEN = MID_ROWS * SEG + GAP
B_LEN = OUT_ROWS * SEG + GAP
MERGED = 512
LANES = 384
SWAP = 256
VMEM = pl.BlockSpec(memory_space=pltpu.VMEM)
ANY = pl.BlockSpec(memory_space=pltpu.HBM)


def call(kernel, out_shape, in_specs, scratch=(), limit=16, out_spec=VMEM):
    return pl.pallas_call(
        kernel,
        out_shape=out_shape,
        in_specs=in_specs,
        out_specs=out_spec if isinstance(out_spec, tuple) else jax.tree.map(lambda _: out_spec, out_shape),
        scratch_shapes=list(scratch),
        compiler_params=pltpu.CompilerParams(vmem_limit_bytes=limit * 1024 * 1024),
    )


def sds(shape, dtype):
    return jax.ShapeDtypeStruct(shape, dtype)


def rows_at(start, size):
    return pl.ds(pl.multiple_of(start, 16), size)


def place():
    return 2 * lax.axis_index(("zp", "zl", "y")), lax.axis_index("x") * WIDE, lax.axis_index("core")


def same_group(n, m, size_n, size_m):
    i = lax.broadcasted_iota(jnp.int32, (n, m), 0)
    j = lax.broadcasted_iota(jnp.int32, (n, m), 1)
    return ((i // size_n) == (j // size_m)).astype(F32)


def exact_dot(a, b):
    return jnp.dot(a, b, preferred_element_type=F32, precision=HIGH)


def tap_dot(a, b):
    return jnp.dot(a, b, preferred_element_type=F32)


def silu_half(h):
    return h + h * jnp.tanh(h)


def pack_kernel(deep_ref, prev_ref, here_ref, next_ref, weight_ref, out_ref, first_ref, last_ref, wpad_ref, tall, wide):
    tall[0:C, :] = deep_ref[...].astype(F32)
    tall[C:LANES, :] = jnp.zeros((LANES - C, WIDE), F32)
    for i, ref in enumerate((prev_ref, here_ref, next_ref)):
        tall[C + 4 * i : C + 4 * i + 4, :] = ref[...].astype(F32)
    out = tall[...].T.astype(BF16)
    out_ref[...] = out
    first_ref[...] = out[0:GAP]
    last_ref[...] = out[WIDE - GAP : WIDE]
    wide[...] = jnp.zeros((LANES, LANES), F32)
    weight = weight_ref[...].astype(F32)
    for tap in range(9):
        a, b = divmod(tap, 3)
        at = 128 * b + 64 + 4 * a
        wide[at : at + 4, 64:LANES] = weight[4 * tap : 4 * tap + 4]
    wpad_ref[...] = wide[...].astype(BF16)


def skip_of(tail, wpad_ref, lo, hi):
    n = tail.shape[0]
    left = pltpu.roll(tail, 1, 0)[lo:hi].astype(BF16)
    right = pltpu.roll(tail, n - 1, 0)[lo:hi].astype(BF16)
    mid = tail[lo:hi].astype(BF16)
    stacked = jnp.concatenate([left, mid, right], axis=1)
    return tap_dot(stacked, wpad_ref[...]).astype(BF16).astype(F32)


def join(cells, skip):
    lane = lax.broadcasted_iota(jnp.int32, (cells.shape[0], 128), 1)
    mixed = jnp.where(lane < 64, cells[:, 256:384], skip[:, 0:128])
    return jnp.concatenate([cells[:, 0:256], mixed, skip[:, 128:384]], axis=1)


def three_terms(values):
    high = values.astype(BF16).astype(F32)
    middle = (values - high).astype(BF16).astype(F32)
    return high, middle, values - high - middle


def stats_kernel(cells_ref, left_ref, right_ref, wpad_ref, quarter_ref, row_ref, sent_ref):
    sub = lax.broadcasted_iota(jnp.int32, (GAP, LANES), 0)
    gap = jnp.where(sub < 8, right_ref[...].astype(F32), left_ref[...].astype(F32))
    cells = jnp.concatenate([cells_ref[...].astype(F32), gap], axis=0)
    row_ref[...] = cells.astype(BF16)
    skip = skip_of(cells[:, 256:384], wpad_ref, 0, WIDE)
    joined = join(cells[0:WIDE], skip)
    sums = jnp.sum(joined, axis=0, keepdims=True)
    squares = jnp.sum(joined * joined, axis=0, keepdims=True)
    both = jnp.concatenate([sums, squares, jnp.zeros((6, 2 * C), F32)], axis=0)
    grouped = exact_dot(both, same_group(2 * C, 32, 20, 1))
    terms = three_terms(jnp.concatenate([grouped[0:1], grouped[1:2]], axis=1))
    line = jnp.concatenate([*terms, jnp.zeros((1, C - 192), F32)], axis=1)
    message = jnp.concatenate([quarter_ref[...].astype(F32), line, jnp.zeros((3, C), F32)], axis=0).astype(BF16)
    for z in range(sent_ref.shape[0]):
        sent_ref[z] = message


def plane_kernel(got_ref, part_ref, sent_hbm, rows, blocks, sems):
    total = jnp.zeros((1, 64), F32)
    for z in range(16):
        got = got_ref[z].astype(F32)
        q, d = divmod(z, 4)
        for half in (0, 1):
            rows[half, 12 * d : 12 * d + 12, 160 * q : 160 * (q + 1)] = got[0:12, 160 * half : 160 * (half + 1)]
        total = total + got[12:13, 0:64] + got[12:13, 64:128] + got[12:13, 128:192]
    first = jnp.concatenate([*three_terms(total), jnp.zeros((1, 4 * HALF - 192), F32)], axis=1)
    second = jnp.concatenate([*three_terms(part_ref[...]), jnp.zeros((1, HALF), F32)], axis=1)
    tail = jnp.concatenate([first, second, jnp.zeros((6, 4 * HALF), F32)], axis=0).astype(BF16)
    copies = []
    for half in (0, 1):
        blocks[half, 0:48, :] = rows[half].astype(BF16)
        blocks[half, 48:56, :] = tail
        for i in range(16):
            goal = 8 * (i // 4) + 4 * half + i % 4
            copies.append(pltpu.make_async_copy(blocks.at[half], sent_hbm.at[goal], sems.at[goal]))
            copies[-1].start()
    for copy in copies:
        copy.wait()


def keep_mask(r, first_row, first_col):
    i = lax.broadcasted_iota(jnp.int32, (SEG, 1), 0)
    here = first_row + r
    row = jnp.where(i < 8, here - 1, here)
    col = first_col + jnp.where(i < 8, i + WIDE, i - GAP)
    good = (row >= 0) & (row < 128) & (col >= 0) & (col < 1024)
    return good.astype(F32)


def shift_add(merged_ref, start, size):
    back = merged_ref[pl.ds(start - 1, size), :]
    mid = merged_ref[pl.ds(start, size), :]
    ahead = merged_ref[pl.ds(start + 1, size), :]
    low = back[:, 0:128] + mid[:, 128:256] + ahead[:, 256:384]
    high = (
        back[:, 384:512]
        + pltpu.roll(mid[:, 384:512], 96, 1)
        + pltpu.roll(ahead[:, 384:512], 64, 1)
    )
    return jnp.concatenate([low, high[:, 0:32]], axis=1)


def join_kernel(own_ref, other_ref, wpad_ref, joined_ref, raw):
    order = ((0, 3), (0, 0), (1, 0), (0, 1), (1, 1), (0, 2), (1, 2), (1, 3))
    sub = lax.broadcasted_iota(jnp.int32, (GAP, LANES), 0)
    zeros = jnp.zeros((GAP, LANES), BF16)
    raw[0:GAP, :] = zeros
    raw[GAP + A_LEN : GAP + A_LEN + GAP, :] = zeros

    def lay_out(sources):
        for r in range(IN_ROWS + 1):
            before, after = None, None
            if r:
                which, at = order[r - 1]
                before = sources[which][at, WIDE:SEG, :].astype(F32)
            if r < IN_ROWS:
                which, at = order[r]
                after = sources[which][at, WIDE:SEG, :].astype(F32)
                raw[2 * GAP + r * SEG : GAP + (r + 1) * SEG, :] = sources[which][at, 0:WIDE, :]
            before = after if before is None else before
            after = before if after is None else after
            raw[GAP + r * SEG : 2 * GAP + r * SEG, :] = jnp.where(sub < 8, before, after).astype(BF16)

    core = lax.axis_index("core")

    @pl.when(core == 0)
    def _():
        lay_out((own_ref, other_ref))

    @pl.when(core == 1)
    def _():
        lay_out((other_ref, own_ref))

    def one(r, size):
        base = r * SEG
        tail = raw[rows_at(base, size + 2 * GAP), 256:384].astype(F32)
        skip = skip_of(tail, wpad_ref, GAP, GAP + size)
        joined = join(raw[rows_at(base + GAP, size), :].astype(F32), skip)
        joined_ref[rows_at(base, size), :] = joined.astype(BF16)

    def build(r, carry):
        one(r, SEG)
        return carry

    lax.fori_loop(0, IN_ROWS, build, 0)
    one(IN_ROWS, GAP)


def first_affine(sums, gain_ref):
    totals = sums / (20.0 * 131072.0)
    mean = totals[:, 0:32]
    var = totals[:, 32:64] - mean * mean
    pair = jnp.concatenate([lax.rsqrt(var + EPS), mean, jnp.zeros((6, 32), F32)], axis=0)
    spread = exact_dot(pair, same_group(32, 2 * C, 1, 20))
    scale = spread[0:1] * gain_ref[...] * 0.5
    return scale, -spread[1:2] * scale


def first_build(joined_ref, act, at, size, mask, scale, offset):
    where = slice(at, at + size)
    for lane in range(0, 2 * C, 128):
        part = slice(lane, lane + 128)
        values = joined_ref[where, part].astype(F32) * scale[:, part] + offset[:, part]
        act[where, part] = (silu_half(values) * mask[0:size]).astype(BF16)


def merged_conv(act, wm_ref, merged, start, size):
    taps = [act[start + a * SEG : start + a * SEG + size, :] for a in range(3)]
    merged[start + GAP : start + GAP + size, :] = tap_dot(jnp.concatenate(taps, axis=1), wm_ref[...])


def clear_ends(merged):
    size = merged.shape[0]
    merged[0:GAP, :] = jnp.zeros((GAP, MERGED), F32)
    merged[size - GAP : size, :] = jnp.zeros((GAP, MERGED), F32)


def first_own_kernel(
    joined_hbm, found_hbm, proj_ref, gain_ref,
    wm_hbm, known_ref, sum_ref,
    joined_ref, found_ref, rows, wm_ref, act, merged, sems,
):
    copies = [
        pltpu.make_async_copy(found_hbm, found_ref, sems.at[0]),
        pltpu.make_async_copy(joined_hbm.at[2 * SEG : 2 * SEG + B_LEN], joined_ref, sems.at[1]),
        pltpu.make_async_copy(wm_ref, wm_hbm, sems.at[2]),
    ]
    copies[0].start()
    copies[1].start()
    copies[0].wait()
    chip_row, first_col, _ = place()
    totals, shift = front_weight(found_ref, proj_ref, wm_ref, rows)
    copies[2].start()
    known_ref[...] = jnp.concatenate([totals, jnp.zeros((1, 64), F32), shift, jnp.zeros((1, 96), F32)], axis=1)
    scale, offset = first_affine(totals, gain_ref)
    clear_ends(merged)
    copies[1].wait()
    for r in range(5):
        mask = keep_mask(r + 2, chip_row - 3, first_col)
        first_build(joined_ref, act, r * SEG, SEG if r < 4 else GAP, mask, scale, offset)
    merged_conv(act, wm_ref, merged, 0, 2 * SEG + GAP)
    sums = jnp.zeros((1, HALF), F32)
    squares = jnp.zeros((1, HALF), F32)
    for r in range(2):
        values = shift_add(merged, 2 * GAP + r * SEG, WIDE) + shift
        sums = sums + jnp.sum(values, axis=0, keepdims=True)
        squares = squares + jnp.sum(values * values, axis=0, keepdims=True)
    send_sums(sums, squares, sum_ref)
    copies[2].wait()


def first_kernel(
    joined_hbm, wm_hbm, known_ref, gain_ref,
    hidden_ref,
    joined_ref, wm_ref, act, merged, sems,
):
    copies = []
    for i, part in enumerate((slice(0, 4 * SEG), slice(4 * SEG, A_LEN))):
        copies.append(pltpu.make_async_copy(joined_hbm.at[part], joined_ref.at[part], sems.at[i]))
    copies.append(pltpu.make_async_copy(wm_hbm, wm_ref, sems.at[2]))
    for copy in copies:
        copy.start()
    chip_row, first_col, _ = place()
    scale, offset = first_affine(known_ref[:, 0:64], gain_ref)
    shift = known_ref[:, 128 : 128 + HALF]

    def build(r):
        mask = keep_mask(r, chip_row - 3, first_col)
        first_build(joined_ref, act, r * SEG, SEG if r < IN_ROWS else GAP, mask, scale, offset)

    clear_ends(merged)
    copies[0].wait()
    for r in range(4):
        build(r)
    copies[2].wait()
    merged_conv(act, wm_ref, merged, 0, 2 * SEG)
    copies[1].wait()
    build(4)
    build(5)
    merged_conv(act, wm_ref, merged, 2 * SEG, 2 * SEG)
    for r in range(6, 9):
        build(r)
    merged_conv(act, wm_ref, merged, 4 * SEG, 2 * SEG + GAP)
    for r in range(MID_ROWS + 1):
        size = SEG if r < MID_ROWS else GAP
        hidden_ref[r * SEG : r * SEG + size, 0:HALF] = shift_add(merged, GAP + r * SEG, size) + shift
    hidden_ref[:, HALF:SWAP] = jnp.zeros((H_LEN, SWAP - HALF), F32)


def send_sums(sums, squares, sent_ref):
    both = jnp.concatenate([sums, squares, jnp.zeros((6, HALF), F32)], axis=0)
    grouped = exact_dot(both, same_group(HALF, 16, 10, 1))
    line = jnp.concatenate([grouped[0:1], grouped[1:2], jnp.zeros((1, 96), F32)], axis=1)
    for i in range(32):
        sent_ref[i] = line


def plane_sums_kernel(got_ref, sent_ref):
    cores = [jnp.zeros((1, 32), F32), jnp.zeros((1, 32), F32)]
    for i in range(32):
        half = (i // 4) % 2
        cores[half] = cores[half] + got_ref[i][:, 0:32]
    line = jnp.concatenate([*cores, jnp.zeros((1, 64), F32)], axis=1)
    for i in range(sent_ref.shape[0]):
        sent_ref[i] = line


def affine(stat_ref, gain_ref):
    both = stat_ref[0]
    for i in range(1, stat_ref.shape[0]):
        both = both + stat_ref[i]
    found = []
    for which in (0, 1):
        at = 32 * which
        padded = jnp.concatenate([both[:, at : at + 16], both[:, at + 16 : at + 32], jnp.zeros((6, 16), F32)], axis=0)
        totals = exact_dot(padded, same_group(16, HALF, 1, 10)) / (10.0 * 131072.0)
        mean = totals[0:1]
        scale = lax.rsqrt(totals[1:2] - mean * mean + EPS) * gain_ref[which : which + 1] * 0.5
        found.append((scale, -mean * scale))
    return found


def second_build(own_ref, other_ref, act, at, size, mask, affines):
    where = slice(at, at + size)
    first = lax.axis_index("core") == 0
    own, other = own_ref[where, 0:HALF], other_ref[where, 0:HALF]
    parts = []
    for which, (scale, offset) in enumerate(affines):
        values = jnp.where(first, own, other) if which == 0 else jnp.where(first, other, own)
        parts.append(silu_half(values * scale + offset) * mask[0:size])
    parts.append(jnp.zeros((size, LANES - C), F32))
    act[where, :] = jnp.concatenate(parts, axis=1).astype(BF16)


def second_own_kernel(
    own_hbm, other_hbm, stat_ref, gain_ref, found_hbm, joined_hbm,
    wm_hbm, skip_hbm, sum_ref,
    own_ref, other_ref, found_ref, joined_ref, wm_ref, skip_ref, act, merged, sems,
):
    part = slice(SEG, SEG + B_LEN)
    copies = [
        pltpu.make_async_copy(found_hbm, found_ref, sems.at[0]),
        pltpu.make_async_copy(own_hbm.at[part], own_ref, sems.at[1]),
        pltpu.make_async_copy(other_hbm.at[part], other_ref, sems.at[2]),
        pltpu.make_async_copy(joined_hbm.at[3 * SEG : 5 * SEG], joined_ref, sems.at[3]),
    ]
    for copy in copies:
        copy.start()
    back = [
        pltpu.make_async_copy(wm_ref, wm_hbm, sems.at[4]),
        pltpu.make_async_copy(skip_ref, skip_hbm, sems.at[5]),
    ]
    chip_row, first_col, _ = place()
    affines = affine(stat_ref, gain_ref)
    clear_ends(merged)
    copies[0].wait()
    middle_weight(found_ref, wm_ref, skip_ref)
    for copy in back:
        copy.start()
    copies[1].wait()
    copies[2].wait()
    for r in range(5):
        mask = keep_mask(r + 1, chip_row - 2, first_col)
        second_build(own_ref, other_ref, act, r * SEG, SEG if r < 4 else GAP, mask, affines)
    merged_conv(act, wm_ref, merged, 0, 2 * SEG + GAP)
    copies[3].wait()
    sums = jnp.zeros((1, HALF), F32)
    squares = jnp.zeros((1, HALF), F32)
    for r in range(2):
        at = r * SEG + GAP
        values = shift_add(merged, GAP + at, WIDE) + tap_dot(joined_ref[at : at + WIDE, :], skip_ref[...])
        sums = sums + jnp.sum(values, axis=0, keepdims=True)
        squares = squares + jnp.sum(values * values, axis=0, keepdims=True)
    send_sums(sums, squares, sum_ref)
    for copy in back:
        copy.wait()


def second_kernel(
    own_hbm, other_hbm, stat_ref, gain_ref, wm_hbm, skip_ref, joined_hbm,
    block_ref,
    own_ref, other_ref, joined_ref, wm_ref, act, merged, sems,
):
    copies = [
        pltpu.make_async_copy(own_hbm, own_ref, sems.at[0]),
        pltpu.make_async_copy(other_hbm, other_ref, sems.at[1]),
        pltpu.make_async_copy(wm_hbm, wm_ref, sems.at[2]),
        pltpu.make_async_copy(joined_hbm.at[2 * SEG : 2 * SEG + B_LEN], joined_ref, sems.at[3]),
    ]
    for copy in copies:
        copy.start()
    chip_row, first_col, _ = place()
    affines = affine(stat_ref, gain_ref)
    clear_ends(merged)
    copies[0].wait()
    copies[1].wait()

    def build(r):
        mask = keep_mask(r, chip_row - 2, first_col)
        second_build(own_ref, other_ref, act, r * SEG, SEG if r < MID_ROWS else GAP, mask, affines)

    for r in range(4):
        build(r)
    copies[2].wait()
    merged_conv(act, wm_ref, merged, 0, 2 * SEG)
    for r in range(4, 7):
        build(r)
    merged_conv(act, wm_ref, merged, 2 * SEG, 2 * SEG + GAP)
    copies[3].wait()
    for r in range(OUT_ROWS + 1):
        size = SEG if r < OUT_ROWS else GAP
        where = slice(r * SEG, r * SEG + size)
        block_ref[where, 0:HALF] = shift_add(merged, GAP + r * SEG, size) + tap_dot(
            joined_ref[where, :], skip_ref[...]
        )
    block_ref[:, HALF:SWAP] = jnp.zeros((B_LEN, SWAP - HALF), F32)


def third_kernel(own_hbm, other_hbm, stat_ref, gain_ref, wout_ref, noise_ref, own_ref, other_ref, sems):
    chip_row, first_col, core = place()
    needed = pl.ds(pl.multiple_of(core * SEG, 16), 3 * SEG + GAP)
    copies = [
        pltpu.make_async_copy(own_hbm.at[needed], own_ref, sems.at[0]),
        pltpu.make_async_copy(other_hbm.at[needed], other_ref, sems.at[1]),
    ]
    for copy in copies:
        copy.start()
    first_row = chip_row - 1 + core
    affines = affine(stat_ref, gain_ref)
    first = core == 0
    for copy in copies:
        copy.wait()
    parts = []
    for r in range(4):
        size = SEG if r < 3 else GAP
        mask = keep_mask(r, first_row, first_col)[0:size]
        where = slice(r * SEG, r * SEG + size)
        total = None
        own, other = own_ref[where, 0:HALF], other_ref[where, 0:HALF]
        for which, (scale, offset) in enumerate(affines):
            values = jnp.where(first, own, other) if which == 0 else jnp.where(first, other, own)
            act = (silu_half(values * scale + offset) * mask).astype(BF16)
            part = tap_dot(act, wout_ref[which])
            total = part if total is None else total + part
        parts.append(total)
    parts.append(jnp.zeros((896 - 3 * SEG - GAP, 128), F32))
    turned = jnp.concatenate(parts, axis=0).T
    noise = None
    for a in range(3):
        for b in range(3):
            tap = 3 * a + b
            at = a * SEG + GAP + b - 1
            piece = turned[8 * tap : 8 * tap + 8, at : at + WIDE]
            noise = piece if noise is None else noise + piece
    for o in range(4):
        noise_ref[o] = noise[o : o + 1]


def place_merged(out_ref, at, size, b, piece):
    out_ref[at : at + size, 128 * b : 128 * (b + 1)] = piece[:, 0:128]
    out_ref[at : at + size, 384 + 32 * b : 384 + 32 * (b + 1)] = piece[:, 128:160]


def front_weight(found_ref, proj_ref, out_ref, rows):
    out_ref[:, 480:512] = jnp.zeros((3 * 2 * C, 32), BF16)
    sums = jnp.zeros((1, 64), F32)
    embedded = []
    for shard in range(8):
        part = jnp.zeros((1, HALF), F32)
        for x in range(4):
            j = 4 * shard + x
            found = found_ref[j].astype(F32)
            size = 12 if x < 3 else 9
            for d in range(4):
                at = 360 * d + 45 * shard + 12 * x
                rows[at : at + size, :] = found[12 * d : 12 * d + size]
            for term in range(3):
                sums = sums + found[48:49, 64 * term : 64 * (term + 1)]
                part = part + found[49:50, HALF * term : HALF * (term + 1)]
        embedded.append(part)
    values = jnp.concatenate(embedded, axis=1)
    values = values / (1.0 + jnp.exp(-values))
    proj = proj_ref[rows_at(lax.axis_index("core") * HALF, HALF), :].astype(F32)
    shift = jnp.sum(proj * values, axis=1, keepdims=True)
    shift = jnp.concatenate([jnp.broadcast_to(shift, (HALF, 128)), jnp.zeros((WIDE - HALF, 128), F32)], axis=0)
    shift = shift.T[0:1, 0:HALF]
    for q in range(4):
        row = 1440 * q
        while row < 1440 * (q + 1):
            tap, channel = divmod(row, 2 * C)
            size = min(1440 * (q + 1) - row, 2 * C - channel)
            a, b = divmod(tap, 3)
            k = row - 1440 * q
            piece = rows[k : k + size, 160 * q : 160 * (q + 1)].astype(BF16)
            place_merged(out_ref, a * 2 * C + channel, size, b, piece)
            row += size
    return sums, shift


def share_kernel(middle_ref, skip_ref, out_ref):
    core = lax.axis_index("core")
    middle = middle_ref[rows_at(core * HALF, HALF), :].astype(F32).T
    wide = skip_ref[...].astype(F32)
    skip = jnp.where(core == 0, wide[:, 0:HALF], wide[:, HALF:C])
    whole = jnp.concatenate([middle, skip, jnp.zeros((16, HALF), F32)], axis=0)
    parts = [whole[224 * q : 224 * (q + 1)] for q in range(4)]
    out_ref[...] = jnp.concatenate(parts, axis=1).astype(BF16)


def middle_weight(found_ref, out_ref, skip_ref):
    out_ref[:, 480:512] = jnp.zeros((3 * LANES, 32), BF16)

    def pieces(x, row, size):
        while size:
            q, i = divmod(row, 224)
            some = min(size, 224 - i)
            yield some, found_ref[x, i : i + some, 160 * q : 160 * (q + 1)]
            row, size = row + some, size - some

    for a in range(3):
        out_ref[a * LANES + C : (a + 1) * LANES, :] = jnp.zeros((LANES - C, MERGED), BF16)
    for tap in range(9):
        a, b = divmod(tap, 3)
        at = a * LANES
        for part in range(4):
            x, i = divmod(tap * C + part * 80, 720)
            for size, piece in pieces(x, i, 80):
                place_merged(out_ref, at, size, b, piece)
                at += size
    at = 0
    for x in range(4):
        for size, piece in pieces(x, 720, HALF):
            skip_ref[at : at + size, :] = piece
            at += size


def shifted(x, axis, step):
    count = lax.axis_size(axis)
    return lax.ppermute(x, axis, [(i, i + step) for i in range(count) if 0 <= i + step < count])


def summed(sums, kept):
    near = lax.all_to_all(sums, PLANE, 0, 0, tiled=True)
    near, kept = lax.optimization_barrier((near, kept))
    near = call(plane_sums_kernel, sds((lax.axis_size(DEPTH), 1, 128), F32), [VMEM])(near)
    return lax.all_to_all(near, DEPTH, 0, 0, tiled=True), kept


def shards(
    latent, deep, timestep, in_weight, front_weight, middle_weight, skip_weight, out_weight,
    time_weight, time_second, time_proj, input_gain, middle_gain, output_gain,
):
    core, x, y = lax.axis_index("core"), lax.axis_index("x"), lax.axis_index("y")
    depths = lax.axis_size(DEPTH)

    above, below = shifted(latent, ROWS, 1), shifted(latent, ROWS, -1)
    quarter = lax.dynamic_slice_in_dim(jnp.pad(front_weight, ((0, 3), (0, 0))), 12 * x, 12, 0)
    cells, first, last, wpad = call(
        pack_kernel,
        (sds((WIDE, LANES), BF16), sds((GAP, LANES), BF16), sds((GAP, LANES), BF16), sds((LANES, LANES), BF16)),
        [VMEM] * 5,
        [pltpu.VMEM((LANES, WIDE), F32), pltpu.VMEM((LANES, LANES), F32)],
    )(deep.reshape(C, WIDE), above.reshape(4, WIDE), latent.reshape(4, WIDE), below.reshape(4, WIDE), in_weight)
    from_right, from_left = shifted(first, "x", -1), shifted(last, "x", 1)
    row, sent = call(stats_kernel, (sds((SEG, LANES), BF16), sds((depths, 16, C), BF16)), [VMEM] * 5)(
        cells, from_left, from_right, wpad, quarter
    )

    row, skip_here = lax.optimization_barrier((row, skip_weight))
    packed = call(share_kernel, sds((224, 4 * HALF), BF16), [VMEM] * 2)(middle_weight.T, skip_here)

    count = lax.axis_size(ROWS)
    crossed = [(i, i + 3) if i % 2 else (i, i - 3) for i in range(count)]
    crossed = [(i, j) for i, j in crossed if 0 <= j < count]
    before, after, across = shifted(row, ROWS, 2), shifted(row, ROWS, -2), lax.ppermute(row, ROWS, crossed)

    half_width = time_weight.shape[0] // 2
    ratios = jnp.exp(-math.log(10000.0) * jnp.arange(half_width, dtype=F32) / half_width)
    angles = timestep[0].astype(F32) * ratios
    features = jnp.concatenate([jnp.cos(angles), jnp.sin(angles)])
    depth_here = time_second.shape[0]
    weight_here = lax.dynamic_slice_in_dim(time_weight, x * depth_here, depth_here, 1)
    hidden = jax.nn.silu(jnp.dot(features, weight_here.astype(F32), precision=HIGH))
    columns = lax.dynamic_slice_in_dim(time_second, (2 * y + core) * HALF, HALF, 1)
    part = jnp.dot(hidden, columns.astype(F32), precision=HIGH)

    got = lax.all_to_all(sent, DEPTH, 0, 0, tiled=True)
    scratch = [
        pltpu.VMEM((2, 48, 4 * HALF), F32),
        pltpu.VMEM((2, 56, 4 * HALF), BF16),
        pltpu.SemaphoreType.DMA((32,)),
    ]
    sent = call(plane_kernel, sds((32, 56, 4 * HALF), BF16), [VMEM] * 2, scratch, 52, ANY)(got, part[None])
    around = jnp.stack([before, row, after, across])
    sent, around = lax.optimization_barrier((sent, around))
    found = lax.all_to_all(sent, PLANE, 0, 0, tiled=True)
    swap = [(0, 1), (1, 0)]
    joined = call(
        join_kernel, sds((A_LEN, 2 * C), BF16), [VMEM] * 3, [pltpu.VMEM((A_LEN + 2 * GAP, LANES), BF16)], 60
    )(around, lax.ppermute(around, "core", swap), wpad)
    own_scratch = [
        pltpu.VMEM((B_LEN, 2 * C), BF16),
        pltpu.VMEM((32, 56, 4 * HALF), BF16),
        pltpu.VMEM((1440, 4 * HALF), F32),
        pltpu.VMEM((3 * 2 * C, MERGED), BF16),
        pltpu.VMEM((B_LEN, 2 * C), BF16),
        pltpu.VMEM((2 * SEG + 3 * GAP, MERGED), F32),
        pltpu.SemaphoreType.DMA((3,)),
    ]
    front, known, sums = call(
        first_own_kernel,
        (sds((3 * 2 * C, MERGED), BF16), sds((1, 384), F32), sds((32, 1, 128), F32)),
        [ANY, ANY, VMEM, VMEM],
        own_scratch,
        52,
        (ANY, VMEM, VMEM),
    )(joined, found, time_proj.T, input_gain[None])
    packed, sums = lax.optimization_barrier((packed, sums))
    middle_found = lax.all_gather(packed, "x", axis=0)
    hidden_own = call(
        first_kernel,
        sds((H_LEN, SWAP), F32),
        [ANY, ANY, VMEM, VMEM],
        [
            pltpu.VMEM((A_LEN, 2 * C), BF16),
            pltpu.VMEM((3 * 2 * C, MERGED), BF16),
            pltpu.VMEM((A_LEN, 2 * C), BF16),
            pltpu.VMEM((H_LEN + 2 * GAP, MERGED), F32),
            pltpu.SemaphoreType.DMA((3,)),
        ],
        52,
    )(joined, front, known, input_gain[None])
    totals, hidden_own = summed(sums, hidden_own)
    hidden_other = lax.ppermute(hidden_own, "core", swap)

    gain_two = middle_gain.reshape(2, HALF)
    middle, shortcut, sums = call(
        second_own_kernel,
        (sds((3 * LANES, MERGED), BF16), sds((2 * C, HALF), BF16), sds((32, 1, 128), F32)),
        [ANY, ANY, VMEM, VMEM, ANY, ANY],
        [
            pltpu.VMEM((B_LEN, SWAP), F32),
            pltpu.VMEM((B_LEN, SWAP), F32),
            pltpu.VMEM((4, 224, 4 * HALF), BF16),
            pltpu.VMEM((2 * SEG, 2 * C), BF16),
            pltpu.VMEM((3 * LANES, MERGED), BF16),
            pltpu.VMEM((2 * C, HALF), BF16),
            pltpu.VMEM((B_LEN, LANES), BF16),
            pltpu.VMEM((2 * SEG + 3 * GAP, MERGED), F32),
            pltpu.SemaphoreType.DMA((6,)),
        ],
        52,
        (ANY, ANY, VMEM),
    )(hidden_own, hidden_other, totals, gain_two, middle_found, joined)
    block_own = call(
        second_kernel,
        sds((B_LEN, SWAP), F32),
        [ANY, ANY, VMEM, VMEM, ANY, VMEM, ANY],
        [
            pltpu.VMEM((H_LEN, SWAP), F32),
            pltpu.VMEM((H_LEN, SWAP), F32),
            pltpu.VMEM((B_LEN, 2 * C), BF16),
            pltpu.VMEM((3 * LANES, MERGED), BF16),
            pltpu.VMEM((H_LEN, LANES), BF16),
            pltpu.VMEM((B_LEN + 2 * GAP, MERGED), F32),
            pltpu.SemaphoreType.DMA((4,)),
        ],
        52,
    )(hidden_own, hidden_other, totals, gain_two, middle, shortcut, joined)
    totals, block_own = summed(sums, block_own)
    block_other = lax.ppermute(block_own, "core", swap)

    wout = out_weight.reshape(9, 2, HALF, 4).transpose(1, 2, 0, 3)
    wout = jnp.pad(jnp.pad(wout, ((0, 0), (0, 0), (0, 0), (0, 4))).reshape(2, HALF, 72), ((0, 0), (0, 0), (0, 56)))
    scratch = [
        pltpu.VMEM((3 * SEG + GAP, SWAP), F32),
        pltpu.VMEM((3 * SEG + GAP, SWAP), F32),
        pltpu.SemaphoreType.DMA((2,)),
    ]
    return call(third_kernel, sds((4, 1, WIDE), F32), [ANY, ANY, VMEM, VMEM, VMEM], scratch, 30)(
        block_own, block_other, totals, output_gain.reshape(2, HALF), wout
    )


def solution(mesh):
    finer = Mesh(
        mesh.devices.reshape(8, 2, 4, 2, mesh.shape["cols"]), ("zp", "zl", "y", "core", "x")
    )
    in_specs = (
        P(None, ROWS, "x"),
        P(None, ROWS, "x"),
        P(),
        P(),
        P(ROWS, None),
        P("x", None),
        P("x", None),
        P(),
        P(),
        P("x", None),
        P(),
        P(),
        P(),
        P(),
    )
    return jax.shard_map(
        shards, mesh=finer, in_specs=in_specs, out_specs=P(None, ROWS, "x"), check_vma=False
    )
```

```python
import math

import jax
import jax.numpy as jnp
from jax import lax
from jax.experimental import pallas as pl
from jax.experimental.pallas import tpu as pltpu
from jax.sharding import Mesh
from jax.sharding import PartitionSpec as P

ROWS = ("zp", "zl", "y", "core")
DEPTH = ("zp", "zl")
PLANE = ("y", "core", "x")
EPS = 1e-05
F32 = jnp.float32
BF16 = jnp.bfloat16
HIGH = lax.Precision.HIGHEST

C = 320
HALF = 160
WIDE = 256
GAP = 16
SEG = WIDE + GAP
IN_ROWS = 8
MID_ROWS = 6
OUT_ROWS = 4
A_LEN = IN_ROWS * SEG + GAP
H_LEN = MID_ROWS * SEG + GAP
B_LEN = OUT_ROWS * SEG + GAP
MERGED = 512
LANES = 384
SWAP = 256
VMEM = pl.BlockSpec(memory_space=pltpu.VMEM)
ANY = pl.BlockSpec(memory_space=pltpu.HBM)


def call(kernel, out_shape, in_specs, scratch=(), limit=16, out_spec=VMEM):
    return pl.pallas_call(
        kernel,
        out_shape=out_shape,
        in_specs=in_specs,
        out_specs=out_spec if isinstance(out_spec, tuple) else jax.tree.map(lambda _: out_spec, out_shape),
        scratch_shapes=list(scratch),
        compiler_params=pltpu.CompilerParams(vmem_limit_bytes=limit * 1024 * 1024),
    )


def sds(shape, dtype):
    return jax.ShapeDtypeStruct(shape, dtype)


def rows_at(start, size):
    return pl.ds(pl.multiple_of(start, 16), size)


def place():
    return 2 * lax.axis_index(("zp", "zl", "y")), lax.axis_index("x") * WIDE, lax.axis_index("core")


def same_group(n, m, size_n, size_m):
    i = lax.broadcasted_iota(jnp.int32, (n, m), 0)
    j = lax.broadcasted_iota(jnp.int32, (n, m), 1)
    return ((i // size_n) == (j // size_m)).astype(F32)


def exact_dot(a, b):
    return jnp.dot(a, b, preferred_element_type=F32, precision=HIGH)


def tap_dot(a, b):
    return jnp.dot(a, b, preferred_element_type=F32)


def silu_half(h):
    return h + h * jnp.tanh(h)


def pack_kernel(deep_ref, prev_ref, here_ref, next_ref, weight_ref, out_ref, first_ref, last_ref, wpad_ref, tall, wide):
    tall[0:C, :] = deep_ref[...].astype(F32)
    tall[C:LANES, :] = jnp.zeros((LANES - C, WIDE), F32)
    for i, ref in enumerate((prev_ref, here_ref, next_ref)):
        tall[C + 4 * i : C + 4 * i + 4, :] = ref[...].astype(F32)
    out = tall[...].T.astype(BF16)
    out_ref[...] = out
    first_ref[...] = out[0:GAP]
    last_ref[...] = out[WIDE - GAP : WIDE]
    wide[...] = jnp.zeros((LANES, LANES), F32)
    weight = weight_ref[...].astype(F32)
    for tap in range(9):
        a, b = divmod(tap, 3)
        at = 128 * b + 64 + 4 * a
        wide[at : at + 4, 64:LANES] = weight[4 * tap : 4 * tap + 4]
    wpad_ref[...] = wide[...].astype(BF16)


def skip_of(tail, wpad_ref, lo, hi):
    n = tail.shape[0]
    left = pltpu.roll(tail, 1, 0)[lo:hi].astype(BF16)
    right = pltpu.roll(tail, n - 1, 0)[lo:hi].astype(BF16)
    mid = tail[lo:hi].astype(BF16)
    stacked = jnp.concatenate([left, mid, right], axis=1)
    return tap_dot(stacked, wpad_ref[...]).astype(BF16).astype(F32)


def join(cells, skip):
    lane = lax.broadcasted_iota(jnp.int32, (cells.shape[0], 128), 1)
    mixed = jnp.where(lane < 64, cells[:, 256:384], skip[:, 0:128])
    return jnp.concatenate([cells[:, 0:256], mixed, skip[:, 128:384]], axis=1)


def three_terms(values):
    high = values.astype(BF16).astype(F32)
    middle = (values - high).astype(BF16).astype(F32)
    return high, middle, values - high - middle


def stats_kernel(cells_ref, left_ref, right_ref, wpad_ref, quarter_ref, row_ref, sent_ref):
    sub = lax.broadcasted_iota(jnp.int32, (GAP, LANES), 0)
    gap = jnp.where(sub < 8, right_ref[...].astype(F32), left_ref[...].astype(F32))
    cells = jnp.concatenate([cells_ref[...].astype(F32), gap], axis=0)
    row_ref[...] = cells.astype(BF16)
    skip = skip_of(cells[:, 256:384], wpad_ref, 0, WIDE)
    joined = join(cells[0:WIDE], skip)
    sums = jnp.sum(joined, axis=0, keepdims=True)
    squares = jnp.sum(joined * joined, axis=0, keepdims=True)
    both = jnp.concatenate([sums, squares, jnp.zeros((6, 2 * C), F32)], axis=0)
    grouped = exact_dot(both, same_group(2 * C, 32, 20, 1))
    terms = three_terms(jnp.concatenate([grouped[0:1], grouped[1:2]], axis=1))
    line = jnp.concatenate([*terms, jnp.zeros((1, 2 * C - 192), F32)], axis=1)
    quarter = quarter_ref[...].astype(F32)
    paired = jnp.concatenate([quarter[0:6], quarter[6:12]], axis=1)
    message = jnp.concatenate([paired, line, jnp.zeros((1, 2 * C), F32)], axis=0).astype(BF16)
    for z in range(sent_ref.shape[0]):
        sent_ref[z] = message


def plane_kernel(got_ref, part_ref, sent_hbm, rows, blocks, sems):
    total = jnp.zeros((1, 64), F32)
    for z in range(16):
        got = got_ref[z].astype(F32)
        q, d = divmod(z, 4)
        for half in (0, 1):
            for side in (0, 1):
                at, lane = 12 * d + 6 * side, C * side + HALF * half
                rows[half, at : at + 6, 160 * q : 160 * (q + 1)] = got[0:6, lane : lane + HALF]
        total = total + got[6:7, 0:64] + got[6:7, 64:128] + got[6:7, 128:192]
    first = jnp.concatenate([*three_terms(total), jnp.zeros((1, 4 * HALF - 192), F32)], axis=1)
    second = jnp.concatenate([*three_terms(part_ref[...]), jnp.zeros((1, HALF), F32)], axis=1)
    tail = jnp.concatenate([first, second, jnp.zeros((6, 4 * HALF), F32)], axis=0).astype(BF16)
    copies = []
    for half in (0, 1):
        blocks[half, 0:48, :] = rows[half].astype(BF16)
        blocks[half, 48:56, :] = tail
        for i in range(16):
            goal = 8 * (i // 4) + 4 * half + i % 4
            copies.append(pltpu.make_async_copy(blocks.at[half], sent_hbm.at[goal], sems.at[goal]))
            copies[-1].start()
    for copy in copies:
        copy.wait()


def keep_mask(r, first_row, first_col):
    i = lax.broadcasted_iota(jnp.int32, (SEG, 1), 0)
    here = first_row + r
    row = jnp.where(i < 8, here - 1, here)
    col = first_col + jnp.where(i < 8, i + WIDE, i - GAP)
    good = (row >= 0) & (row < 128) & (col >= 0) & (col < 1024)
    return good.astype(F32)


def shift_add(merged_ref, start, size):
    back = merged_ref[pl.ds(start - 1, size), :]
    mid = merged_ref[pl.ds(start, size), :]
    ahead = merged_ref[pl.ds(start + 1, size), :]
    low = back[:, 0:128] + mid[:, 128:256] + ahead[:, 256:384]
    high = (
        back[:, 384:512]
        + pltpu.roll(mid[:, 384:512], 96, 1)
        + pltpu.roll(ahead[:, 384:512], 64, 1)
    )
    return jnp.concatenate([low, high[:, 0:32]], axis=1)


def join_kernel(own_ref, other_ref, wpad_ref, joined_ref, raw):
    order = ((0, 3), (0, 0), (1, 0), (0, 1), (1, 1), (0, 2), (1, 2), (1, 3))
    sub = lax.broadcasted_iota(jnp.int32, (GAP, LANES), 0)
    zeros = jnp.zeros((GAP, LANES), BF16)
    raw[0:GAP, :] = zeros
    raw[GAP + A_LEN : GAP + A_LEN + GAP, :] = zeros

    def lay_out(sources):
        for r in range(IN_ROWS + 1):
            before, after = None, None
            if r:
                which, at = order[r - 1]
                before = sources[which][at, WIDE:SEG, :].astype(F32)
            if r < IN_ROWS:
                which, at = order[r]
                after = sources[which][at, WIDE:SEG, :].astype(F32)
                raw[2 * GAP + r * SEG : GAP + (r + 1) * SEG, :] = sources[which][at, 0:WIDE, :]
            before = after if before is None else before
            after = before if after is None else after
            raw[GAP + r * SEG : 2 * GAP + r * SEG, :] = jnp.where(sub < 8, before, after).astype(BF16)

    core = lax.axis_index("core")

    @pl.when(core == 0)
    def _():
        lay_out((own_ref, other_ref))

    @pl.when(core == 1)
    def _():
        lay_out((other_ref, own_ref))

    def one(r, size):
        base = r * SEG
        tail = raw[rows_at(base, size + 2 * GAP), 256:384].astype(F32)
        skip = skip_of(tail, wpad_ref, GAP, GAP + size)
        joined = join(raw[rows_at(base + GAP, size), :].astype(F32), skip)
        joined_ref[rows_at(base, size), :] = joined.astype(BF16)

    def build(r, carry):
        one(r, SEG)
        return carry

    lax.fori_loop(0, IN_ROWS, build, 0)
    one(IN_ROWS, GAP)


def first_affine(sums, gain_ref):
    totals = sums / (20.0 * 131072.0)
    mean = totals[:, 0:32]
    var = totals[:, 32:64] - mean * mean
    pair = jnp.concatenate([lax.rsqrt(var + EPS), mean, jnp.zeros((6, 32), F32)], axis=0)
    spread = exact_dot(pair, same_group(32, 2 * C, 1, 20))
    scale = spread[0:1] * gain_ref[...] * 0.5
    return scale, -spread[1:2] * scale


def first_build(joined_ref, act, at, size, mask, scale, offset):
    where = slice(at, at + size)
    for lane in range(0, 2 * C, 128):
        part = slice(lane, lane + 128)
        values = joined_ref[where, part].astype(F32) * scale[:, part] + offset[:, part]
        act[where, part] = (silu_half(values) * mask[0:size]).astype(BF16)


def merged_conv(act, wm_ref, merged, start, size):
    taps = [act[start + a * SEG : start + a * SEG + size, :] for a in range(3)]
    merged[start + GAP : start + GAP + size, :] = tap_dot(jnp.concatenate(taps, axis=1), wm_ref[...])


def clear_ends(merged):
    size = merged.shape[0]
    merged[0:GAP, :] = jnp.zeros((GAP, MERGED), F32)
    merged[size - GAP : size, :] = jnp.zeros((GAP, MERGED), F32)


def first_own_kernel(
    joined_hbm, found_hbm, proj_ref, gain_ref,
    wm_hbm, known_ref, sum_ref,
    joined_ref, found_ref, rows, wm_ref, act, merged, sems,
):
    copies = [
        pltpu.make_async_copy(found_hbm, found_ref, sems.at[0]),
        pltpu.make_async_copy(joined_hbm.at[2 * SEG : 2 * SEG + B_LEN], joined_ref, sems.at[1]),
        pltpu.make_async_copy(wm_ref, wm_hbm, sems.at[2]),
    ]
    copies[0].start()
    copies[1].start()
    copies[0].wait()
    chip_row, first_col, _ = place()
    totals, shift = front_weight(found_ref, proj_ref, wm_ref, rows)
    copies[2].start()
    known_ref[...] = jnp.concatenate([totals, jnp.zeros((1, 64), F32), shift, jnp.zeros((1, 96), F32)], axis=1)
    scale, offset = first_affine(totals, gain_ref)
    clear_ends(merged)
    copies[1].wait()
    for r in range(5):
        mask = keep_mask(r + 2, chip_row - 3, first_col)
        first_build(joined_ref, act, r * SEG, SEG if r < 4 else GAP, mask, scale, offset)
    merged_conv(act, wm_ref, merged, 0, 2 * SEG + GAP)
    sums = jnp.zeros((1, HALF), F32)
    squares = jnp.zeros((1, HALF), F32)
    for r in range(2):
        values = shift_add(merged, 2 * GAP + r * SEG, WIDE) + shift
        sums = sums + jnp.sum(values, axis=0, keepdims=True)
        squares = squares + jnp.sum(values * values, axis=0, keepdims=True)
    send_sums(sums, squares, sum_ref)
    copies[2].wait()


def first_kernel(
    joined_hbm, wm_hbm, known_ref, gain_ref,
    hidden_ref,
    joined_ref, wm_ref, act, merged, sems,
):
    copies = []
    for i, part in enumerate((slice(0, 4 * SEG), slice(4 * SEG, A_LEN))):
        copies.append(pltpu.make_async_copy(joined_hbm.at[part], joined_ref.at[part], sems.at[i]))
    copies.append(pltpu.make_async_copy(wm_hbm, wm_ref, sems.at[2]))
    for copy in copies:
        copy.start()
    chip_row, first_col, _ = place()
    scale, offset = first_affine(known_ref[:, 0:64], gain_ref)
    shift = known_ref[:, 128 : 128 + HALF]

    def build(r):
        mask = keep_mask(r, chip_row - 3, first_col)
        first_build(joined_ref, act, r * SEG, SEG if r < IN_ROWS else GAP, mask, scale, offset)

    clear_ends(merged)
    copies[0].wait()
    for r in range(4):
        build(r)
    copies[2].wait()
    merged_conv(act, wm_ref, merged, 0, 2 * SEG)
    copies[1].wait()
    build(4)
    build(5)
    merged_conv(act, wm_ref, merged, 2 * SEG, 2 * SEG)
    for r in range(6, 9):
        build(r)
    merged_conv(act, wm_ref, merged, 4 * SEG, 2 * SEG + GAP)
    for r in range(MID_ROWS + 1):
        size = SEG if r < MID_ROWS else GAP
        hidden_ref[r * SEG : r * SEG + size, 0:HALF] = shift_add(merged, GAP + r * SEG, size) + shift
    hidden_ref[:, HALF:SWAP] = jnp.zeros((H_LEN, SWAP - HALF), F32)


def send_sums(sums, squares, sent_ref):
    both = jnp.concatenate([sums, squares, jnp.zeros((6, HALF), F32)], axis=0)
    grouped = exact_dot(both, same_group(HALF, 16, 10, 1))
    line = jnp.concatenate([grouped[0:1], grouped[1:2], jnp.zeros((1, 96), F32)], axis=1)
    for i in range(32):
        sent_ref[i] = line


def plane_sums_kernel(got_ref, sent_ref):
    cores = [jnp.zeros((1, 32), F32), jnp.zeros((1, 32), F32)]
    for i in range(32):
        half = (i // 4) % 2
        cores[half] = cores[half] + got_ref[i][:, 0:32]
    line = jnp.concatenate([*cores, jnp.zeros((1, 64), F32)], axis=1)
    for i in range(sent_ref.shape[0]):
        sent_ref[i] = line


def affine(stat_ref, gain_ref):
    both = stat_ref[0]
    for i in range(1, stat_ref.shape[0]):
        both = both + stat_ref[i]
    found = []
    for which in (0, 1):
        at = 32 * which
        padded = jnp.concatenate([both[:, at : at + 16], both[:, at + 16 : at + 32], jnp.zeros((6, 16), F32)], axis=0)
        totals = exact_dot(padded, same_group(16, HALF, 1, 10)) / (10.0 * 131072.0)
        mean = totals[0:1]
        scale = lax.rsqrt(totals[1:2] - mean * mean + EPS) * gain_ref[which : which + 1] * 0.5
        found.append((scale, -mean * scale))
    return found


def second_build(own_ref, other_ref, act, at, size, mask, affines):
    where = slice(at, at + size)
    first = lax.axis_index("core") == 0
    own, other = own_ref[where, 0:HALF], other_ref[where, 0:HALF]
    parts = []
    for which, (scale, offset) in enumerate(affines):
        values = jnp.where(first, own, other) if which == 0 else jnp.where(first, other, own)
        parts.append(silu_half(values * scale + offset) * mask[0:size])
    parts.append(jnp.zeros((size, LANES - C), F32))
    act[where, :] = jnp.concatenate(parts, axis=1).astype(BF16)


def second_own_kernel(
    own_hbm, other_hbm, stat_ref, gain_ref, found_hbm, joined_hbm,
    wm_hbm, skip_hbm, sum_ref,
    own_ref, other_ref, found_ref, joined_ref, wm_ref, skip_ref, act, merged, sems,
):
    part = slice(SEG, SEG + B_LEN)
    copies = [
        pltpu.make_async_copy(found_hbm, found_ref, sems.at[0]),
        pltpu.make_async_copy(own_hbm.at[part], own_ref, sems.at[1]),
        pltpu.make_async_copy(other_hbm.at[part], other_ref, sems.at[2]),
        pltpu.make_async_copy(joined_hbm.at[3 * SEG : 5 * SEG], joined_ref, sems.at[3]),
    ]
    for copy in copies:
        copy.start()
    back = [
        pltpu.make_async_copy(wm_ref, wm_hbm, sems.at[4]),
        pltpu.make_async_copy(skip_ref, skip_hbm, sems.at[5]),
    ]
    chip_row, first_col, _ = place()
    affines = affine(stat_ref, gain_ref)
    clear_ends(merged)
    copies[0].wait()
    middle_weight(found_ref, wm_ref, skip_ref)
    for copy in back:
        copy.start()
    copies[1].wait()
    copies[2].wait()
    for r in range(5):
        mask = keep_mask(r + 1, chip_row - 2, first_col)
        second_build(own_ref, other_ref, act, r * SEG, SEG if r < 4 else GAP, mask, affines)
    merged_conv(act, wm_ref, merged, 0, 2 * SEG + GAP)
    copies[3].wait()
    sums = jnp.zeros((1, HALF), F32)
    squares = jnp.zeros((1, HALF), F32)
    for r in range(2):
        at = r * SEG + GAP
        values = shift_add(merged, GAP + at, WIDE) + tap_dot(joined_ref[at : at + WIDE, :], skip_ref[...])
        sums = sums + jnp.sum(values, axis=0, keepdims=True)
        squares = squares + jnp.sum(values * values, axis=0, keepdims=True)
    send_sums(sums, squares, sum_ref)
    for copy in back:
        copy.wait()


def second_kernel(
    own_hbm, other_hbm, stat_ref, gain_ref, wm_hbm, skip_ref, joined_hbm,
    block_ref,
    own_ref, other_ref, joined_ref, wm_ref, act, merged, sems,
):
    copies = [
        pltpu.make_async_copy(own_hbm, own_ref, sems.at[0]),
        pltpu.make_async_copy(other_hbm, other_ref, sems.at[1]),
        pltpu.make_async_copy(wm_hbm, wm_ref, sems.at[2]),
        pltpu.make_async_copy(joined_hbm.at[2 * SEG : 2 * SEG + B_LEN], joined_ref, sems.at[3]),
    ]
    for copy in copies:
        copy.start()
    chip_row, first_col, _ = place()
    affines = affine(stat_ref, gain_ref)
    clear_ends(merged)
    copies[0].wait()
    copies[1].wait()

    def build(r):
        mask = keep_mask(r, chip_row - 2, first_col)
        second_build(own_ref, other_ref, act, r * SEG, SEG if r < MID_ROWS else GAP, mask, affines)

    for r in range(4):
        build(r)
    copies[2].wait()
    merged_conv(act, wm_ref, merged, 0, 2 * SEG)
    for r in range(4, 7):
        build(r)
    merged_conv(act, wm_ref, merged, 2 * SEG, 2 * SEG + GAP)
    copies[3].wait()
    for r in range(OUT_ROWS + 1):
        size = SEG if r < OUT_ROWS else GAP
        where = slice(r * SEG, r * SEG + size)
        block_ref[where, 0:HALF] = shift_add(merged, GAP + r * SEG, size) + tap_dot(
            joined_ref[where, :], skip_ref[...]
        )
    block_ref[:, HALF:SWAP] = jnp.zeros((B_LEN, SWAP - HALF), F32)


def third_kernel(own_hbm, other_hbm, stat_ref, gain_ref, wout_ref, noise_ref, own_ref, other_ref, sems):
    chip_row, first_col, core = place()
    needed = pl.ds(pl.multiple_of(core * SEG, 16), 3 * SEG + GAP)
    copies = [
        pltpu.make_async_copy(own_hbm.at[needed], own_ref, sems.at[0]),
        pltpu.make_async_copy(other_hbm.at[needed], other_ref, sems.at[1]),
    ]
    for copy in copies:
        copy.start()
    first_row = chip_row - 1 + core
    affines = affine(stat_ref, gain_ref)
    first = core == 0
    for copy in copies:
        copy.wait()
    parts = []
    for r in range(4):
        size = SEG if r < 3 else GAP
        mask = keep_mask(r, first_row, first_col)[0:size]
        where = slice(r * SEG, r * SEG + size)
        total = None
        own, other = own_ref[where, 0:HALF], other_ref[where, 0:HALF]
        for which, (scale, offset) in enumerate(affines):
            values = jnp.where(first, own, other) if which == 0 else jnp.where(first, other, own)
            act = (silu_half(values * scale + offset) * mask).astype(BF16)
            part = tap_dot(act, wout_ref[which])
            total = part if total is None else total + part
        parts.append(total)
    parts.append(jnp.zeros((896 - 3 * SEG - GAP, 128), F32))
    turned = jnp.concatenate(parts, axis=0).T
    noise = None
    for a in range(3):
        for b in range(3):
            tap = 3 * a + b
            at = a * SEG + GAP + b - 1
            piece = turned[8 * tap : 8 * tap + 8, at : at + WIDE]
            noise = piece if noise is None else noise + piece
    for o in range(4):
        noise_ref[o] = noise[o : o + 1]


def place_merged(out_ref, at, size, b, piece):
    out_ref[at : at + size, 128 * b : 128 * (b + 1)] = piece[:, 0:128]
    out_ref[at : at + size, 384 + 32 * b : 384 + 32 * (b + 1)] = piece[:, 128:160]


def front_weight(found_ref, proj_ref, out_ref, rows):
    out_ref[:, 480:512] = jnp.zeros((3 * 2 * C, 32), BF16)
    sums = jnp.zeros((1, 64), F32)
    embedded = []
    for shard in range(8):
        part = jnp.zeros((1, HALF), F32)
        for x in range(4):
            j = 4 * shard + x
            found = found_ref[j].astype(F32)
            size = 12 if x < 3 else 9
            for d in range(4):
                at = 360 * d + 45 * shard + 12 * x
                rows[at : at + size, :] = found[12 * d : 12 * d + size]
            for term in range(3):
                sums = sums + found[48:49, 64 * term : 64 * (term + 1)]
                part = part + found[49:50, HALF * term : HALF * (term + 1)]
        embedded.append(part)
    values = jnp.concatenate(embedded, axis=1)
    values = values / (1.0 + jnp.exp(-values))
    proj = proj_ref[rows_at(lax.axis_index("core") * HALF, HALF), :].astype(F32)
    shift = jnp.sum(proj * values, axis=1, keepdims=True)
    shift = jnp.concatenate([jnp.broadcast_to(shift, (HALF, 128)), jnp.zeros((WIDE - HALF, 128), F32)], axis=0)
    shift = shift.T[0:1, 0:HALF]
    for q in range(4):
        row = 1440 * q
        while row < 1440 * (q + 1):
            tap, channel = divmod(row, 2 * C)
            size = min(1440 * (q + 1) - row, 2 * C - channel)
            a, b = divmod(tap, 3)
            k = row - 1440 * q
            piece = rows[k : k + size, 160 * q : 160 * (q + 1)].astype(BF16)
            place_merged(out_ref, a * 2 * C + channel, size, b, piece)
            row += size
    return sums, shift


def share_kernel(middle_ref, skip_ref, out_ref):
    core = lax.axis_index("core")
    middle = middle_ref[rows_at(core * HALF, HALF), :].astype(F32).T
    wide = skip_ref[...].astype(F32)
    skip = jnp.where(core == 0, wide[:, 0:HALF], wide[:, HALF:C])
    whole = jnp.concatenate([middle, skip, jnp.zeros((16, HALF), F32)], axis=0)
    parts = [whole[224 * q : 224 * (q + 1)] for q in range(4)]
    out_ref[...] = jnp.concatenate(parts, axis=1).astype(BF16)


def middle_weight(found_ref, out_ref, skip_ref):
    out_ref[:, 480:512] = jnp.zeros((3 * LANES, 32), BF16)

    def pieces(x, row, size):
        while size:
            q, i = divmod(row, 224)
            some = min(size, 224 - i)
            yield some, found_ref[x, i : i + some, 160 * q : 160 * (q + 1)]
            row, size = row + some, size - some

    for a in range(3):
        out_ref[a * LANES + C : (a + 1) * LANES, :] = jnp.zeros((LANES - C, MERGED), BF16)
    for tap in range(9):
        a, b = divmod(tap, 3)
        at = a * LANES
        for part in range(4):
            x, i = divmod(tap * C + part * 80, 720)
            for size, piece in pieces(x, i, 80):
                place_merged(out_ref, at, size, b, piece)
                at += size
    at = 0
    for x in range(4):
        for size, piece in pieces(x, 720, HALF):
            skip_ref[at : at + size, :] = piece
            at += size


def shifted(x, axis, step):
    count = lax.axis_size(axis)
    return lax.ppermute(x, axis, [(i, i + step) for i in range(count) if 0 <= i + step < count])


def summed(sums, kept):
    near = lax.all_to_all(sums, PLANE, 0, 0, tiled=True)
    near, kept = lax.optimization_barrier((near, kept))
    near = call(plane_sums_kernel, sds((lax.axis_size(DEPTH), 1, 128), F32), [VMEM])(near)
    return lax.all_to_all(near, DEPTH, 0, 0, tiled=True), kept


def shards(
    latent, deep, timestep, in_weight, front_weight, middle_weight, skip_weight, out_weight,
    time_weight, time_second, time_proj, input_gain, middle_gain, output_gain,
):
    core, x, y = lax.axis_index("core"), lax.axis_index("x"), lax.axis_index("y")
    depths = lax.axis_size(DEPTH)

    above, below = shifted(latent, ROWS, 1), shifted(latent, ROWS, -1)
    quarter = lax.dynamic_slice_in_dim(jnp.pad(front_weight, ((0, 3), (0, 0))), 12 * x, 12, 0)
    cells, first, last, wpad = call(
        pack_kernel,
        (sds((WIDE, LANES), BF16), sds((GAP, LANES), BF16), sds((GAP, LANES), BF16), sds((LANES, LANES), BF16)),
        [VMEM] * 5,
        [pltpu.VMEM((LANES, WIDE), F32), pltpu.VMEM((LANES, LANES), F32)],
    )(deep.reshape(C, WIDE), above.reshape(4, WIDE), latent.reshape(4, WIDE), below.reshape(4, WIDE), in_weight)
    from_right, from_left = shifted(first, "x", -1), shifted(last, "x", 1)
    row, sent = call(stats_kernel, (sds((SEG, LANES), BF16), sds((depths, 8, 2 * C), BF16)), [VMEM] * 5)(
        cells, from_left, from_right, wpad, quarter
    )

    row, skip_here = lax.optimization_barrier((row, skip_weight))
    packed = call(share_kernel, sds((224, 4 * HALF), BF16), [VMEM] * 2)(middle_weight.T, skip_here)

    count = lax.axis_size(ROWS)
    crossed = [(i, i + 3) if i % 2 else (i, i - 3) for i in range(count)]
    crossed = [(i, j) for i, j in crossed if 0 <= j < count]
    before, after, across = shifted(row, ROWS, 2), shifted(row, ROWS, -2), lax.ppermute(row, ROWS, crossed)

    half_width = time_weight.shape[0] // 2
    ratios = jnp.exp(-math.log(10000.0) * jnp.arange(half_width, dtype=F32) / half_width)
    angles = timestep[0].astype(F32) * ratios
    features = jnp.concatenate([jnp.cos(angles), jnp.sin(angles)])
    depth_here = time_second.shape[0]
    weight_here = lax.dynamic_slice_in_dim(time_weight, x * depth_here, depth_here, 1)
    hidden = jax.nn.silu(jnp.dot(features, weight_here.astype(F32), precision=HIGH))
    columns = lax.dynamic_slice_in_dim(time_second, (2 * y + core) * HALF, HALF, 1)
    part = jnp.dot(hidden, columns.astype(F32), precision=HIGH)

    got = lax.all_to_all(sent, DEPTH, 0, 0, tiled=True)
    scratch = [
        pltpu.VMEM((2, 48, 4 * HALF), F32),
        pltpu.VMEM((2, 56, 4 * HALF), BF16),
        pltpu.SemaphoreType.DMA((32,)),
    ]
    sent = call(plane_kernel, sds((32, 56, 4 * HALF), BF16), [VMEM] * 2, scratch, 52, ANY)(got, part[None])
    around = jnp.stack([before, row, after, across])
    sent, around = lax.optimization_barrier((sent, around))
    found = lax.all_to_all(sent, PLANE, 0, 0, tiled=True)
    swap = [(0, 1), (1, 0)]
    joined = call(
        join_kernel, sds((A_LEN, 2 * C), BF16), [VMEM] * 3, [pltpu.VMEM((A_LEN + 2 * GAP, LANES), BF16)], 60
    )(around, lax.ppermute(around, "core", swap), wpad)
    own_scratch = [
        pltpu.VMEM((B_LEN, 2 * C), BF16),
        pltpu.VMEM((32, 56, 4 * HALF), BF16),
        pltpu.VMEM((1440, 4 * HALF), F32),
        pltpu.VMEM((3 * 2 * C, MERGED), BF16),
        pltpu.VMEM((B_LEN, 2 * C), BF16),
        pltpu.VMEM((2 * SEG + 3 * GAP, MERGED), F32),
        pltpu.SemaphoreType.DMA((3,)),
    ]
    front, known, sums = call(
        first_own_kernel,
        (sds((3 * 2 * C, MERGED), BF16), sds((1, 384), F32), sds((32, 1, 128), F32)),
        [ANY, ANY, VMEM, VMEM],
        own_scratch,
        52,
        (ANY, VMEM, VMEM),
    )(joined, found, time_proj.T, input_gain[None])
    packed, sums = lax.optimization_barrier((packed, sums))
    middle_found = lax.all_gather(packed, "x", axis=0)
    hidden_own = call(
        first_kernel,
        sds((H_LEN, SWAP), F32),
        [ANY, ANY, VMEM, VMEM],
        [
            pltpu.VMEM((A_LEN, 2 * C), BF16),
            pltpu.VMEM((3 * 2 * C, MERGED), BF16),
            pltpu.VMEM((A_LEN, 2 * C), BF16),
            pltpu.VMEM((H_LEN + 2 * GAP, MERGED), F32),
            pltpu.SemaphoreType.DMA((3,)),
        ],
        52,
    )(joined, front, known, input_gain[None])
    totals, hidden_own = summed(sums, hidden_own)
    hidden_other = lax.ppermute(hidden_own, "core", swap)

    gain_two = middle_gain.reshape(2, HALF)
    middle, shortcut, sums = call(
        second_own_kernel,
        (sds((3 * LANES, MERGED), BF16), sds((2 * C, HALF), BF16), sds((32, 1, 128), F32)),
        [ANY, ANY, VMEM, VMEM, ANY, ANY],
        [
            pltpu.VMEM((B_LEN, SWAP), F32),
            pltpu.VMEM((B_LEN, SWAP), F32),
            pltpu.VMEM((4, 224, 4 * HALF), BF16),
            pltpu.VMEM((2 * SEG, 2 * C), BF16),
            pltpu.VMEM((3 * LANES, MERGED), BF16),
            pltpu.VMEM((2 * C, HALF), BF16),
            pltpu.VMEM((B_LEN, LANES), BF16),
            pltpu.VMEM((2 * SEG + 3 * GAP, MERGED), F32),
            pltpu.SemaphoreType.DMA((6,)),
        ],
        52,
        (ANY, ANY, VMEM),
    )(hidden_own, hidden_other, totals, gain_two, middle_found, joined)
    block_own = call(
        second_kernel,
        sds((B_LEN, SWAP), F32),
        [ANY, ANY, VMEM, VMEM, ANY, VMEM, ANY],
        [
            pltpu.VMEM((H_LEN, SWAP), F32),
            pltpu.VMEM((H_LEN, SWAP), F32),
            pltpu.VMEM((B_LEN, 2 * C), BF16),
            pltpu.VMEM((3 * LANES, MERGED), BF16),
            pltpu.VMEM((H_LEN, LANES), BF16),
            pltpu.VMEM((B_LEN + 2 * GAP, MERGED), F32),
            pltpu.SemaphoreType.DMA((4,)),
        ],
        52,
    )(hidden_own, hidden_other, totals, gain_two, middle, shortcut, joined)
    totals, block_own = summed(sums, block_own)
    block_other = lax.ppermute(block_own, "core", swap)

    wout = out_weight.reshape(9, 2, HALF, 4).transpose(1, 2, 0, 3)
    wout = jnp.pad(jnp.pad(wout, ((0, 0), (0, 0), (0, 0), (0, 4))).reshape(2, HALF, 72), ((0, 0), (0, 0), (0, 56)))
    scratch = [
        pltpu.VMEM((3 * SEG + GAP, SWAP), F32),
        pltpu.VMEM((3 * SEG + GAP, SWAP), F32),
        pltpu.SemaphoreType.DMA((2,)),
    ]
    return call(third_kernel, sds((4, 1, WIDE), F32), [ANY, ANY, VMEM, VMEM, VMEM], scratch, 30)(
        block_own, block_other, totals, output_gain.reshape(2, HALF), wout
    )


def solution(mesh):
    finer = Mesh(
        mesh.devices.reshape(8, 2, 4, 2, mesh.shape["cols"]), ("zp", "zl", "y", "core", "x")
    )
    in_specs = (
        P(None, ROWS, "x"),
        P(None, ROWS, "x"),
        P(),
        P(),
        P(ROWS, None),
        P("x", None),
        P("x", None),
        P(),
        P(),
        P("x", None),
        P(),
        P(),
        P(),
        P(),
    )
    return jax.shard_map(
        shards, mesh=finer, in_specs=in_specs, out_specs=P(None, ROWS, "x"), check_vma=False
    )
```

```python
import math

import jax
import jax.numpy as jnp
from jax import lax
from jax.experimental import pallas as pl
from jax.experimental.pallas import tpu as pltpu
from jax.sharding import Mesh
from jax.sharding import PartitionSpec as P

ROWS = ("zp", "zl", "y", "core")
DEPTH = ("zp", "zl")
PLANE = ("y", "core", "x")
EPS = 1e-05
F32 = jnp.float32
BF16 = jnp.bfloat16
HIGH = lax.Precision.HIGHEST

C = 320
HALF = 160
WIDE = 256
GAP = 16
SEG = WIDE + GAP
IN_ROWS = 8
MID_ROWS = 6
OUT_ROWS = 4
A_LEN = IN_ROWS * SEG + GAP
H_LEN = MID_ROWS * SEG + GAP
B_LEN = OUT_ROWS * SEG + GAP
MERGED = 512
LANES = 384
SWAP = 256
VMEM = pl.BlockSpec(memory_space=pltpu.VMEM)
ANY = pl.BlockSpec(memory_space=pltpu.HBM)


def call(kernel, out_shape, in_specs, scratch=(), limit=16, out_spec=VMEM):
    return pl.pallas_call(
        kernel,
        out_shape=out_shape,
        in_specs=in_specs,
        out_specs=out_spec if isinstance(out_spec, tuple) else jax.tree.map(lambda _: out_spec, out_shape),
        scratch_shapes=list(scratch),
        compiler_params=pltpu.CompilerParams(vmem_limit_bytes=limit * 1024 * 1024),
    )


def sds(shape, dtype):
    return jax.ShapeDtypeStruct(shape, dtype)


def rows_at(start, size):
    return pl.ds(pl.multiple_of(start, 16), size)


def place():
    return 2 * lax.axis_index(("zp", "zl", "y")), lax.axis_index("x") * WIDE, lax.axis_index("core")


def same_group(n, m, size_n, size_m):
    i = lax.broadcasted_iota(jnp.int32, (n, m), 0)
    j = lax.broadcasted_iota(jnp.int32, (n, m), 1)
    return ((i // size_n) == (j // size_m)).astype(F32)


def exact_dot(a, b):
    return jnp.dot(a, b, preferred_element_type=F32, precision=HIGH)


def tap_dot(a, b):
    return jnp.dot(a, b, preferred_element_type=F32)


def silu_half(h):
    return h + h * jnp.tanh(h)


def pack_kernel(deep_ref, prev_ref, here_ref, next_ref, weight_ref, out_ref, first_ref, last_ref, wpad_ref, tall, wide):
    tall[0:C, :] = deep_ref[...].astype(F32)
    tall[C:LANES, :] = jnp.zeros((LANES - C, WIDE), F32)
    for i, ref in enumerate((prev_ref, here_ref, next_ref)):
        tall[C + 4 * i : C + 4 * i + 4, :] = ref[...].astype(F32)
    out = tall[...].T.astype(BF16)
    out_ref[...] = out
    first_ref[...] = out[0:GAP]
    last_ref[...] = out[WIDE - GAP : WIDE]
    wide[...] = jnp.zeros((LANES, LANES), F32)
    weight = weight_ref[...].astype(F32)
    for tap in range(9):
        a, b = divmod(tap, 3)
        at = 128 * b + 64 + 4 * a
        wide[at : at + 4, 64:LANES] = weight[4 * tap : 4 * tap + 4]
    wpad_ref[...] = wide[...].astype(BF16)


def skip_of(tail, wpad_ref, lo, hi):
    n = tail.shape[0]
    left = pltpu.roll(tail, 1, 0)[lo:hi].astype(BF16)
    right = pltpu.roll(tail, n - 1, 0)[lo:hi].astype(BF16)
    mid = tail[lo:hi].astype(BF16)
    stacked = jnp.concatenate([left, mid, right], axis=1)
    return tap_dot(stacked, wpad_ref[...]).astype(BF16).astype(F32)


def join(cells, skip):
    lane = lax.broadcasted_iota(jnp.int32, (cells.shape[0], 128), 1)
    mixed = jnp.where(lane < 64, cells[:, 256:384], skip[:, 0:128])
    return jnp.concatenate([cells[:, 0:256], mixed, skip[:, 128:384]], axis=1)


def three_terms(values):
    high = values.astype(BF16).astype(F32)
    middle = (values - high).astype(BF16).astype(F32)
    return high, middle, values - high - middle


def stats_kernel(cells_ref, left_ref, right_ref, wpad_ref, quarter_ref, row_ref, sent_ref):
    sub = lax.broadcasted_iota(jnp.int32, (GAP, LANES), 0)
    gap = jnp.where(sub < 8, right_ref[...].astype(F32), left_ref[...].astype(F32))
    cells = jnp.concatenate([cells_ref[...].astype(F32), gap], axis=0)
    row_ref[...] = cells.astype(BF16)
    skip = skip_of(cells[:, 256:384], wpad_ref, 0, WIDE)
    joined = join(cells[0:WIDE], skip)
    sums = jnp.sum(joined, axis=0, keepdims=True)
    squares = jnp.sum(joined * joined, axis=0, keepdims=True)
    both = jnp.concatenate([sums, squares, jnp.zeros((6, 2 * C), F32)], axis=0)
    grouped = exact_dot(both, same_group(2 * C, 32, 20, 1))
    terms = three_terms(jnp.concatenate([grouped[0:1], grouped[1:2]], axis=1))
    line = jnp.concatenate([*terms, jnp.zeros((1, C - 192), F32)], axis=1)
    message = jnp.concatenate([quarter_ref[...].astype(F32), line, jnp.zeros((3, C), F32)], axis=0).astype(BF16)
    for z in range(sent_ref.shape[0]):
        sent_ref[z] = message


def plane_kernel(got_ref, part_ref, sent_hbm, rows, blocks, sems):
    total = jnp.zeros((1, 64), F32)
    for z in range(16):
        got = got_ref[z].astype(F32)
        q, d = divmod(z, 4)
        for half in (0, 1):
            rows[half, 12 * d : 12 * d + 12, 160 * q : 160 * (q + 1)] = got[0:12, 160 * half : 160 * (half + 1)]
        total = total + got[12:13, 0:64] + got[12:13, 64:128] + got[12:13, 128:192]
    first = jnp.concatenate([*three_terms(total), jnp.zeros((1, 4 * HALF - 192), F32)], axis=1)
    second = jnp.concatenate([*three_terms(part_ref[...]), jnp.zeros((1, HALF), F32)], axis=1)
    tail = jnp.concatenate([first, second, jnp.zeros((6, 4 * HALF), F32)], axis=0).astype(BF16)
    copies = []
    for half in (0, 1):
        blocks[half, 0:48, :] = rows[half].astype(BF16)
        blocks[half, 48:56, :] = tail
        for i in range(16):
            goal = 8 * (i // 4) + 4 * half + i % 4
            copies.append(pltpu.make_async_copy(blocks.at[half], sent_hbm.at[goal], sems.at[goal]))
            copies[-1].start()
    for copy in copies:
        copy.wait()


def keep_mask(r, first_row, first_col):
    i = lax.broadcasted_iota(jnp.int32, (SEG, 1), 0)
    here = first_row + r
    row = jnp.where(i < 8, here - 1, here)
    col = first_col + jnp.where(i < 8, i + WIDE, i - GAP)
    good = (row >= 0) & (row < 128) & (col >= 0) & (col < 1024)
    return good.astype(F32)


def shift_add(merged_ref, start, size):
    back = merged_ref[pl.ds(start - 1, size), :]
    mid = merged_ref[pl.ds(start, size), :]
    ahead = merged_ref[pl.ds(start + 1, size), :]
    low = back[:, 0:128] + mid[:, 128:256] + ahead[:, 256:384]
    high = (
        back[:, 384:512]
        + pltpu.roll(mid[:, 384:512], 96, 1)
        + pltpu.roll(ahead[:, 384:512], 64, 1)
    )
    return jnp.concatenate([low, high[:, 0:32]], axis=1)


def join_kernel(own_ref, other_ref, wpad_ref, joined_ref, raw):
    order = ((0, 3), (0, 0), (1, 0), (0, 1), (1, 1), (0, 2), (1, 2), (1, 3))
    sub = lax.broadcasted_iota(jnp.int32, (GAP, LANES), 0)
    zeros = jnp.zeros((GAP, LANES), BF16)
    raw[0:GAP, :] = zeros
    raw[GAP + A_LEN : GAP + A_LEN + GAP, :] = zeros

    def lay_out(sources):
        for r in range(IN_ROWS + 1):
            before, after = None, None
            if r:
                which, at = order[r - 1]
                before = sources[which][at, WIDE:SEG, :].astype(F32)
            if r < IN_ROWS:
                which, at = order[r]
                after = sources[which][at, WIDE:SEG, :].astype(F32)
                raw[2 * GAP + r * SEG : GAP + (r + 1) * SEG, :] = sources[which][at, 0:WIDE, :]
            before = after if before is None else before
            after = before if after is None else after
            raw[GAP + r * SEG : 2 * GAP + r * SEG, :] = jnp.where(sub < 8, before, after).astype(BF16)

    core = lax.axis_index("core")

    @pl.when(core == 0)
    def _():
        lay_out((own_ref, other_ref))

    @pl.when(core == 1)
    def _():
        lay_out((other_ref, own_ref))

    def one(r, size):
        base = r * SEG
        tail = raw[rows_at(base, size + 2 * GAP), 256:384].astype(F32)
        skip = skip_of(tail, wpad_ref, GAP, GAP + size)
        joined = join(raw[rows_at(base + GAP, size), :].astype(F32), skip)
        joined_ref[rows_at(base, size), :] = joined.astype(BF16)

    def build(r, carry):
        one(r, SEG)
        return carry

    lax.fori_loop(0, IN_ROWS, build, 0)
    one(IN_ROWS, GAP)


def first_affine(sums, gain_ref):
    totals = sums / (20.0 * 131072.0)
    mean = totals[:, 0:32]
    var = totals[:, 32:64] - mean * mean
    pair = jnp.concatenate([lax.rsqrt(var + EPS), mean, jnp.zeros((6, 32), F32)], axis=0)
    spread = exact_dot(pair, same_group(32, 2 * C, 1, 20))
    scale = spread[0:1] * gain_ref[...] * 0.5
    return scale, -spread[1:2] * scale


def first_build(joined_ref, act, at, size, mask, scale, offset):
    where = slice(at, at + size)
    for lane in range(0, 2 * C, 128):
        part = slice(lane, lane + 128)
        values = joined_ref[where, part].astype(F32) * scale[:, part] + offset[:, part]
        act[where, part] = (silu_half(values) * mask[0:size]).astype(BF16)


def merged_conv(act, wm_ref, merged, start, size):
    taps = [act[start + a * SEG : start + a * SEG + size, :] for a in range(3)]
    merged[start + GAP : start + GAP + size, :] = tap_dot(jnp.concatenate(taps, axis=1), wm_ref[...])


def clear_ends(merged):
    size = merged.shape[0]
    merged[0:GAP, :] = jnp.zeros((GAP, MERGED), F32)
    merged[size - GAP : size, :] = jnp.zeros((GAP, MERGED), F32)


def first_own_kernel(
    joined_hbm, found_hbm, proj_ref, gain_ref,
    wm_hbm, known_ref, sum_ref,
    joined_ref, found_ref, rows, wm_ref, act, merged, sems,
):
    copies = [
        pltpu.make_async_copy(found_hbm, found_ref, sems.at[0]),
        pltpu.make_async_copy(joined_hbm.at[2 * SEG : 2 * SEG + B_LEN], joined_ref, sems.at[1]),
        pltpu.make_async_copy(wm_ref, wm_hbm, sems.at[2]),
    ]
    copies[0].start()
    copies[1].start()
    copies[0].wait()
    chip_row, first_col, _ = place()
    totals, shift = front_weight(found_ref, proj_ref, wm_ref, rows)
    copies[2].start()
    known_ref[...] = jnp.concatenate([totals, jnp.zeros((1, 64), F32), shift, jnp.zeros((1, 96), F32)], axis=1)
    scale, offset = first_affine(totals, gain_ref)
    clear_ends(merged)
    copies[1].wait()
    for r in range(5):
        mask = keep_mask(r + 2, chip_row - 3, first_col)
        first_build(joined_ref, act, r * SEG, SEG if r < 4 else GAP, mask, scale, offset)
    merged_conv(act, wm_ref, merged, 0, 2 * SEG + GAP)
    sums = jnp.zeros((1, HALF), F32)
    squares = jnp.zeros((1, HALF), F32)
    for r in range(2):
        values = shift_add(merged, 2 * GAP + r * SEG, WIDE) + shift
        sums = sums + jnp.sum(values, axis=0, keepdims=True)
        squares = squares + jnp.sum(values * values, axis=0, keepdims=True)
    send_sums(sums, squares, sum_ref)
    copies[2].wait()


def first_kernel(
    joined_hbm, wm_hbm, known_ref, gain_ref,
    hidden_ref,
    joined_ref, wm_ref, act, merged, sems,
):
    copies = []
    for i, part in enumerate((slice(0, 4 * SEG), slice(4 * SEG, A_LEN))):
        copies.append(pltpu.make_async_copy(joined_hbm.at[part], joined_ref.at[part], sems.at[i]))
    copies.append(pltpu.make_async_copy(wm_hbm, wm_ref, sems.at[2]))
    for copy in copies:
        copy.start()
    chip_row, first_col, _ = place()
    scale, offset = first_affine(known_ref[:, 0:64], gain_ref)
    shift = known_ref[:, 128 : 128 + HALF]

    def build(r):
        mask = keep_mask(r, chip_row - 3, first_col)
        first_build(joined_ref, act, r * SEG, SEG if r < IN_ROWS else GAP, mask, scale, offset)

    clear_ends(merged)
    copies[0].wait()
    for r in range(4):
        build(r)
    copies[2].wait()
    merged_conv(act, wm_ref, merged, 0, 2 * SEG)
    copies[1].wait()
    build(4)
    build(5)
    merged_conv(act, wm_ref, merged, 2 * SEG, 2 * SEG)
    for r in range(6, 9):
        build(r)
    merged_conv(act, wm_ref, merged, 4 * SEG, 2 * SEG + GAP)
    for r in range(MID_ROWS + 1):
        size = SEG if r < MID_ROWS else GAP
        hidden_ref[r * SEG : r * SEG + size, 0:HALF] = shift_add(merged, GAP + r * SEG, size) + shift
    hidden_ref[:, HALF:SWAP] = jnp.zeros((H_LEN, SWAP - HALF), F32)


def send_sums(sums, squares, sent_ref):
    both = jnp.concatenate([sums, squares, jnp.zeros((6, HALF), F32)], axis=0)
    grouped = exact_dot(both, same_group(HALF, 16, 10, 1))
    line = jnp.concatenate([grouped[0:1], grouped[1:2], jnp.zeros((1, 96), F32)], axis=1)
    for i in range(32):
        sent_ref[i] = line


def plane_sums_kernel(got_ref, sent_ref):
    cores = [jnp.zeros((1, 32), F32), jnp.zeros((1, 32), F32)]
    for i in range(32):
        half = (i // 4) % 2
        cores[half] = cores[half] + got_ref[i][:, 0:32]
    line = jnp.concatenate([*cores, jnp.zeros((1, 64), F32)], axis=1)
    for i in range(sent_ref.shape[0]):
        sent_ref[i] = line


def affine(stat_ref, gain_ref):
    both = stat_ref[0]
    for i in range(1, stat_ref.shape[0]):
        both = both + stat_ref[i]
    found = []
    for which in (0, 1):
        at = 32 * which
        padded = jnp.concatenate([both[:, at : at + 16], both[:, at + 16 : at + 32], jnp.zeros((6, 16), F32)], axis=0)
        totals = exact_dot(padded, same_group(16, HALF, 1, 10)) / (10.0 * 131072.0)
        mean = totals[0:1]
        scale = lax.rsqrt(totals[1:2] - mean * mean + EPS) * gain_ref[which : which + 1] * 0.5
        found.append((scale, -mean * scale))
    return found


def second_build(own_ref, other_ref, act, at, size, mask, affines):
    where = slice(at, at + size)
    first = lax.axis_index("core") == 0
    own, other = own_ref[where, 0:HALF], other_ref[where, 0:HALF]
    parts = []
    for which, (scale, offset) in enumerate(affines):
        values = jnp.where(first, own, other) if which == 0 else jnp.where(first, other, own)
        parts.append(silu_half(values * scale + offset) * mask[0:size])
    parts.append(jnp.zeros((size, LANES - C), F32))
    act[where, :] = jnp.concatenate(parts, axis=1).astype(BF16)


def middle_weight_kernel(found_hbm, wm_hbm, skip_hbm, found_ref, wm_ref, skip_ref, sems):
    copy = pltpu.make_async_copy(found_hbm, found_ref, sems.at[0])
    copy.start()
    copy.wait()
    middle_weight(found_ref, wm_ref, skip_ref)
    back = [
        pltpu.make_async_copy(wm_ref, wm_hbm, sems.at[1]),
        pltpu.make_async_copy(skip_ref, skip_hbm, sems.at[2]),
    ]
    for copy in back:
        copy.start()
    for copy in back:
        copy.wait()


def second_own_kernel(
    own_hbm, other_hbm, stat_ref, gain_ref, wm_hbm, skip_hbm, joined_hbm,
    sum_ref,
    own_ref, other_ref, joined_ref, wm_ref, skip_ref, act, merged, sems,
):
    part = slice(SEG, SEG + B_LEN)
    copies = [
        pltpu.make_async_copy(own_hbm.at[part], own_ref, sems.at[0]),
        pltpu.make_async_copy(other_hbm.at[part], other_ref, sems.at[1]),
        pltpu.make_async_copy(wm_hbm, wm_ref, sems.at[2]),
        pltpu.make_async_copy(joined_hbm.at[3 * SEG : 5 * SEG], joined_ref, sems.at[3]),
        pltpu.make_async_copy(skip_hbm, skip_ref, sems.at[4]),
    ]
    for copy in copies:
        copy.start()
    chip_row, first_col, _ = place()
    affines = affine(stat_ref, gain_ref)
    clear_ends(merged)
    copies[0].wait()
    copies[1].wait()
    for r in range(5):
        mask = keep_mask(r + 1, chip_row - 2, first_col)
        second_build(own_ref, other_ref, act, r * SEG, SEG if r < 4 else GAP, mask, affines)
    copies[2].wait()
    merged_conv(act, wm_ref, merged, 0, 2 * SEG + GAP)
    copies[3].wait()
    copies[4].wait()
    sums = jnp.zeros((1, HALF), F32)
    squares = jnp.zeros((1, HALF), F32)
    for r in range(2):
        at = r * SEG + GAP
        values = shift_add(merged, GAP + at, WIDE) + tap_dot(joined_ref[at : at + WIDE, :], skip_ref[...])
        sums = sums + jnp.sum(values, axis=0, keepdims=True)
        squares = squares + jnp.sum(values * values, axis=0, keepdims=True)
    send_sums(sums, squares, sum_ref)


def second_kernel(
    own_hbm, other_hbm, stat_ref, gain_ref, wm_hbm, skip_ref, joined_hbm,
    block_ref,
    own_ref, other_ref, joined_ref, wm_ref, act, merged, sems,
):
    copies = [
        pltpu.make_async_copy(own_hbm, own_ref, sems.at[0]),
        pltpu.make_async_copy(other_hbm, other_ref, sems.at[1]),
        pltpu.make_async_copy(wm_hbm, wm_ref, sems.at[2]),
        pltpu.make_async_copy(joined_hbm.at[2 * SEG : 2 * SEG + B_LEN], joined_ref, sems.at[3]),
    ]
    for copy in copies:
        copy.start()
    chip_row, first_col, _ = place()
    affines = affine(stat_ref, gain_ref)
    clear_ends(merged)
    copies[0].wait()
    copies[1].wait()

    def build(r):
        mask = keep_mask(r, chip_row - 2, first_col)
        second_build(own_ref, other_ref, act, r * SEG, SEG if r < MID_ROWS else GAP, mask, affines)

    for r in range(4):
        build(r)
    copies[2].wait()
    merged_conv(act, wm_ref, merged, 0, 2 * SEG)
    for r in range(4, 7):
        build(r)
    merged_conv(act, wm_ref, merged, 2 * SEG, 2 * SEG + GAP)
    copies[3].wait()
    for r in range(OUT_ROWS + 1):
        size = SEG if r < OUT_ROWS else GAP
        where = slice(r * SEG, r * SEG + size)
        block_ref[where, 0:HALF] = shift_add(merged, GAP + r * SEG, size) + tap_dot(
            joined_ref[where, :], skip_ref[...]
        )
    block_ref[:, HALF:SWAP] = jnp.zeros((B_LEN, SWAP - HALF), F32)


def third_kernel(own_hbm, other_hbm, stat_ref, gain_ref, wout_ref, noise_ref, own_ref, other_ref, sems):
    chip_row, first_col, core = place()
    needed = pl.ds(pl.multiple_of(core * SEG, 16), 3 * SEG + GAP)
    copies = [
        pltpu.make_async_copy(own_hbm.at[needed], own_ref, sems.at[0]),
        pltpu.make_async_copy(other_hbm.at[needed], other_ref, sems.at[1]),
    ]
    for copy in copies:
        copy.start()
    first_row = chip_row - 1 + core
    affines = affine(stat_ref, gain_ref)
    first = core == 0
    for copy in copies:
        copy.wait()
    parts = []
    for r in range(4):
        size = SEG if r < 3 else GAP
        mask = keep_mask(r, first_row, first_col)[0:size]
        where = slice(r * SEG, r * SEG + size)
        total = None
        own, other = own_ref[where, 0:HALF], other_ref[where, 0:HALF]
        for which, (scale, offset) in enumerate(affines):
            values = jnp.where(first, own, other) if which == 0 else jnp.where(first, other, own)
            act = (silu_half(values * scale + offset) * mask).astype(BF16)
            part = tap_dot(act, wout_ref[which])
            total = part if total is None else total + part
        parts.append(total)
    parts.append(jnp.zeros((896 - 3 * SEG - GAP, 128), F32))
    turned = jnp.concatenate(parts, axis=0).T
    noise = None
    for a in range(3):
        for b in range(3):
            tap = 3 * a + b
            at = a * SEG + GAP + b - 1
            piece = turned[8 * tap : 8 * tap + 8, at : at + WIDE]
            noise = piece if noise is None else noise + piece
    for o in range(4):
        noise_ref[o] = noise[o : o + 1]


def place_merged(out_ref, at, size, b, piece):
    out_ref[at : at + size, 128 * b : 128 * (b + 1)] = piece[:, 0:128]
    out_ref[at : at + size, 384 + 32 * b : 384 + 32 * (b + 1)] = piece[:, 128:160]


def front_weight(found_ref, proj_ref, out_ref, rows):
    out_ref[:, 480:512] = jnp.zeros((3 * 2 * C, 32), BF16)
    sums = jnp.zeros((1, 64), F32)
    embedded = []
    for shard in range(8):
        part = jnp.zeros((1, HALF), F32)
        for x in range(4):
            j = 4 * shard + x
            found = found_ref[j].astype(F32)
            size = 12 if x < 3 else 9
            for d in range(4):
                at = 360 * d + 45 * shard + 12 * x
                rows[at : at + size, :] = found[12 * d : 12 * d + size]
            for term in range(3):
                sums = sums + found[48:49, 64 * term : 64 * (term + 1)]
                part = part + found[49:50, HALF * term : HALF * (term + 1)]
        embedded.append(part)
    values = jnp.concatenate(embedded, axis=1)
    values = values / (1.0 + jnp.exp(-values))
    proj = proj_ref[rows_at(lax.axis_index("core") * HALF, HALF), :].astype(F32)
    shift = jnp.sum(proj * values, axis=1, keepdims=True)
    shift = jnp.concatenate([jnp.broadcast_to(shift, (HALF, 128)), jnp.zeros((WIDE - HALF, 128), F32)], axis=0)
    shift = shift.T[0:1, 0:HALF]
    for q in range(4):
        row = 1440 * q
        while row < 1440 * (q + 1):
            tap, channel = divmod(row, 2 * C)
            size = min(1440 * (q + 1) - row, 2 * C - channel)
            a, b = divmod(tap, 3)
            k = row - 1440 * q
            piece = rows[k : k + size, 160 * q : 160 * (q + 1)].astype(BF16)
            place_merged(out_ref, a * 2 * C + channel, size, b, piece)
            row += size
    return sums, shift


def share_kernel(middle_ref, skip_ref, out_ref):
    core = lax.axis_index("core")
    middle = middle_ref[rows_at(core * HALF, HALF), :].astype(F32).T
    wide = skip_ref[...].astype(F32)
    skip = jnp.where(core == 0, wide[:, 0:HALF], wide[:, HALF:C])
    whole = jnp.concatenate([middle, skip, jnp.zeros((16, HALF), F32)], axis=0)
    parts = [whole[224 * q : 224 * (q + 1)] for q in range(4)]
    out_ref[...] = jnp.concatenate(parts, axis=1).astype(BF16)


def middle_weight(found_ref, out_ref, skip_ref):
    out_ref[:, 480:512] = jnp.zeros((3 * LANES, 32), BF16)

    def pieces(x, row, size):
        while size:
            q, i = divmod(row, 224)
            some = min(size, 224 - i)
            yield some, found_ref[x, i : i + some, 160 * q : 160 * (q + 1)]
            row, size = row + some, size - some

    for a in range(3):
        out_ref[a * LANES + C : (a + 1) * LANES, :] = jnp.zeros((LANES - C, MERGED), BF16)
    for tap in range(9):
        a, b = divmod(tap, 3)
        at = a * LANES
        for part in range(4):
            x, i = divmod(tap * C + part * 80, 720)
            for size, piece in pieces(x, i, 80):
                place_merged(out_ref, at, size, b, piece)
                at += size
    at = 0
    for x in range(4):
        for size, piece in pieces(x, 720, HALF):
            skip_ref[at : at + size, :] = piece
            at += size


def shifted(x, axis, step):
    count = lax.axis_size(axis)
    return lax.ppermute(x, axis, [(i, i + step) for i in range(count) if 0 <= i + step < count])


def summed(sums, kept):
    near = lax.all_to_all(sums, PLANE, 0, 0, tiled=True)
    near, kept = lax.optimization_barrier((near, kept))
    near = call(plane_sums_kernel, sds((lax.axis_size(DEPTH), 1, 128), F32), [VMEM])(near)
    return lax.all_to_all(near, DEPTH, 0, 0, tiled=True), kept


def shards(
    latent, deep, timestep, in_weight, front_weight, middle_weight, skip_weight, out_weight,
    time_weight, time_second, time_proj, input_gain, middle_gain, output_gain,
):
    core, x, y = lax.axis_index("core"), lax.axis_index("x"), lax.axis_index("y")
    depths = lax.axis_size(DEPTH)

    above, below = shifted(latent, ROWS, 1), shifted(latent, ROWS, -1)
    quarter = lax.dynamic_slice_in_dim(jnp.pad(front_weight, ((0, 3), (0, 0))), 12 * x, 12, 0)
    cells, first, last, wpad = call(
        pack_kernel,
        (sds((WIDE, LANES), BF16), sds((GAP, LANES), BF16), sds((GAP, LANES), BF16), sds((LANES, LANES), BF16)),
        [VMEM] * 5,
        [pltpu.VMEM((LANES, WIDE), F32), pltpu.VMEM((LANES, LANES), F32)],
    )(deep.reshape(C, WIDE), above.reshape(4, WIDE), latent.reshape(4, WIDE), below.reshape(4, WIDE), in_weight)
    from_right, from_left = shifted(first, "x", -1), shifted(last, "x", 1)
    row, sent = call(stats_kernel, (sds((SEG, LANES), BF16), sds((depths, 16, C), BF16)), [VMEM] * 5)(
        cells, from_left, from_right, wpad, quarter
    )

    row, skip_here = lax.optimization_barrier((row, skip_weight))
    packed = call(share_kernel, sds((224, 4 * HALF), BF16), [VMEM] * 2)(middle_weight.T, skip_here)

    count = lax.axis_size(ROWS)
    crossed = [(i, i + 3) if i % 2 else (i, i - 3) for i in range(count)]
    crossed = [(i, j) for i, j in crossed if 0 <= j < count]
    before, after, across = shifted(row, ROWS, 2), shifted(row, ROWS, -2), lax.ppermute(row, ROWS, crossed)

    half_width = time_weight.shape[0] // 2
    ratios = jnp.exp(-math.log(10000.0) * jnp.arange(half_width, dtype=F32) / half_width)
    angles = timestep[0].astype(F32) * ratios
    features = jnp.concatenate([jnp.cos(angles), jnp.sin(angles)])
    depth_here = time_second.shape[0]
    weight_here = lax.dynamic_slice_in_dim(time_weight, x * depth_here, depth_here, 1)
    hidden = jax.nn.silu(jnp.dot(features, weight_here.astype(F32), precision=HIGH))
    columns = lax.dynamic_slice_in_dim(time_second, (2 * y + core) * HALF, HALF, 1)
    part = jnp.dot(hidden, columns.astype(F32), precision=HIGH)

    got = lax.all_to_all(sent, DEPTH, 0, 0, tiled=True)
    scratch = [
        pltpu.VMEM((2, 48, 4 * HALF), F32),
        pltpu.VMEM((2, 56, 4 * HALF), BF16),
        pltpu.SemaphoreType.DMA((32,)),
    ]
    sent = call(plane_kernel, sds((32, 56, 4 * HALF), BF16), [VMEM] * 2, scratch, 52, ANY)(got, part[None])
    around = jnp.stack([before, row, after, across])
    sent, around = lax.optimization_barrier((sent, around))
    found = lax.all_to_all(sent, PLANE, 0, 0, tiled=True)
    swap = [(0, 1), (1, 0)]
    joined = call(
        join_kernel, sds((A_LEN, 2 * C), BF16), [VMEM] * 3, [pltpu.VMEM((A_LEN + 2 * GAP, LANES), BF16)], 60
    )(around, lax.ppermute(around, "core", swap), wpad)
    packed, found, joined = lax.optimization_barrier((packed, found, joined))
    middle_found = lax.all_gather(packed, "x", axis=0)
    own_scratch = [
        pltpu.VMEM((B_LEN, 2 * C), BF16),
        pltpu.VMEM((32, 56, 4 * HALF), BF16),
        pltpu.VMEM((1440, 4 * HALF), F32),
        pltpu.VMEM((3 * 2 * C, MERGED), BF16),
        pltpu.VMEM((B_LEN, 2 * C), BF16),
        pltpu.VMEM((2 * SEG + 3 * GAP, MERGED), F32),
        pltpu.SemaphoreType.DMA((3,)),
    ]
    front, known, sums = call(
        first_own_kernel,
        (sds((3 * 2 * C, MERGED), BF16), sds((1, 384), F32), sds((32, 1, 128), F32)),
        [ANY, ANY, VMEM, VMEM],
        own_scratch,
        52,
        (ANY, VMEM, VMEM),
    )(joined, found, time_proj.T, input_gain[None])
    hidden_own = call(
        first_kernel,
        sds((H_LEN, SWAP), F32),
        [ANY, ANY, VMEM, VMEM],
        [
            pltpu.VMEM((A_LEN, 2 * C), BF16),
            pltpu.VMEM((3 * 2 * C, MERGED), BF16),
            pltpu.VMEM((A_LEN, 2 * C), BF16),
            pltpu.VMEM((H_LEN + 2 * GAP, MERGED), F32),
            pltpu.SemaphoreType.DMA((3,)),
        ],
        52,
    )(joined, front, known, input_gain[None])
    totals, hidden_own = summed(sums, hidden_own)
    hidden_other = lax.ppermute(hidden_own, "core", swap)

    gain_two = middle_gain.reshape(2, HALF)
    middle, shortcut = call(
        middle_weight_kernel,
        (sds((3 * LANES, MERGED), BF16), sds((2 * C, HALF), BF16)),
        [ANY],
        [
            pltpu.VMEM((4, 224, 4 * HALF), BF16),
            pltpu.VMEM((3 * LANES, MERGED), BF16),
            pltpu.VMEM((2 * C, HALF), BF16),
            pltpu.SemaphoreType.DMA((3,)),
        ],
        52,
        (ANY, ANY),
    )(middle_found.reshape(4, 224, 4 * HALF))
    sums = call(
        second_own_kernel,
        sds((32, 1, 128), F32),
        [ANY, ANY, VMEM, VMEM, ANY, ANY, ANY],
        [
            pltpu.VMEM((B_LEN, SWAP), F32),
            pltpu.VMEM((B_LEN, SWAP), F32),
            pltpu.VMEM((2 * SEG, 2 * C), BF16),
            pltpu.VMEM((3 * LANES, MERGED), BF16),
            pltpu.VMEM((2 * C, HALF), BF16),
            pltpu.VMEM((B_LEN, LANES), BF16),
            pltpu.VMEM((2 * SEG + 3 * GAP, MERGED), F32),
            pltpu.SemaphoreType.DMA((5,)),
        ],
        52,
    )(hidden_own, hidden_other, totals, gain_two, middle, shortcut, joined)
    block_own = call(
        second_kernel,
        sds((B_LEN, SWAP), F32),
        [ANY, ANY, VMEM, VMEM, ANY, VMEM, ANY],
        [
            pltpu.VMEM((H_LEN, SWAP), F32),
            pltpu.VMEM((H_LEN, SWAP), F32),
            pltpu.VMEM((B_LEN, 2 * C), BF16),
            pltpu.VMEM((3 * LANES, MERGED), BF16),
            pltpu.VMEM((H_LEN, LANES), BF16),
            pltpu.VMEM((B_LEN + 2 * GAP, MERGED), F32),
            pltpu.SemaphoreType.DMA((4,)),
        ],
        52,
    )(hidden_own, hidden_other, totals, gain_two, middle, shortcut, joined)
    totals, block_own = summed(sums, block_own)
    block_other = lax.ppermute(block_own, "core", swap)

    wout = out_weight.reshape(9, 2, HALF, 4).transpose(1, 2, 0, 3)
    wout = jnp.pad(jnp.pad(wout, ((0, 0), (0, 0), (0, 0), (0, 4))).reshape(2, HALF, 72), ((0, 0), (0, 0), (0, 56)))
    scratch = [
        pltpu.VMEM((3 * SEG + GAP, SWAP), F32),
        pltpu.VMEM((3 * SEG + GAP, SWAP), F32),
        pltpu.SemaphoreType.DMA((2,)),
    ]
    return call(third_kernel, sds((4, 1, WIDE), F32), [ANY, ANY, VMEM, VMEM, VMEM], scratch, 30)(
        block_own, block_other, totals, output_gain.reshape(2, HALF), wout
    )


def solution(mesh):
    finer = Mesh(
        mesh.devices.reshape(8, 2, 4, 2, mesh.shape["cols"]), ("zp", "zl", "y", "core", "x")
    )
    in_specs = (
        P(None, ROWS, "x"),
        P(None, ROWS, "x"),
        P(),
        P(),
        P(ROWS, None),
        P("x", None),
        P("x", None),
        P(),
        P(),
        P("x", None),
        P(),
        P(),
        P(),
        P(),
    )
    return jax.shard_map(
        shards, mesh=finer, in_specs=in_specs, out_specs=P(None, ROWS, "x"), check_vma=False
    )
```

```python
import math

import jax
import jax.numpy as jnp
from jax import lax
from jax.experimental import pallas as pl
from jax.experimental.pallas import tpu as pltpu
from jax.sharding import Mesh
from jax.sharding import PartitionSpec as P

ROWS = ("zp", "zl", "y", "core")
DEPTH = ("zp", "zl")
PLANE = ("y", "core", "x")
EPS = 1e-05
F32 = jnp.float32
BF16 = jnp.bfloat16
HIGH = lax.Precision.HIGHEST

C = 320
HALF = 160
WIDE = 256
GAP = 16
SEG = WIDE + GAP
IN_ROWS = 8
MID_ROWS = 6
OUT_ROWS = 4
A_LEN = IN_ROWS * SEG + GAP
H_LEN = MID_ROWS * SEG + GAP
B_LEN = OUT_ROWS * SEG + GAP
MERGED = 512
LANES = 384
SWAP = 256
VMEM = pl.BlockSpec(memory_space=pltpu.VMEM)
ANY = pl.BlockSpec(memory_space=pltpu.HBM)


def call(kernel, out_shape, in_specs, scratch=(), limit=16, out_spec=VMEM):
    return pl.pallas_call(
        kernel,
        out_shape=out_shape,
        in_specs=in_specs,
        out_specs=out_spec if isinstance(out_spec, tuple) else jax.tree.map(lambda _: out_spec, out_shape),
        scratch_shapes=list(scratch),
        compiler_params=pltpu.CompilerParams(vmem_limit_bytes=limit * 1024 * 1024),
    )


def sds(shape, dtype):
    return jax.ShapeDtypeStruct(shape, dtype)


def rows_at(start, size):
    return pl.ds(pl.multiple_of(start, 16), size)


def place():
    return 2 * lax.axis_index(("zp", "zl", "y")), lax.axis_index("x") * WIDE, lax.axis_index("core")


def same_group(n, m, size_n, size_m):
    i = lax.broadcasted_iota(jnp.int32, (n, m), 0)
    j = lax.broadcasted_iota(jnp.int32, (n, m), 1)
    return ((i // size_n) == (j // size_m)).astype(F32)


def exact_dot(a, b):
    return jnp.dot(a, b, preferred_element_type=F32, precision=HIGH)


def tap_dot(a, b):
    return jnp.dot(a, b, preferred_element_type=F32)


def silu_half(h):
    return h + h * jnp.tanh(h)


def pack_kernel(deep_ref, prev_ref, here_ref, next_ref, weight_ref, out_ref, first_ref, last_ref, wpad_ref, tall, wide):
    tall[0:C, :] = deep_ref[...].astype(F32)
    tall[C:LANES, :] = jnp.zeros((LANES - C, WIDE), F32)
    for i, ref in enumerate((prev_ref, here_ref, next_ref)):
        tall[C + 4 * i : C + 4 * i + 4, :] = ref[...].astype(F32)
    out = tall[...].T.astype(BF16)
    out_ref[...] = out
    first_ref[...] = out[0:GAP]
    last_ref[...] = out[WIDE - GAP : WIDE]
    wide[...] = jnp.zeros((LANES, LANES), F32)
    weight = weight_ref[...].astype(F32)
    for tap in range(9):
        a, b = divmod(tap, 3)
        at = 128 * b + 64 + 4 * a
        wide[at : at + 4, 64:LANES] = weight[4 * tap : 4 * tap + 4]
    wpad_ref[...] = wide[...].astype(BF16)


def skip_of(tail, wpad_ref, lo, hi):
    n = tail.shape[0]
    left = pltpu.roll(tail, 1, 0)[lo:hi].astype(BF16)
    right = pltpu.roll(tail, n - 1, 0)[lo:hi].astype(BF16)
    mid = tail[lo:hi].astype(BF16)
    stacked = jnp.concatenate([left, mid, right], axis=1)
    return tap_dot(stacked, wpad_ref[...]).astype(BF16).astype(F32)


def join(cells, skip):
    lane = lax.broadcasted_iota(jnp.int32, (cells.shape[0], 128), 1)
    mixed = jnp.where(lane < 64, cells[:, 256:384], skip[:, 0:128])
    return jnp.concatenate([cells[:, 0:256], mixed, skip[:, 128:384]], axis=1)


def three_terms(values):
    high = values.astype(BF16).astype(F32)
    middle = (values - high).astype(BF16).astype(F32)
    return high, middle, values - high - middle


def stats_kernel(cells_ref, left_ref, right_ref, wpad_ref, quarter_ref, row_ref, sent_ref):
    sub = lax.broadcasted_iota(jnp.int32, (GAP, LANES), 0)
    gap = jnp.where(sub < 8, right_ref[...].astype(F32), left_ref[...].astype(F32))
    cells = jnp.concatenate([cells_ref[...].astype(F32), gap], axis=0)
    row_ref[...] = cells.astype(BF16)
    skip = skip_of(cells[:, 256:384], wpad_ref, 0, WIDE)
    joined = join(cells[0:WIDE], skip)
    sums = jnp.sum(joined, axis=0, keepdims=True)
    squares = jnp.sum(joined * joined, axis=0, keepdims=True)
    both = jnp.concatenate([sums, squares, jnp.zeros((6, 2 * C), F32)], axis=0)
    grouped = exact_dot(both, same_group(2 * C, 32, 20, 1))
    terms = three_terms(jnp.concatenate([grouped[0:1], grouped[1:2]], axis=1))
    line = jnp.concatenate([*terms, jnp.zeros((1, C - 192), F32)], axis=1)
    message = jnp.concatenate([quarter_ref[...].astype(F32), line, jnp.zeros((3, C), F32)], axis=0).astype(BF16)
    for z in range(sent_ref.shape[0]):
        sent_ref[z] = message


def plane_kernel(got_ref, part_ref, sent_hbm, rows, blocks, sems):
    total = jnp.zeros((1, 64), F32)
    for z in range(16):
        got = got_ref[z].astype(F32)
        q, d = divmod(z, 4)
        for half in (0, 1):
            rows[half, 12 * d : 12 * d + 12, 160 * q : 160 * (q + 1)] = got[0:12, 160 * half : 160 * (half + 1)]
        total = total + got[12:13, 0:64] + got[12:13, 64:128] + got[12:13, 128:192]
    first = jnp.concatenate([*three_terms(total), jnp.zeros((1, 4 * HALF - 192), F32)], axis=1)
    second = jnp.concatenate([*three_terms(part_ref[...]), jnp.zeros((1, HALF), F32)], axis=1)
    tail = jnp.concatenate([first, second, jnp.zeros((6, 4 * HALF), F32)], axis=0).astype(BF16)
    copies = []
    for half in (0, 1):
        blocks[half, 0:48, :] = rows[half].astype(BF16)
        blocks[half, 48:56, :] = tail
        for i in range(16):
            goal = 8 * (i // 4) + 4 * half + i % 4
            copies.append(pltpu.make_async_copy(blocks.at[half], sent_hbm.at[goal], sems.at[goal]))
            copies[-1].start()
    for copy in copies:
        copy.wait()


def keep_mask(r, first_row, first_col):
    i = lax.broadcasted_iota(jnp.int32, (SEG, 1), 0)
    here = first_row + r
    row = jnp.where(i < 8, here - 1, here)
    col = first_col + jnp.where(i < 8, i + WIDE, i - GAP)
    good = (row >= 0) & (row < 128) & (col >= 0) & (col < 1024)
    return good.astype(F32)


def shift_add(merged_ref, start, size):
    back = merged_ref[pl.ds(start - 1, size), :]
    mid = merged_ref[pl.ds(start, size), :]
    ahead = merged_ref[pl.ds(start + 1, size), :]
    low = back[:, 0:128] + mid[:, 128:256] + ahead[:, 256:384]
    high = (
        back[:, 384:512]
        + pltpu.roll(mid[:, 384:512], 96, 1)
        + pltpu.roll(ahead[:, 384:512], 64, 1)
    )
    return jnp.concatenate([low, high[:, 0:32]], axis=1)


def join_kernel(own_ref, other_ref, wpad_ref, joined_ref, raw):
    order = ((0, 3), (0, 0), (1, 0), (0, 1), (1, 1), (0, 2), (1, 2), (1, 3))
    sub = lax.broadcasted_iota(jnp.int32, (GAP, LANES), 0)
    zeros = jnp.zeros((GAP, LANES), BF16)
    raw[0:GAP, :] = zeros
    raw[GAP + A_LEN : GAP + A_LEN + GAP, :] = zeros

    def lay_out(sources):
        for r in range(IN_ROWS + 1):
            before, after = None, None
            if r:
                which, at = order[r - 1]
                before = sources[which][at, WIDE:SEG, :].astype(F32)
            if r < IN_ROWS:
                which, at = order[r]
                after = sources[which][at, WIDE:SEG, :].astype(F32)
                raw[2 * GAP + r * SEG : GAP + (r + 1) * SEG, :] = sources[which][at, 0:WIDE, :]
            before = after if before is None else before
            after = before if after is None else after
            raw[GAP + r * SEG : 2 * GAP + r * SEG, :] = jnp.where(sub < 8, before, after).astype(BF16)

    core = lax.axis_index("core")

    @pl.when(core == 0)
    def _():
        lay_out((own_ref, other_ref))

    @pl.when(core == 1)
    def _():
        lay_out((other_ref, own_ref))

    def one(r, size):
        base = r * SEG
        tail = raw[rows_at(base, size + 2 * GAP), 256:384].astype(F32)
        skip = skip_of(tail, wpad_ref, GAP, GAP + size)
        joined = join(raw[rows_at(base + GAP, size), :].astype(F32), skip)
        joined_ref[rows_at(base, size), :] = joined.astype(BF16)

    def build(r, carry):
        one(r, SEG)
        return carry

    lax.fori_loop(0, IN_ROWS, build, 0)
    one(IN_ROWS, GAP)


def first_affine(sums, gain_ref):
    totals = sums / (20.0 * 131072.0)
    mean = totals[:, 0:32]
    var = totals[:, 32:64] - mean * mean
    pair = jnp.concatenate([lax.rsqrt(var + EPS), mean, jnp.zeros((6, 32), F32)], axis=0)
    spread = exact_dot(pair, same_group(32, 2 * C, 1, 20))
    scale = spread[0:1] * gain_ref[...] * 0.5
    return scale, -spread[1:2] * scale


def first_build(joined_ref, act, at, size, mask, scale, offset):
    where = slice(at, at + size)
    for lane in range(0, 2 * C, 128):
        part = slice(lane, lane + 128)
        values = joined_ref[where, part].astype(F32) * scale[:, part] + offset[:, part]
        act[where, part] = (silu_half(values) * mask[0:size]).astype(BF16)


def merged_conv(act, wm_ref, merged, start, size):
    taps = [act[start + a * SEG : start + a * SEG + size, :] for a in range(3)]
    merged[start + GAP : start + GAP + size, :] = tap_dot(jnp.concatenate(taps, axis=1), wm_ref[...])


def clear_ends(merged):
    size = merged.shape[0]
    merged[0:GAP, :] = jnp.zeros((GAP, MERGED), F32)
    merged[size - GAP : size, :] = jnp.zeros((GAP, MERGED), F32)


def first_own_kernel(
    joined_hbm, found_hbm, proj_ref, gain_ref,
    wm_hbm, known_ref, sum_ref,
    joined_ref, found_ref, rows, wm_ref, act, merged, sems,
):
    copies = [
        pltpu.make_async_copy(found_hbm, found_ref, sems.at[0]),
        pltpu.make_async_copy(joined_hbm.at[2 * SEG : 2 * SEG + B_LEN], joined_ref, sems.at[1]),
        pltpu.make_async_copy(wm_ref, wm_hbm, sems.at[2]),
    ]
    copies[0].start()
    copies[1].start()
    copies[0].wait()
    chip_row, first_col, _ = place()
    totals, shift = front_weight(found_ref, proj_ref, wm_ref, rows)
    copies[2].start()
    known_ref[...] = jnp.concatenate([totals, jnp.zeros((1, 64), F32), shift, jnp.zeros((1, 96), F32)], axis=1)
    scale, offset = first_affine(totals, gain_ref)
    clear_ends(merged)
    copies[1].wait()
    for r in range(5):
        mask = keep_mask(r + 2, chip_row - 3, first_col)
        first_build(joined_ref, act, r * SEG, SEG if r < 4 else GAP, mask, scale, offset)
    merged_conv(act, wm_ref, merged, 0, 2 * SEG + GAP)
    sums = jnp.zeros((1, HALF), F32)
    squares = jnp.zeros((1, HALF), F32)
    for r in range(2):
        values = shift_add(merged, 2 * GAP + r * SEG, WIDE) + shift
        sums = sums + jnp.sum(values, axis=0, keepdims=True)
        squares = squares + jnp.sum(values * values, axis=0, keepdims=True)
    send_sums(sums, squares, sum_ref)
    copies[2].wait()


def first_kernel(
    joined_hbm, wm_hbm, known_ref, gain_ref,
    hidden_ref,
    joined_ref, wm_ref, act, merged, sems,
):
    copies = []
    for i, part in enumerate((slice(0, 4 * SEG), slice(4 * SEG, A_LEN))):
        copies.append(pltpu.make_async_copy(joined_hbm.at[part], joined_ref.at[part], sems.at[i]))
    copies.append(pltpu.make_async_copy(wm_hbm, wm_ref, sems.at[2]))
    for copy in copies:
        copy.start()
    chip_row, first_col, _ = place()
    scale, offset = first_affine(known_ref[:, 0:64], gain_ref)
    shift = known_ref[:, 128 : 128 + HALF]

    def build(r):
        mask = keep_mask(r, chip_row - 3, first_col)
        first_build(joined_ref, act, r * SEG, SEG if r < IN_ROWS else GAP, mask, scale, offset)

    clear_ends(merged)
    copies[0].wait()
    for r in range(4):
        build(r)
    copies[2].wait()
    merged_conv(act, wm_ref, merged, 0, 2 * SEG)
    copies[1].wait()
    build(4)
    build(5)
    merged_conv(act, wm_ref, merged, 2 * SEG, 2 * SEG)
    for r in range(6, 9):
        build(r)
    merged_conv(act, wm_ref, merged, 4 * SEG, 2 * SEG + GAP)
    for r in range(MID_ROWS + 1):
        size = SEG if r < MID_ROWS else GAP
        hidden_ref[r * SEG : r * SEG + size, 0:HALF] = shift_add(merged, GAP + r * SEG, size) + shift
    hidden_ref[:, HALF:SWAP] = jnp.zeros((H_LEN, SWAP - HALF), F32)


def send_sums(sums, squares, sent_ref):
    both = jnp.concatenate([sums, squares, jnp.zeros((6, HALF), F32)], axis=0)
    grouped = exact_dot(both, same_group(HALF, 16, 10, 1))
    line = jnp.concatenate([grouped[0:1], grouped[1:2], jnp.zeros((1, 96), F32)], axis=1)
    for i in range(32):
        sent_ref[i] = line


def plane_sums_kernel(got_ref, sent_ref):
    cores = [jnp.zeros((1, 32), F32), jnp.zeros((1, 32), F32)]
    for i in range(32):
        half = (i // 4) % 2
        cores[half] = cores[half] + got_ref[i][:, 0:32]
    line = jnp.concatenate([*cores, jnp.zeros((1, 64), F32)], axis=1)
    for i in range(sent_ref.shape[0]):
        sent_ref[i] = line


def affine(stat_ref, gain_ref):
    both = stat_ref[0]
    for i in range(1, stat_ref.shape[0]):
        both = both + stat_ref[i]
    found = []
    for which in (0, 1):
        at = 32 * which
        padded = jnp.concatenate([both[:, at : at + 16], both[:, at + 16 : at + 32], jnp.zeros((6, 16), F32)], axis=0)
        totals = exact_dot(padded, same_group(16, HALF, 1, 10)) / (10.0 * 131072.0)
        mean = totals[0:1]
        scale = lax.rsqrt(totals[1:2] - mean * mean + EPS) * gain_ref[which : which + 1] * 0.5
        found.append((scale, -mean * scale))
    return found


def second_build(own_ref, other_ref, act, at, size, mask, affines):
    where = slice(at, at + size)
    first = lax.axis_index("core") == 0
    own, other = own_ref[where, 0:HALF], other_ref[where, 0:HALF]
    parts = []
    for which, (scale, offset) in enumerate(affines):
        values = jnp.where(first, own, other) if which == 0 else jnp.where(first, other, own)
        parts.append(silu_half(values * scale + offset) * mask[0:size])
    parts.append(jnp.zeros((size, LANES - C), F32))
    act[where, :] = jnp.concatenate(parts, axis=1).astype(BF16)


def middle_weight_kernel(found_hbm, wm_hbm, skip_hbm, found_ref, wm_ref, skip_ref, sems):
    copy = pltpu.make_async_copy(found_hbm, found_ref, sems.at[0])
    copy.start()
    copy.wait()
    middle_weight(found_ref, wm_ref, skip_ref)
    back = [
        pltpu.make_async_copy(wm_ref, wm_hbm, sems.at[1]),
        pltpu.make_async_copy(skip_ref, skip_hbm, sems.at[2]),
    ]
    for copy in back:
        copy.start()
    for copy in back:
        copy.wait()


def second_own_kernel(
    own_hbm, other_hbm, stat_ref, gain_ref, wm_hbm, skip_hbm, joined_hbm,
    sum_ref,
    own_ref, other_ref, joined_ref, wm_ref, skip_ref, act, merged, sems,
):
    part = slice(SEG, SEG + B_LEN)
    copies = [
        pltpu.make_async_copy(own_hbm.at[part], own_ref, sems.at[0]),
        pltpu.make_async_copy(other_hbm.at[part], other_ref, sems.at[1]),
        pltpu.make_async_copy(wm_hbm, wm_ref, sems.at[2]),
        pltpu.make_async_copy(joined_hbm.at[3 * SEG : 5 * SEG], joined_ref, sems.at[3]),
        pltpu.make_async_copy(skip_hbm, skip_ref, sems.at[4]),
    ]
    for copy in copies:
        copy.start()
    chip_row, first_col, _ = place()
    affines = affine(stat_ref, gain_ref)
    clear_ends(merged)
    copies[0].wait()
    copies[1].wait()
    for r in range(5):
        mask = keep_mask(r + 1, chip_row - 2, first_col)
        second_build(own_ref, other_ref, act, r * SEG, SEG if r < 4 else GAP, mask, affines)
    copies[2].wait()
    merged_conv(act, wm_ref, merged, 0, 2 * SEG + GAP)
    copies[3].wait()
    copies[4].wait()
    sums = jnp.zeros((1, HALF), F32)
    squares = jnp.zeros((1, HALF), F32)
    for r in range(2):
        at = r * SEG + GAP
        values = shift_add(merged, GAP + at, WIDE) + tap_dot(joined_ref[at : at + WIDE, :], skip_ref[...])
        sums = sums + jnp.sum(values, axis=0, keepdims=True)
        squares = squares + jnp.sum(values * values, axis=0, keepdims=True)
    send_sums(sums, squares, sum_ref)


def second_kernel(
    own_hbm, other_hbm, stat_ref, gain_ref, wm_hbm, skip_ref, joined_hbm,
    block_ref,
    own_ref, other_ref, joined_ref, wm_ref, act, merged, sems,
):
    copies = [
        pltpu.make_async_copy(own_hbm, own_ref, sems.at[0]),
        pltpu.make_async_copy(other_hbm, other_ref, sems.at[1]),
        pltpu.make_async_copy(wm_hbm, wm_ref, sems.at[2]),
        pltpu.make_async_copy(joined_hbm.at[2 * SEG : 2 * SEG + B_LEN], joined_ref, sems.at[3]),
    ]
    for copy in copies:
        copy.start()
    chip_row, first_col, _ = place()
    affines = affine(stat_ref, gain_ref)
    clear_ends(merged)
    copies[0].wait()
    copies[1].wait()

    def build(r):
        mask = keep_mask(r, chip_row - 2, first_col)
        second_build(own_ref, other_ref, act, r * SEG, SEG if r < MID_ROWS else GAP, mask, affines)

    for r in range(4):
        build(r)
    copies[2].wait()
    merged_conv(act, wm_ref, merged, 0, 2 * SEG)
    for r in range(4, 7):
        build(r)
    merged_conv(act, wm_ref, merged, 2 * SEG, 2 * SEG + GAP)
    copies[3].wait()
    for r in range(OUT_ROWS + 1):
        size = SEG if r < OUT_ROWS else GAP
        where = slice(r * SEG, r * SEG + size)
        block_ref[where, 0:HALF] = shift_add(merged, GAP + r * SEG, size) + tap_dot(
            joined_ref[where, :], skip_ref[...]
        )
    block_ref[:, HALF:SWAP] = jnp.zeros((B_LEN, SWAP - HALF), F32)


def third_kernel(own_hbm, other_hbm, stat_ref, gain_ref, wout_ref, noise_ref, own_ref, other_ref, sems):
    chip_row, first_col, core = place()
    needed = pl.ds(pl.multiple_of(core * SEG, 16), 3 * SEG + GAP)
    copies = [
        pltpu.make_async_copy(own_hbm.at[needed], own_ref, sems.at[0]),
        pltpu.make_async_copy(other_hbm.at[needed], other_ref, sems.at[1]),
    ]
    for copy in copies:
        copy.start()
    first_row = chip_row - 1 + core
    affines = affine(stat_ref, gain_ref)
    first = core == 0
    for copy in copies:
        copy.wait()
    parts = []
    for r in range(4):
        size = SEG if r < 3 else GAP
        mask = keep_mask(r, first_row, first_col)[0:size]
        where = slice(r * SEG, r * SEG + size)
        total = None
        own, other = own_ref[where, 0:HALF], other_ref[where, 0:HALF]
        for which, (scale, offset) in enumerate(affines):
            values = jnp.where(first, own, other) if which == 0 else jnp.where(first, other, own)
            act = (silu_half(values * scale + offset) * mask).astype(BF16)
            part = tap_dot(act, wout_ref[which])
            total = part if total is None else total + part
        parts.append(total)
    parts.append(jnp.zeros((896 - 3 * SEG - GAP, 128), F32))
    turned = jnp.concatenate(parts, axis=0).T
    noise = None
    for a in range(3):
        for b in range(3):
            tap = 3 * a + b
            at = a * SEG + GAP + b - 1
            piece = turned[8 * tap : 8 * tap + 8, at : at + WIDE]
            noise = piece if noise is None else noise + piece
    for o in range(4):
        noise_ref[o] = noise[o : o + 1]


def place_merged(out_ref, at, size, b, piece):
    out_ref[at : at + size, 128 * b : 128 * (b + 1)] = piece[:, 0:128]
    out_ref[at : at + size, 384 + 32 * b : 384 + 32 * (b + 1)] = piece[:, 128:160]


def front_weight(found_ref, proj_ref, out_ref, rows):
    out_ref[:, 480:512] = jnp.zeros((3 * 2 * C, 32), BF16)
    sums = jnp.zeros((1, 64), F32)
    embedded = []
    for shard in range(8):
        part = jnp.zeros((1, HALF), F32)
        for x in range(4):
            j = 4 * shard + x
            found = found_ref[j].astype(F32)
            size = 12 if x < 3 else 9
            for d in range(4):
                at = 360 * d + 45 * shard + 12 * x
                rows[at : at + size, :] = found[12 * d : 12 * d + size]
            for term in range(3):
                sums = sums + found[48:49, 64 * term : 64 * (term + 1)]
                part = part + found[49:50, HALF * term : HALF * (term + 1)]
        embedded.append(part)
    values = jnp.concatenate(embedded, axis=1)
    values = values / (1.0 + jnp.exp(-values))
    proj = proj_ref[rows_at(lax.axis_index("core") * HALF, HALF), :].astype(F32)
    shift = jnp.sum(proj * values, axis=1, keepdims=True)
    shift = jnp.concatenate([jnp.broadcast_to(shift, (HALF, 128)), jnp.zeros((WIDE - HALF, 128), F32)], axis=0)
    shift = shift.T[0:1, 0:HALF]
    for q in range(4):
        row = 1440 * q
        while row < 1440 * (q + 1):
            tap, channel = divmod(row, 2 * C)
            size = min(1440 * (q + 1) - row, 2 * C - channel)
            a, b = divmod(tap, 3)
            k = row - 1440 * q
            piece = rows[k : k + size, 160 * q : 160 * (q + 1)].astype(BF16)
            place_merged(out_ref, a * 2 * C + channel, size, b, piece)
            row += size
    return sums, shift


def share_kernel(middle_ref, skip_ref, out_ref):
    core = lax.axis_index("core")
    middle = middle_ref[rows_at(core * HALF, HALF), :].astype(F32).T
    wide = skip_ref[...].astype(F32)
    skip = jnp.where(core == 0, wide[:, 0:HALF], wide[:, HALF:C])
    whole = jnp.concatenate([middle, skip, jnp.zeros((16, HALF), F32)], axis=0)
    parts = [whole[224 * q : 224 * (q + 1)] for q in range(4)]
    out_ref[...] = jnp.concatenate(parts, axis=1).astype(BF16)


def middle_weight(found_ref, out_ref, skip_ref):
    out_ref[:, 480:512] = jnp.zeros((3 * LANES, 32), BF16)

    def pieces(x, row, size):
        while size:
            q, i = divmod(row, 224)
            some = min(size, 224 - i)
            yield some, found_ref[x, i : i + some, 160 * q : 160 * (q + 1)]
            row, size = row + some, size - some

    for a in range(3):
        out_ref[a * LANES + C : (a + 1) * LANES, :] = jnp.zeros((LANES - C, MERGED), BF16)
    for tap in range(9):
        a, b = divmod(tap, 3)
        at = a * LANES
        for part in range(4):
            x, i = divmod(tap * C + part * 80, 720)
            for size, piece in pieces(x, i, 80):
                place_merged(out_ref, at, size, b, piece)
                at += size
    at = 0
    for x in range(4):
        for size, piece in pieces(x, 720, HALF):
            skip_ref[at : at + size, :] = piece
            at += size


def shifted(x, axis, step):
    count = lax.axis_size(axis)
    return lax.ppermute(x, axis, [(i, i + step) for i in range(count) if 0 <= i + step < count])


def summed(sums, kept):
    near = lax.all_to_all(sums, PLANE, 0, 0, tiled=True)
    near, kept = lax.optimization_barrier((near, kept))
    near = call(plane_sums_kernel, sds((lax.axis_size(DEPTH), 1, 128), F32), [VMEM])(near)
    return lax.all_to_all(near, DEPTH, 0, 0, tiled=True), kept


def shards(
    latent, deep, timestep, in_weight, front_weight, middle_weight, skip_weight, out_weight,
    time_weight, time_second, time_proj, input_gain, middle_gain, output_gain,
):
    core, x, y = lax.axis_index("core"), lax.axis_index("x"), lax.axis_index("y")
    depths = lax.axis_size(DEPTH)

    above, below = shifted(latent, ROWS, 1), shifted(latent, ROWS, -1)
    quarter = lax.dynamic_slice_in_dim(jnp.pad(front_weight, ((0, 3), (0, 0))), 12 * x, 12, 0)
    cells, first, last, wpad = call(
        pack_kernel,
        (sds((WIDE, LANES), BF16), sds((GAP, LANES), BF16), sds((GAP, LANES), BF16), sds((LANES, LANES), BF16)),
        [VMEM] * 5,
        [pltpu.VMEM((LANES, WIDE), F32), pltpu.VMEM((LANES, LANES), F32)],
    )(deep.reshape(C, WIDE), above.reshape(4, WIDE), latent.reshape(4, WIDE), below.reshape(4, WIDE), in_weight)
    from_right, from_left = shifted(first, "x", -1), shifted(last, "x", 1)
    row, sent = call(stats_kernel, (sds((SEG, LANES), BF16), sds((depths, 16, C), BF16)), [VMEM] * 5)(
        cells, from_left, from_right, wpad, quarter
    )

    row, skip_here = lax.optimization_barrier((row, skip_weight))
    packed = call(share_kernel, sds((224, 4 * HALF), BF16), [VMEM] * 2)(middle_weight.T, skip_here)

    count = lax.axis_size(ROWS)
    crossed = [(i, i + 3) if i % 2 else (i, i - 3) for i in range(count)]
    crossed = [(i, j) for i, j in crossed if 0 <= j < count]
    before, after, across = shifted(row, ROWS, 2), shifted(row, ROWS, -2), lax.ppermute(row, ROWS, crossed)

    half_width = time_weight.shape[0] // 2
    ratios = jnp.exp(-math.log(10000.0) * jnp.arange(half_width, dtype=F32) / half_width)
    angles = timestep[0].astype(F32) * ratios
    features = jnp.concatenate([jnp.cos(angles), jnp.sin(angles)])
    depth_here = time_second.shape[0]
    weight_here = lax.dynamic_slice_in_dim(time_weight, x * depth_here, depth_here, 1)
    hidden = jax.nn.silu(jnp.dot(features, weight_here.astype(F32), precision=HIGH))
    columns = lax.dynamic_slice_in_dim(time_second, (2 * y + core) * HALF, HALF, 1)
    part = jnp.dot(hidden, columns.astype(F32), precision=HIGH)

    got = lax.all_to_all(sent, DEPTH, 0, 0, tiled=True)
    scratch = [
        pltpu.VMEM((2, 48, 4 * HALF), F32),
        pltpu.VMEM((2, 56, 4 * HALF), BF16),
        pltpu.SemaphoreType.DMA((32,)),
    ]
    sent = call(plane_kernel, sds((32, 56, 4 * HALF), BF16), [VMEM] * 2, scratch, 52, ANY)(got, part[None])
    around = jnp.stack([before, row, after, across])
    sent, around = lax.optimization_barrier((sent, around))
    found = lax.all_to_all(sent, PLANE, 0, 0, tiled=True)
    swap = [(0, 1), (1, 0)]
    joined = call(
        join_kernel, sds((A_LEN, 2 * C), BF16), [VMEM] * 3, [pltpu.VMEM((A_LEN + 2 * GAP, LANES), BF16)], 60
    )(around, lax.ppermute(around, "core", swap), wpad)
    packed, found, joined = lax.optimization_barrier((packed, found, joined))
    middle_found = lax.all_gather(packed, "x", axis=0)
    own_scratch = [
        pltpu.VMEM((B_LEN, 2 * C), BF16),
        pltpu.VMEM((32, 56, 4 * HALF), BF16),
        pltpu.VMEM((1440, 4 * HALF), F32),
        pltpu.VMEM((3 * 2 * C, MERGED), BF16),
        pltpu.VMEM((B_LEN, 2 * C), BF16),
        pltpu.VMEM((2 * SEG + 3 * GAP, MERGED), F32),
        pltpu.SemaphoreType.DMA((3,)),
    ]
    front, known, sums = call(
        first_own_kernel,
        (sds((3 * 2 * C, MERGED), BF16), sds((1, 384), F32), sds((32, 1, 128), F32)),
        [ANY, ANY, VMEM, VMEM],
        own_scratch,
        52,
        (ANY, VMEM, VMEM),
    )(joined, found, time_proj.T, input_gain[None])
    hidden_own = call(
        first_kernel,
        sds((H_LEN, SWAP), F32),
        [ANY, ANY, VMEM, VMEM],
        [
            pltpu.VMEM((A_LEN, 2 * C), BF16),
            pltpu.VMEM((3 * 2 * C, MERGED), BF16),
            pltpu.VMEM((A_LEN, 2 * C), BF16),
            pltpu.VMEM((H_LEN + 2 * GAP, MERGED), F32),
            pltpu.SemaphoreType.DMA((3,)),
        ],
        52,
    )(joined, front, known, input_gain[None])
    totals, hidden_own = summed(sums, hidden_own)
    hidden_other = lax.ppermute(hidden_own, "core", swap)

    gain_two = middle_gain.reshape(2, HALF)
    middle, shortcut = call(
        middle_weight_kernel,
        (sds((3 * LANES, MERGED), BF16), sds((2 * C, HALF), BF16)),
        [ANY],
        [
            pltpu.VMEM((4, 224, 4 * HALF), BF16),
            pltpu.VMEM((3 * LANES, MERGED), BF16),
            pltpu.VMEM((2 * C, HALF), BF16),
            pltpu.SemaphoreType.DMA((3,)),
        ],
        52,
        (ANY, ANY),
    )(middle_found.reshape(4, 224, 4 * HALF))
    sums = call(
        second_own_kernel,
        sds((32, 1, 128), F32),
        [ANY, ANY, VMEM, VMEM, ANY, ANY, ANY],
        [
            pltpu.VMEM((B_LEN, SWAP), F32),
            pltpu.VMEM((B_LEN, SWAP), F32),
            pltpu.VMEM((2 * SEG, 2 * C), BF16),
            pltpu.VMEM((3 * LANES, MERGED), BF16),
            pltpu.VMEM((2 * C, HALF), BF16),
            pltpu.VMEM((B_LEN, LANES), BF16),
            pltpu.VMEM((2 * SEG + 3 * GAP, MERGED), F32),
            pltpu.SemaphoreType.DMA((5,)),
        ],
        60,
    )(hidden_own, hidden_other, totals, gain_two, middle, shortcut, joined)
    block_own = call(
        second_kernel,
        sds((B_LEN, SWAP), F32),
        [ANY, ANY, VMEM, VMEM, ANY, VMEM, ANY],
        [
            pltpu.VMEM((H_LEN, SWAP), F32),
            pltpu.VMEM((H_LEN, SWAP), F32),
            pltpu.VMEM((B_LEN, 2 * C), BF16),
            pltpu.VMEM((3 * LANES, MERGED), BF16),
            pltpu.VMEM((H_LEN, LANES), BF16),
            pltpu.VMEM((B_LEN + 2 * GAP, MERGED), F32),
            pltpu.SemaphoreType.DMA((4,)),
        ],
        52,
    )(hidden_own, hidden_other, totals, gain_two, middle, shortcut, joined)
    totals, block_own = summed(sums, block_own)
    block_other = lax.ppermute(block_own, "core", swap)

    wout = out_weight.reshape(9, 2, HALF, 4).transpose(1, 2, 0, 3)
    wout = jnp.pad(jnp.pad(wout, ((0, 0), (0, 0), (0, 0), (0, 4))).reshape(2, HALF, 72), ((0, 0), (0, 0), (0, 56)))
    scratch = [
        pltpu.VMEM((3 * SEG + GAP, SWAP), F32),
        pltpu.VMEM((3 * SEG + GAP, SWAP), F32),
        pltpu.SemaphoreType.DMA((2,)),
    ]
    return call(third_kernel, sds((4, 1, WIDE), F32), [ANY, ANY, VMEM, VMEM, VMEM], scratch, 30)(
        block_own, block_other, totals, output_gain.reshape(2, HALF), wout
    )


def solution(mesh):
    finer = Mesh(
        mesh.devices.reshape(8, 2, 4, 2, mesh.shape["cols"]), ("zp", "zl", "y", "core", "x")
    )
    in_specs = (
        P(None, ROWS, "x"),
        P(None, ROWS, "x"),
        P(),
        P(),
        P(ROWS, None),
        P("x", None),
        P("x", None),
        P(),
        P(),
        P("x", None),
        P(),
        P(),
        P(),
        P(),
    )
    return jax.shard_map(
        shards, mesh=finer, in_specs=in_specs, out_specs=P(None, ROWS, "x"), check_vma=False
    )
```
